32 devices in a mesh: dp: 8 (over y, x, core), sub: 4 (over z).
Axes of the slice: x: 2, y: 2, z: 4, core: 2. Of those that a mesh axis runs over, the one named last changes fastest.
Arguments:
- inputs: float32 [147456, 256], P(('dp', 'sub')), may hold values from -6 to 6
- matrices: bfloat16 [2, 3072, 256], P(None, ('dp', 'sub'))
- vectors: bfloat16 [2, 2560], P(None, ('dp', 'sub'))
- lengths: int32 [128], P(('dp', 'sub')), may hold values from 576 to 1152, as said below
- cotangent: float32 [147456, 256], P(('dp', 'sub')), may hold values from -6 to 6
Outputs:
- outputs: float32 [147456, 256], P(('dp', 'sub'))
- grad_inputs: float32 [147456, 256], P(('dp', 'sub'))
- grad_matrices: float32 [2, 3072, 256], P(None, ('dp', 'sub'))
- grad_vectors: float32 [2, 2560], P(None, ('dp', 'sub'))
The draws below stay inside these ranges and needn't reach their ends.
Inputs may be any that keep to these rules, and one draw needn't show every extreme that they name: `lengths`: real tokens of each image, counted from its start; the rest is padding.
All inputs are finite; a program needn't handle non-finite values.
Results may differ from the reference program's by a relative error of at most 0.015.
The reference program's roundings to bfloat16 on the way count: a program that leaves them out, or rounds other values in their place, can miss the bound.
Values may be sent and summed in bfloat16 or wider, within the bound.
A program may use at most 320 MiB of HBM per device.

```python
import jax
import jax.numpy as jnp
from jax import lax

D = 256
FF = 1024
HEAD_COUNT = 2
HEAD_WIDTH = 128
ROW_LENGTH = 96
IMAGE_ROWS = 12
S = 1152
IMAGES = 128
TOKENS = 147456
MROWS = 3072
VLEN = 2560


def draw_matrices(key, part):
    key = jax.random.fold_in(key, 11)
    base = jnp.clip(jax.random.normal(key, (2, MROWS, D), jnp.float32), -4.0, 4.0)
    row_index = jnp.arange(MROWS)
    scale = jnp.where(row_index < 3 * D, 1.2 / D ** 0.5, jnp.where(row_index < 4 * D, 3.0 / D ** 0.5, jnp.where(row_index < 4 * D + FF, 1.0 / D ** 0.5, 1.6 / FF ** 0.5)))
    return (base * scale[None, :, None]).astype(jnp.bfloat16)


def draw_vectors(key, part):
    key = jax.random.fold_in(key, 12)
    key_bias, key_gain = jax.random.split(key)
    position = jnp.arange(VLEN)
    segment = jnp.minimum(position // D, 6)
    spread = jnp.clip(jax.random.normal(key_bias, (2, VLEN), jnp.float32), -4.0, 4.0) * 0.3
    gains = jax.random.uniform(key_gain, (2, VLEN), jnp.float32, 0.5, 1.5)
    is_gain = (segment == 0) | (segment == 3)
    return jnp.where(is_gain[None, :], gains, spread).astype(jnp.bfloat16)


def draw_lengths(key, part):
    key = jax.random.fold_in(key, 13)
    key_length, key_pick = jax.random.split(key)
    lengths_drawn = jax.random.randint(key_length, (IMAGES,), S // 2, S + 1)
    shuffled = jax.random.permutation(key_pick, IMAGES)
    lengths_drawn = lengths_drawn.at[shuffled[0]].set(S).at[shuffled[1]].set(S // 2)
    return lengths_drawn.astype(jnp.int32)


def block_levels(stream_key, dims, cuts, least, high):
    def one(dim, blocks):
        heights = jax.random.uniform(jax.random.fold_in(jax.random.fold_in(stream_key, 6), dim), (blocks,), jnp.float32, least / len(cuts), high / len(cuts))
        return jnp.repeat(jnp.exp(heights), dims[dim] // blocks).reshape((-1,) + (1,) * (len(dims) - dim - 1))

    level = one(*cuts[0])
    for cut in cuts[1:]:
        level = level * one(*cut)
    return level


def normal_values(own_key, shape, deviation, reach, cuts=(), kind=jnp.bfloat16):
    factor_of = block_levels(own_key, shape, cuts, -0.22, 0.18) if cuts else 1.0
    array = jax.random.normal(own_key, shape, jnp.float32) * deviation * factor_of
    return jnp.minimum(jnp.maximum(array, -reach), reach).astype(kind)


def setup_inputs(seed: int = 0) -> dict:
    splits = jax.random.split(jax.random.key(seed), 6)
    return {
        "inputs": normal_values(splits[0], (TOKENS, D), 1.0, 6.0, ((0, 32),), jnp.float32),
        "matrices": draw_matrices(jax.random.fold_in(splits[5], 71), 0),
        "vectors": draw_vectors(jax.random.fold_in(splits[5], 71), 0),
        "lengths": draw_lengths(jax.random.fold_in(splits[5], 71), 0),
        "cotangent": normal_values(splits[4], (TOKENS, D), 1.0, 6.0, ((0, 32),), jnp.float32),
    }


highest = lax.Precision.HIGHEST

@jax.custom_vjp
def low(v):
    return lax.optimization_barrier(v.astype(jnp.bfloat16)).astype(jnp.float32)

@jax.custom_vjp
def low_back(v):
    return v

def low_keep(v):
    return (low(v), None)

def low_pass(kept, grad):
    return (grad,)

def back_keep(v):
    return (v, None)

def back_low(kept, grad):
    return (low(grad),)
low.defvjp(low_keep, low_pass)
low_back.defvjp(back_keep, back_low)

def normalize(source, gains, shifts):
    average = lax.optimization_barrier(jnp.mean(source, -1, keepdims=True))
    centred = source - average
    variance = lax.optimization_barrier(jnp.mean(centred * centred, -1, keepdims=True))
    return centred * lax.rsqrt(variance + 1e-05) * gains + shifts

def regroup(input_tensor, token_layout):
    grouped_heads = input_tensor.reshape(IMAGE_ROWS, ROW_LENGTH, HEAD_COUNT, HEAD_WIDTH)
    if token_layout == 'column':
        grouped_heads = jnp.swapaxes(grouped_heads, 0, 1)
    return grouped_heads

def ungroup(input_tensor, token_layout):
    if token_layout == 'column':
        input_tensor = jnp.swapaxes(input_tensor, 0, 1)
    return input_tensor.reshape(S, D)

def sparse_block(current, matrix, vector, token_layout):
    w_qkv = matrix[:3 * D]
    w_out = matrix[3 * D:4 * D]
    w_up = matrix[4 * D:4 * D + FF]
    w_down = matrix[4 * D + FF:]
    normed = low(normalize(current, vector[:D], vector[D:2 * D]))
    packed = low(low_back(jnp.dot(normed, w_qkv.T, precision=highest)))
    queries = regroup(packed[:, :D], token_layout)
    key_rows = regroup(packed[:, D:2 * D], token_layout)
    value_rows = regroup(packed[:, 2 * D:], token_layout)
    token_span = ROW_LENGTH if token_layout == 'row' else IMAGE_ROWS
    causal = jnp.tril(jnp.ones((token_span, token_span), bool))
    raw_scores = low_back(jnp.einsum('glhd,gmhd->ghlm', queries, key_rows, precision=highest))
    scores = jnp.where(causal, raw_scores * HEAD_WIDTH ** (-0.5), -1e+30)
    row_peak = lax.optimization_barrier(jnp.max(scores, -1, keepdims=True))
    exponent = jnp.exp(scores - row_peak)
    attention = low(exponent / lax.optimization_barrier(jnp.sum(exponent, -1, keepdims=True)))
    mixture = low(low_back(jnp.einsum('ghlm,gmhd->glhd', attention, value_rows, precision=highest)))
    mixture = ungroup(mixture, token_layout)
    middle = current + low_back(jnp.dot(mixture, w_out.T, precision=highest)) + vector[2 * D:3 * D]
    normed_two = low(normalize(middle, vector[3 * D:4 * D], vector[4 * D:5 * D]))
    up_pre = low_back(jnp.dot(normed_two, w_up.T, precision=highest)) + vector[6 * D:]
    active = low(jax.nn.gelu(up_pre, approximate=False))
    return middle + low_back(jnp.dot(active, w_down, precision=highest)) + vector[5 * D:6 * D]

def image_pass(current, length, matrices, vectors):
    current = sparse_block(current, matrices[0], vectors[0], 'row')
    current = sparse_block(current, matrices[1], vectors[1], 'column')
    live_rows = (jnp.arange(S) < length).astype(jnp.float32)
    return current * live_rows[:, None]

def reference(inputs, matrices, vectors, lengths, cotangent):

    def forward(flat_inputs, matrix_all, vector_all):
        images = flat_inputs.reshape(IMAGES, S, D)

        def single(image_pair):
            return image_pass(image_pair[0], image_pair[1], matrix_all, vector_all)
        results = lax.map(jax.checkpoint(single), (images, lengths))
        return results.reshape(IMAGES * S, D)
    outputs, pullback = jax.vjp(forward, inputs.astype(jnp.float32), matrices.astype(jnp.float32), vectors.astype(jnp.float32))
    grad_inputs, grad_matrices, grad_vectors = pullback(cotangent.astype(jnp.float32))
    return (outputs, grad_inputs, grad_matrices, grad_vectors)
```

```python
from functools import partial

import jax
import jax.numpy as jnp
from jax import lax
from jax.experimental import pallas as pl
from jax.experimental.pallas import tpu as pltpu
from jax.sharding import PartitionSpec as P

HEADS = 2
COLS = 96
ROWS = 12
SUBL = 8
BLOCK = 96
NBLK = 12
S = COLS * ROWS
LOG2E = 1.4426950408889634
BF = jnp.bfloat16
F32 = jnp.float32


def mm(a, b, ca, cb):
    return lax.dot_general(a, b, (((ca,), (cb,)), ((), ())), preferred_element_type=F32)


def standardize(v):
    c = v - jnp.mean(v, -1, keepdims=True)
    r = lax.rsqrt(jnp.mean(c * c, -1, keepdims=True) + 1e-05)
    return c * r, r


def rowsum8(v):
    return jnp.sum(v.reshape(v.shape[0] // 8, 8, v.shape[1]), axis=0)


def live_mask(length, slab, width):
    row = lax.broadcasted_iota(jnp.int32, (ROWS, SUBL, width), 0)
    col = lax.broadcasted_iota(jnp.int32, (ROWS, SUBL, width), 1)
    return row * COLS + col + slab * SUBL < length


def kernel(
    dims, len_ref, x_ref, cot_ref, w_ref, v_ref,
    out_ref, gin_ref, gwt_ref, gv_ref,
    n1_s, pk_s, pt_s, mix_s, mid_s, n2_s, act_s, dact_s,
    x1_s, gy0_s, gy_s, gup_s, gmid_s, gmidl_s, gmix_s, gpk_s,
):
    d, ff = dims
    hw = d // HEADS
    img = pl.program_id(0)
    length = len_ref[img]
    qs = hw ** -0.5

    @pl.when(img == 0)
    def _():
        gwt_ref[...] = jnp.zeros_like(gwt_ref)
        gv_ref[...] = jnp.zeros_like(gv_ref)

    def wqkv(l):
        return w_ref[l, 0 : 3 * d, :]

    def wout(l):
        return w_ref[l, 3 * d : 4 * d, :]

    def vec(l, i, n=1):
        return v_ref[l, 0:1, i * d : (i + n) * d]

    tril_b = lax.broadcasted_iota(jnp.int32, (BLOCK, BLOCK), 0)
    tril_a = lax.broadcasted_iota(jnp.int32, (BLOCK, BLOCK), 1)
    masks = (
        tril_b <= tril_a,
        (tril_b <= tril_a) & ((tril_b & (SUBL - 1)) == (tril_a & (SUBL - 1))),
    )

    def load_x(l, c, nb):
        if l == 0:
            return x_ref[0, pl.ds(c * nb, nb)].reshape(nb * BLOCK, d)
        return x1_s[pl.ds(c * nb, nb)].reshape(nb * BLOCK, d)

    def store_perm(ref, c, nb, val, lead=()):
        v4 = val.reshape(nb, NBLK, SUBL, d)
        for b in range(nb):
            ref[lead + (slice(None), c * nb + b)] = v4[b]

    def rows(c, nb):
        return pl.ds(pl.multiple_of(c * nb * BLOCK, BLOCK), nb * BLOCK)

    def qkv_fwd(l, nb):
        def step(c, _):
            s = rows(c, nb)
            xh, _r = standardize(load_x(l, c, nb))
            n1 = (xh * vec(l, 0) + vec(l, 1)).astype(BF)
            n1_s[l, s, :] = n1
            pk_s[l, s, :] = mm(n1, wqkv(l), 1, 1).astype(BF)
            return 0

        lax.fori_loop(0, NBLK // nb, step, 0)

    def attn_fwd(l, nb):
        mask = masks[l]

        def step(c, _):
            for b in range(nb):
                s = pl.ds(pl.multiple_of((c * nb + b) * BLOCK, BLOCK), BLOCK)
                pk = pk_s[l, s, :]
                for h in range(HEADS):
                    q = pk[:, h * hw : (h + 1) * hw]
                    k = pk[:, d + h * hw : d + (h + 1) * hw]
                    v = pk[:, 2 * d + h * hw : 2 * d + (h + 1) * hw]
                    st = jnp.where(mask, mm(k, q, 1, 1), -1e30)
                    m = jnp.max(st, 0, keepdims=True)
                    p = jnp.exp2((st - m) * (qs * LOG2E))
                    p = p * (1.0 / jnp.sum(p, 0, keepdims=True))
                    p = p.astype(BF)
                    pt_s[l, c * nb + b, h, :, 0:BLOCK] = p
                    mix_s[l, s, h * hw : (h + 1) * hw] = mm(p, v, 0, 0).astype(BF)
            return 0

        lax.fori_loop(0, NBLK // nb, step, 0)

    def ffn_fwd(l, nb):
        def step(c, _):
            s = rows(c, nb)
            mid = load_x(l, c, nb) + mm(mix_s[l, s, :], wout(l), 1, 1) + vec(l, 2)
            mid_s[l, s, :] = mid
            xh, _r = standardize(mid)
            n2 = (xh * vec(l, 3) + vec(l, 4)).astype(BF)
            n2_s[l, s, :] = n2
            y = mid + vec(l, 5)
            for f in range(ff // d):
                h = mm(n2, w_ref[l, (4 + f) * d : (5 + f) * d, :], 1, 1) + vec(l, 6 + f)
                phi = lax.erf(h * (2 ** -0.5)) * 0.5 + 0.5
                e = jnp.exp2(h * h * (-0.5 * LOG2E)) * 0.3989422804014327
                act = (h * phi).astype(BF)
                act_s[l, s, f * d : (f + 1) * d] = act
                dact_s[l, s, f * d : (f + 1) * d] = (phi + h * e).astype(BF)
                y = y + mm(act, w_ref[l, 4 * d + ff + f * d : 4 * d + ff + (f + 1) * d, :], 1, 0)
            if l == 0:
                store_perm(x1_s, c, nb, y)
            else:
                y4 = y.reshape(nb, NBLK, SUBL, d)
                for b in range(nb):
                    live = live_mask(length, c * nb + b, d)
                    out_ref[0, :, c * nb + b] = jnp.where(live, y4[b], 0.0)
            return 0

        lax.fori_loop(0, NBLK // nb, step, 0)

    def acc_vec(l, i, val, n=1):
        gv_ref[l, :, i * d : (i + n) * d] += rowsum8(val)

    def norm_back(l, gi, v, gn):
        xh, r = standardize(v)
        acc_vec(l, gi, gn * xh)
        acc_vec(l, gi + 1, gn)
        e = gn * vec(l, gi)
        me = jnp.mean(e, -1, keepdims=True)
        mx = jnp.mean(e * xh, -1, keepdims=True)
        return r * (e - me - xh * mx)

    def ffn_bwd(l, nb):
        def step(c, _):
            s = rows(c, nb)
            if l == 0:
                gy = gy0_s[pl.ds(c * nb, nb)].reshape(nb * BLOCK, d)
            else:
                parts = []
                for b in range(nb):
                    live = live_mask(length, c * nb + b, d)
                    part = jnp.where(live, cot_ref[0, :, c * nb + b], 0.0)
                    parts.append(part.reshape(BLOCK, d))
                gy = jnp.concatenate(parts, 0) if nb > 1 else parts[0]
            acc_vec(l, 5, gy)
            gyl = gy.astype(BF)
            gy_s[s, :] = gyl
            gn2 = jnp.zeros((nb * BLOCK, d), F32)
            for f in range(ff // d):
                wd = w_ref[l, 4 * d + ff + f * d : 4 * d + ff + (f + 1) * d, :]
                gup = mm(gyl, wd, 1, 1) * dact_s[l, s, f * d : (f + 1) * d].astype(F32)
                acc_vec(l, 6 + f, gup)
                gupl = gup.astype(BF)
                gup_s[s, f * d : (f + 1) * d] = gupl
                gn2 = gn2 + mm(gupl, w_ref[l, (4 + f) * d : (5 + f) * d, :], 1, 0)
            gmid = gy + norm_back(l, 3, mid_s[l, s, :], gn2)
            gmid_s[s, :] = gmid
            acc_vec(l, 2, gmid)
            gml = gmid.astype(BF)
            gmidl_s[s, :] = gml
            gmix_s[s, :] = mm(gml, wout(l), 1, 0).astype(BF)
            return 0

        lax.fori_loop(0, NBLK // nb, step, 0)

    def attn_bwd(l, nb):
        def step(c, _):
            for b in range(nb):
                s = pl.ds(pl.multiple_of((c * nb + b) * BLOCK, BLOCK), BLOCK)
                pk = pk_s[l, s, :]
                gm2 = gmix_s[s, :]
                for h in range(HEADS):
                    q = pk[:, h * hw : (h + 1) * hw]
                    k = pk[:, d + h * hw : d + (h + 1) * hw]
                    v = pk[:, 2 * d + h * hw : 2 * d + (h + 1) * hw]
                    gm = gm2[:, h * hw : (h + 1) * hw]
                    pt = pt_s[l, c * nb + b, h, :, 0:BLOCK]
                    pf = pt.astype(F32)
                    gp = mm(v, gm, 1, 1)
                    pg = pf * gp
                    gs = (pg - pf * jnp.sum(pg, 0, keepdims=True)) * qs
                    gs = gs.astype(BF)
                    gpk_s[s, h * hw : (h + 1) * hw] = mm(gs, k, 0, 0).astype(BF)
                    gpk_s[s, d + h * hw : d + (h + 1) * hw] = mm(gs, q, 1, 0).astype(BF)
                    gpk_s[s, 2 * d + h * hw : 2 * d + (h + 1) * hw] = mm(pt, gm, 1, 0).astype(BF)
            return 0

        lax.fori_loop(0, NBLK // nb, step, 0)

    def qkv_bwd(l, nb):
        def step(c, _):
            s = rows(c, nb)
            gn1 = mm(gpk_s[s, :], wqkv(l), 1, 0)
            gx = gmid_s[s, :] + norm_back(l, 0, load_x(l, c, nb), gn1)
            if l == 0:
                gin_ref[0, pl.ds(c * nb, nb)] = gx.reshape(nb, NBLK, SUBL, d)
            else:
                store_perm(gy0_s, c, nb, gx)
            return 0

        lax.fori_loop(0, NBLK // nb, step, 0)

    def wgrads(l):
        gwt_ref[l, :, 0 : 3 * d] += mm(n1_s[l], gpk_s[...], 0, 0)
        gwt_ref[l, :, 3 * d : 4 * d] += mm(mix_s[l], gmidl_s[...], 0, 0)
        gwt_ref[l, :, 4 * d : 4 * d + ff] += mm(n2_s[l], gup_s[...], 0, 0)
        gwt_ref[l, :, 4 * d + ff :] += mm(gy_s[...], act_s[l], 0, 0)

    for l in range(2):
        qkv_fwd(l, 4)
        attn_fwd(l, 2)
        ffn_fwd(l, 4)
    for l in (1, 0):
        ffn_bwd(l, 4)
        attn_bwd(l, 2)
        qkv_bwd(l, 4)
        wgrads(l)


def compute(x, cot, w, v, lengths, d, ff):
    n = lengths.shape[0]
    mrows = w.shape[1]
    img = pl.BlockSpec((1, ROWS, NBLK, SUBL, d), lambda i: (i, 0, 0, 0, 0))
    def const(shape):
        return pl.BlockSpec(shape, lambda i: (0,) * len(shape), pipeline_mode=pl.Buffered(1))
    shp = (n, ROWS, NBLK, SUBL, d)
    return pl.pallas_call(
        partial(kernel, (d, ff)),
        grid=(n,),
        in_specs=[
            pl.BlockSpec(memory_space=pltpu.SMEM),
            img,
            img,
            const(w.shape),
            const(v.shape),
        ],
        out_specs=[img, img, const((2, d, mrows)), const((2, 8, v.shape[2]))],
        out_shape=[
            jax.ShapeDtypeStruct(shp, F32),
            jax.ShapeDtypeStruct(shp, F32),
            jax.ShapeDtypeStruct((2, d, mrows), F32),
            jax.ShapeDtypeStruct((2, 8, v.shape[2]), F32),
        ],
        scratch_shapes=[
            pltpu.VMEM((2, S, d), BF),
            pltpu.VMEM((2, S, 3 * d), BF),
            pltpu.VMEM((2, NBLK, HEADS, BLOCK, 128), BF),
            pltpu.VMEM((2, S, d), BF),
            pltpu.VMEM((2, S, d), F32),
            pltpu.VMEM((2, S, d), BF),
            pltpu.VMEM((2, S, ff), BF),
            pltpu.VMEM((2, S, ff), BF),
            pltpu.VMEM((NBLK, ROWS, SUBL, d), F32),
            pltpu.VMEM((ROWS, NBLK, SUBL, d), F32),
            pltpu.VMEM((S, d), BF),
            pltpu.VMEM((S, ff), BF),
            pltpu.VMEM((S, d), F32),
            pltpu.VMEM((S, d), BF),
            pltpu.VMEM((S, d), BF),
            pltpu.VMEM((S, 3 * d), BF),
        ],
        compiler_params=pltpu.CompilerParams(
            dimension_semantics=("arbitrary",), vmem_limit_bytes=63 << 20
        ),
        cost_estimate=pl.CostEstimate(flops=46 * 10**9, bytes_accessed=30 * 10**6, transcendentals=0),
        name="layers",
    )(lengths, x.reshape(shp), cot.reshape(shp), w, v)


def body(inputs, matrices, vectors, lengths, cotangent):
    d = inputs.shape[1]
    w = lax.all_gather(matrices, ("dp", "sub"), axis=1, tiled=True)
    v = lax.all_gather(vectors, ("dp", "sub"), axis=1, tiled=True).astype(F32)
    ff = (w.shape[1] - 4 * d) // 2
    out, gin, gwt, gv = compute(inputs, cotangent, w, v[:, None, :], lengths, d, ff)
    gw = jnp.swapaxes(gwt, 1, 2)
    gw = lax.psum_scatter(gw, ("dp", "sub"), scatter_dimension=1, tiled=True)
    gv = lax.psum_scatter(jnp.sum(gv, 1), ("dp", "sub"), scatter_dimension=1, tiled=True)
    return (out.reshape(inputs.shape), gin.reshape(inputs.shape), gw, gv)


def solution(mesh):
    split = ("dp", "sub")
    return jax.shard_map(
        body,
        mesh=mesh,
        in_specs=(P(split, None), P(None, split, None), P(None, split), P(split), P(split, None)),
        out_specs=(P(split, None), P(split, None), P(None, split, None), P(None, split)),
        check_vma=False,
    )
```

```python
from functools import partial

import jax
import jax.numpy as jnp
from jax import lax
from jax.experimental import pallas as pl
from jax.experimental.pallas import tpu as pltpu
from jax.sharding import PartitionSpec as P

HEADS = 2
COLS = 96
ROWS = 12
SUBL = 8
BLOCK = 96
NBLK = 12
S = COLS * ROWS
LOG2E = 1.4426950408889634
BF = jnp.bfloat16
F32 = jnp.float32


def mm(a, b, ca, cb):
    return lax.dot_general(a, b, (((ca,), (cb,)), ((), ())), preferred_element_type=F32)


def standardize(v):
    c = v - jnp.mean(v, -1, keepdims=True)
    r = lax.rsqrt(jnp.mean(c * c, -1, keepdims=True) + 1e-05)
    return c * r, r


def rowsum8(v):
    return jnp.sum(v.reshape(v.shape[0] // 8, 8, v.shape[1]), axis=0)


def live_mask(length, slab, width):
    row = lax.broadcasted_iota(jnp.int32, (ROWS, SUBL, width), 0)
    col = lax.broadcasted_iota(jnp.int32, (ROWS, SUBL, width), 1)
    return row * COLS + col + slab * SUBL < length


def kernel(
    dims, len_ref, x_ref, cot_ref, full_ref,
    out_ref, gin_ref, gb_ref,
    w_ref, v_ref, gwt_ref, gv_ref,
    n1_s, pk_s, pt_s, mix_s, mid_s, n2_s, act_s, dact_s,
    x1_s, gy0_s, gy_s, gup_s, gmid_s, gmidl_s, gmix_s, gpk_s,
):
    d, ff = dims
    devices, block, _d = full_ref.shape
    rows_dev, vlen = w_ref.shape[1] // devices, v_ref.shape[2]
    vrow = vlen // devices
    hw = d // HEADS
    img = pl.program_id(0)
    length = len_ref[img]
    qs = hw ** -0.5

    @pl.when(img == 0)
    def _():
        gwt_ref[...] = jnp.zeros_like(gwt_ref)
        gv_ref[...] = jnp.zeros_like(gv_ref)
        v_ref[...] = jnp.zeros_like(v_ref)
        for i in range(devices):
            for l in range(2):
                w_ref[l, i * rows_dev : (i + 1) * rows_dev] = full_ref[
                    i, l * rows_dev : (l + 1) * rows_dev
                ]
            part = full_ref[i, 2 * rows_dev : block, 0:128].astype(F32)[0:8]
            at = i * vrow // 128 * 128
            wide = jnp.concatenate([part, jnp.zeros_like(part)], 1)
            if i * vrow > at:
                wide = pltpu.roll(wide, i * vrow - at, 1)
            n = min(256, vlen - at)
            for l in range(2):
                v_ref[l, 0:1, at : at + n] += wide[l : l + 1, 0:n]

    def wqkv(l):
        return w_ref[l, 0 : 3 * d, :]

    def wout(l):
        return w_ref[l, 3 * d : 4 * d, :]

    def vec(l, i, n=1):
        return v_ref[l, 0:1, i * d : (i + n) * d]

    tril_b = lax.broadcasted_iota(jnp.int32, (BLOCK, BLOCK), 0)
    tril_a = lax.broadcasted_iota(jnp.int32, (BLOCK, BLOCK), 1)
    masks = (
        tril_b <= tril_a,
        (tril_b <= tril_a) & ((tril_b & (SUBL - 1)) == (tril_a & (SUBL - 1))),
    )

    def load_x(l, c, nb):
        if l == 0:
            return x_ref[0, pl.ds(c * nb, nb)].reshape(nb * BLOCK, d)
        return x1_s[pl.ds(c * nb, nb)].reshape(nb * BLOCK, d)

    def store_perm(ref, c, nb, val, lead=()):
        v4 = val.reshape(nb, NBLK, SUBL, d)
        for b in range(nb):
            ref[lead + (slice(None), c * nb + b)] = v4[b]

    def rows(c, nb):
        return pl.ds(pl.multiple_of(c * nb * BLOCK, BLOCK), nb * BLOCK)

    def qkv_fwd(l, nb):
        def step(c, _):
            s = rows(c, nb)
            xh, _r = standardize(load_x(l, c, nb))
            n1 = (xh * vec(l, 0) + vec(l, 1)).astype(BF)
            n1_s[l, s, :] = n1
            pk_s[l, s, :] = mm(n1, wqkv(l), 1, 1).astype(BF)
            return 0

        lax.fori_loop(0, NBLK // nb, step, 0)

    def attn_fwd(l, nb):
        mask = masks[l]

        def step(c, _):
            for b in range(nb):
                s = pl.ds(pl.multiple_of((c * nb + b) * BLOCK, BLOCK), BLOCK)
                pk = pk_s[l, s, :]
                for h in range(HEADS):
                    q = pk[:, h * hw : (h + 1) * hw]
                    k = pk[:, d + h * hw : d + (h + 1) * hw]
                    v = pk[:, 2 * d + h * hw : 2 * d + (h + 1) * hw]
                    st = jnp.where(mask, mm(k, q, 1, 1), -1e30)
                    m = jnp.max(st, 0, keepdims=True)
                    p = jnp.exp2((st - m) * (qs * LOG2E))
                    p = p * (1.0 / jnp.sum(p, 0, keepdims=True))
                    p = p.astype(BF)
                    pt_s[l, c * nb + b, h, :, 0:BLOCK] = p
                    mix_s[l, s, h * hw : (h + 1) * hw] = mm(p, v, 0, 0).astype(BF)
            return 0

        lax.fori_loop(0, NBLK // nb, step, 0)

    def ffn_fwd(l, nb):
        def step(c, _):
            s = rows(c, nb)
            mid = load_x(l, c, nb) + mm(mix_s[l, s, :], wout(l), 1, 1) + vec(l, 2)
            mid_s[l, s, :] = mid
            xh, _r = standardize(mid)
            n2 = (xh * vec(l, 3) + vec(l, 4)).astype(BF)
            n2_s[l, s, :] = n2
            y = mid + vec(l, 5)
            for f in range(ff // d):
                h = mm(n2, w_ref[l, (4 + f) * d : (5 + f) * d, :], 1, 1) + vec(l, 6 + f)
                phi = lax.erf(h * (2 ** -0.5)) * 0.5 + 0.5
                e = jnp.exp2(h * h * (-0.5 * LOG2E)) * 0.3989422804014327
                act = (h * phi).astype(BF)
                act_s[l, s, f * d : (f + 1) * d] = act
                dact_s[l, s, f * d : (f + 1) * d] = (phi + h * e).astype(BF)
                y = y + mm(act, w_ref[l, 4 * d + ff + f * d : 4 * d + ff + (f + 1) * d, :], 1, 0)
            if l == 0:
                store_perm(x1_s, c, nb, y)
            else:
                y4 = y.reshape(nb, NBLK, SUBL, d)
                for b in range(nb):
                    live = live_mask(length, c * nb + b, d)
                    out_ref[0, :, c * nb + b] = jnp.where(live, y4[b], 0.0)
            return 0

        lax.fori_loop(0, NBLK // nb, step, 0)

    def acc_vec(l, i, val, n=1):
        gv_ref[l, :, i * d : (i + n) * d] += rowsum8(val)

    def norm_back(l, gi, v, gn):
        xh, r = standardize(v)
        acc_vec(l, gi, gn * xh)
        acc_vec(l, gi + 1, gn)
        e = gn * vec(l, gi)
        me = jnp.mean(e, -1, keepdims=True)
        mx = jnp.mean(e * xh, -1, keepdims=True)
        return r * (e - me - xh * mx)

    def ffn_bwd(l, nb):
        def step(c, _):
            s = rows(c, nb)
            if l == 0:
                gy = gy0_s[pl.ds(c * nb, nb)].reshape(nb * BLOCK, d)
            else:
                parts = []
                for b in range(nb):
                    live = live_mask(length, c * nb + b, d)
                    part = jnp.where(live, cot_ref[0, :, c * nb + b], 0.0)
                    parts.append(part.reshape(BLOCK, d))
                gy = jnp.concatenate(parts, 0) if nb > 1 else parts[0]
            acc_vec(l, 5, gy)
            gyl = gy.astype(BF)
            gy_s[s, :] = gyl
            gn2 = jnp.zeros((nb * BLOCK, d), F32)
            for f in range(ff // d):
                wd = w_ref[l, 4 * d + ff + f * d : 4 * d + ff + (f + 1) * d, :]
                gup = mm(gyl, wd, 1, 1) * dact_s[l, s, f * d : (f + 1) * d].astype(F32)
                acc_vec(l, 6 + f, gup)
                gupl = gup.astype(BF)
                gup_s[s, f * d : (f + 1) * d] = gupl
                gn2 = gn2 + mm(gupl, w_ref[l, (4 + f) * d : (5 + f) * d, :], 1, 0)
            gmid = gy + norm_back(l, 3, mid_s[l, s, :], gn2)
            gmid_s[s, :] = gmid
            acc_vec(l, 2, gmid)
            gml = gmid.astype(BF)
            gmidl_s[s, :] = gml
            gmix_s[s, :] = mm(gml, wout(l), 1, 0).astype(BF)
            return 0

        lax.fori_loop(0, NBLK // nb, step, 0)

    def attn_bwd(l, nb):
        def step(c, _):
            for b in range(nb):
                s = pl.ds(pl.multiple_of((c * nb + b) * BLOCK, BLOCK), BLOCK)
                pk = pk_s[l, s, :]
                gm2 = gmix_s[s, :]
                for h in range(HEADS):
                    q = pk[:, h * hw : (h + 1) * hw]
                    k = pk[:, d + h * hw : d + (h + 1) * hw]
                    v = pk[:, 2 * d + h * hw : 2 * d + (h + 1) * hw]
                    gm = gm2[:, h * hw : (h + 1) * hw]
                    pt = pt_s[l, c * nb + b, h, :, 0:BLOCK]
                    pf = pt.astype(F32)
                    gp = mm(v, gm, 1, 1)
                    pg = pf * gp
                    gs = (pg - pf * jnp.sum(pg, 0, keepdims=True)) * qs
                    gs = gs.astype(BF)
                    gpk_s[s, h * hw : (h + 1) * hw] = mm(gs, k, 0, 0).astype(BF)
                    gpk_s[s, d + h * hw : d + (h + 1) * hw] = mm(gs, q, 1, 0).astype(BF)
                    gpk_s[s, 2 * d + h * hw : 2 * d + (h + 1) * hw] = mm(pt, gm, 1, 0).astype(BF)
            return 0

        lax.fori_loop(0, NBLK // nb, step, 0)

    def qkv_bwd(l, nb):
        def step(c, _):
            s = rows(c, nb)
            gn1 = mm(gpk_s[s, :], wqkv(l), 1, 0)
            gx = gmid_s[s, :] + norm_back(l, 0, load_x(l, c, nb), gn1)
            if l == 0:
                gin_ref[0, pl.ds(c * nb, nb)] = gx.reshape(nb, NBLK, SUBL, d)
            else:
                store_perm(gy0_s, c, nb, gx)
            return 0

        lax.fori_loop(0, NBLK // nb, step, 0)

    def wgrads(l):
        gwt_ref[l, :, 0 : 3 * d] += mm(n1_s[l], gpk_s[...], 0, 0)
        gwt_ref[l, :, 3 * d : 4 * d] += mm(mix_s[l], gmidl_s[...], 0, 0)
        gwt_ref[l, :, 4 * d : 4 * d + ff] += mm(n2_s[l], gup_s[...], 0, 0)
        gwt_ref[l, :, 4 * d + ff :] += mm(gy_s[...], act_s[l], 0, 0)

    for l in range(2):
        qkv_fwd(l, 4)
        attn_fwd(l, 2)
        ffn_fwd(l, 4)
    for l in (1, 0):
        ffn_bwd(l, 4)
        attn_bwd(l, 2)
        qkv_bwd(l, 4)
        wgrads(l)

    @pl.when(img == pl.num_programs(0) - 1)
    def _():
        zeros = jnp.zeros((block - 2 * rows_dev, d), F32)
        for l in range(2):
            g = gwt_ref[l].T.astype(BF)
            for i in range(devices):
                gb_ref[i, l * rows_dev : (l + 1) * rows_dev] = g[i * rows_dev : (i + 1) * rows_dev]
        gv = jnp.concatenate([jnp.sum(gv_ref[l], 0, keepdims=True) for l in range(2)], 0)
        gv = jnp.concatenate([gv, jnp.zeros((6, vlen), F32)], 0)
        for i in range(devices):
            at = i * vrow // 128 * 128
            n = min(256, vlen - at)
            wide = gv[:, at : at + n]
            if n < 256:
                wide = jnp.concatenate([wide, jnp.zeros_like(wide)], 1)
            if i * vrow > at:
                wide = pltpu.roll(wide, 256 - (i * vrow - at), 1)
            wide = jnp.concatenate([wide, jnp.zeros_like(wide)], 0)
            gb_ref[i, 2 * rows_dev : block] = wide.astype(BF)


MESH = pl.DeviceIdType.MESH


def place(z_count):
    dp, z = lax.axis_index("dp"), lax.axis_index("sub")
    core = dp % 2
    x = (dp // 2) % 2
    y = dp // 4
    return y, x, core, z


def column(y, x, core):
    return (y * 2 + x) * 2 + core


def greet(z, z_count, partners):
    barrier = pltpu.get_barrier_semaphore()
    dp = lax.axis_index("dp")
    for p in partners:
        pl.semaphore_signal(barrier, inc=1, device_id=(p, z), device_id_type=MESH)

    @pl.when(z > 0)
    def _():
        pl.semaphore_signal(barrier, inc=1, device_id=(dp, z - 1), device_id_type=MESH)

    @pl.when(z < z_count - 1)
    def _():
        pl.semaphore_signal(barrier, inc=1, device_id=(dp, z + 1), device_id_type=MESH)

    ends = jnp.where(z > 0, 1, 0) + jnp.where(z < z_count - 1, 1, 0)
    pl.semaphore_wait(barrier, len(partners) + ends)


def gather_kernel(z_count, w_ref, v_ref, full_ref, link_sem, core_sem, send_sem):
    y, x, core, z = place(z_count)
    dp = lax.axis_index("dp")
    rows = w_ref.shape[1]
    block = full_ref.shape[1]
    half = (block // 2 + 15) // 16 * 16
    cut = (pl.ds(0, half), pl.ds(half, block - half))
    dp_x, dp_y, dp_c = column(y, 1 - x, core), column(1 - y, x, core), column(y, x, 1 - core)
    me = dp * z_count + z

    greet(z, z_count, (dp_x, dp_y, dp_c))
    full_ref[me, 0:rows] = w_ref[0]
    full_ref[me, rows : 2 * rows] = w_ref[1]
    pad = jnp.zeros((block - 2 * rows, full_ref.shape[2]), full_ref.dtype)
    full_ref[me, 2 * rows : block] = pad
    full_ref[me, 2 * rows : 2 * rows + 2, 0 : v_ref.shape[1]] = v_ref[...]

    def copy(i, h, slot, target, sem):
        ref = full_ref.at[i, cut[h], :]
        return pltpu.make_async_remote_copy(
            src_ref=ref, dst_ref=ref, send_sem=send_sem.at[i, h, slot], recv_sem=sem.at[i, h],
            device_id=target, device_id_type=MESH,
        )

    def to_right(i, h):
        return copy(i, h, 0, (dp, z + 1), link_sem)

    def to_left(i, h):
        return copy(i, h, 1, (dp, z - 1), link_sem)

    def to_x(i, h):
        return copy(i, h, 2, (dp_x, z), link_sem)

    def to_y(i, h):
        return copy(i, h, 3, (dp_y, z), link_sem)

    def to_core(i, h):
        return copy(i, h, 4, (dp_c, z), core_sem)

    def spread_column(i):
        to_x(i, 0).start()
        to_y(i, 1).start()
        to_core(i, 0).start()
        to_core(i, 1).start()
        to_x(i, 1).start()
        to_y(i, 0).start()

    def wait_link(i, h):
        pltpu.make_async_remote_copy(
            src_ref=full_ref.at[i, cut[h], :], dst_ref=full_ref.at[i, cut[h], :],
            send_sem=send_sem.at[i, h, 4], recv_sem=link_sem.at[i, h],
            device_id=(dp_c, z), device_id_type=MESH,
        ).wait_recv()

    @pl.when(z < z_count - 1)
    def _():
        for h in range(2):
            to_right(me, h).start()

    @pl.when(z > 0)
    def _():
        for h in range(2):
            to_left(me, h).start()

    spread_column(me)
    for k in range(1, z_count):

        @pl.when(z - k >= 0)
        def _():
            i = me - k
            for h in range(2):
                wait_link(i, h)

            @pl.when(z < z_count - 1)
            def _():
                for h in range(2):
                    to_right(i, h).start()

            spread_column(i)

        @pl.when(z + k < z_count)
        def _():
            i = me + k
            for h in range(2):
                wait_link(i, h)

            @pl.when(z > 0)
            def _():
                for h in range(2):
                    to_left(i, h).start()

            spread_column(i)

    order = []
    for k in range(z_count):
        order.append(lax.rem(z + k, z_count))
    for zz in order:
        i = dp_x * z_count + zz
        wait_link(i, 0)
        to_y(i, 0).start()
        to_core(i, 0).start()
        i = dp_y * z_count + zz
        wait_link(i, 1)
        to_x(i, 1).start()
        to_core(i, 1).start()
    for zz in order:
        i = dp_x * z_count + zz
        wait_link(i, 1)
        to_core(i, 1).start()
        i = dp_y * z_count + zz
        wait_link(i, 0)
        to_core(i, 0).start()
    dp_d = column(1 - y, 1 - x, core)
    for zz in order:
        i = dp_d * z_count + zz
        for h in range(2):
            wait_link(i, h)
            to_core(i, h).start()
    for yy in range(2):
        for xx in range(2):
            for zz in range(z_count):
                i = column(yy, xx, 1 - core) * z_count + zz
                for h in range(2):
                    to_core(i, h).wait_recv()
    for yy in range(2):
        for xx in range(2):
            for zz in range(z_count):
                i = column(yy, xx, core) * z_count + zz
                for h in range(2):
                    to_core(i, h).wait_send()
    for zz in range(z_count):
        i = dp * z_count + zz
        for h in range(2):
            to_x(i, h).wait_send()
            to_y(i, h).wait_send()

        @pl.when((zz <= z) & (z < z_count - 1))
        def _():
            for h in range(2):
                to_right(i, h).wait_send()

        @pl.when((zz >= z) & (z > 0))
        def _():
            for h in range(2):
                to_left(i, h).wait_send()

        to_y(dp_x * z_count + zz, 0).wait_send()
        to_x(dp_y * z_count + zz, 1).wait_send()


def scatter_kernel(
    z_count, g_ref, gw_ref, gv_ref,
    sib_s, acc_s, own_s, xa_s, yb_s, oya_s, oxb_s, oxa_s, oyb_s, zl_s, zr_s,
    sib_send, sib_recv, xy_send, xy_recv, z_send, z_recv,
):
    y, x, core, z = place(z_count)
    dp = lax.axis_index("dp")
    block, width = g_ref.shape[1], g_ref.shape[2]
    half = xa_s.shape[1]
    top, low = pl.ds(0, half), pl.ds(half, block - half)
    dp_x, dp_y, dp_c = column(y, 1 - x, core), column(1 - y, x, core), column(y, x, 1 - core)
    kinds = ((y, x), (y, 1 - x), (1 - y, x), (1 - y, 1 - x))
    order = []
    for k in range((z_count + 1) // 2):
        order.append(z_count - 1 - k)
        if k != z_count - 1 - k:
            order.append(k)

    greet(z, z_count, (dp_x, dp_y, dp_c))

    def to_core(kind):
        yy, xx = kinds[kind]
        return pltpu.make_async_remote_copy(
            src_ref=g_ref.at[pl.ds(column(yy, xx, 1 - core) * z_count, z_count)],
            dst_ref=sib_s.at[kind],
            send_sem=sib_send.at[kind], recv_sem=sib_recv.at[kind],
            device_id=(dp_c, z), device_id_type=MESH,
        )

    def across(kind, rows, dst, slot, target, t):
        return pltpu.make_async_remote_copy(
            src_ref=acc_s.at[kind, t, rows, :], dst_ref=dst.at[t],
            send_sem=xy_send.at[slot, t], recv_sem=xy_recv.at[slot, t],
            device_id=(target, z), device_id_type=MESH,
        )

    def diag_top(t):
        return across(3, top, xa_s, 0, dp_y, t)

    def diag_low(t):
        return across(3, low, yb_s, 1, dp_x, t)

    def ycol_top(t):
        return across(2, top, oya_s, 2, dp_y, t)

    def xcol_low(t):
        return across(1, low, oxb_s, 3, dp_x, t)

    def xcol_top(t):
        return across(1, top, oxa_s, 4, dp_x, t)

    def ycol_low(t):
        return across(2, low, oyb_s, 5, dp_y, t)

    def to_right(t):
        return pltpu.make_async_remote_copy(
            src_ref=acc_s.at[0, t], dst_ref=zl_s.at[t],
            send_sem=z_send.at[0, t], recv_sem=z_recv.at[0, t],
            device_id=(dp, z + 1), device_id_type=MESH,
        )

    def to_left(t):
        return pltpu.make_async_remote_copy(
            src_ref=acc_s.at[0, t], dst_ref=zr_s.at[t],
            send_sem=z_send.at[1, t], recv_sem=z_recv.at[1, t],
            device_id=(dp, z - 1), device_id_type=MESH,
        )

    def chip_sum(kind, t):
        yy, xx = kinds[kind]
        mine = g_ref[column(yy, xx, core) * z_count + t].astype(F32)
        return mine + sib_s[kind, t].astype(F32)

    for kind in (3, 1, 2, 0):
        to_core(kind).start()
    to_core(3).wait_recv()
    for t in order:
        acc_s[3, t] = chip_sum(3, t).astype(BF)
        diag_top(t).start()
        diag_low(t).start()
    to_core(1).wait_recv()
    for t in order:
        acc_s[1, t] = chip_sum(1, t).astype(BF)
        xcol_low(t).start()
    to_core(2).wait_recv()
    for t in order:
        acc_s[2, t] = chip_sum(2, t).astype(BF)
        ycol_top(t).start()
    to_core(0).wait_recv()
    for t in order:
        own_s[t] = chip_sum(0, t)
    for t in order:
        diag_top(t).wait_recv()
        acc_s[1, t, top] = (acc_s[1, t, top].astype(F32) + xa_s[t].astype(F32)).astype(BF)
        xcol_top(t).start()
        diag_low(t).wait_recv()
        acc_s[2, t, low] = (acc_s[2, t, low].astype(F32) + yb_s[t].astype(F32)).astype(BF)
        ycol_low(t).start()
    for t in order:
        xcol_low(t).wait_recv()
        ycol_top(t).wait_recv()
        xcol_top(t).wait_recv()
        ycol_low(t).wait_recv()
        own_s[t, top] += oya_s[t].astype(F32) + oxa_s[t].astype(F32)
        own_s[t, low] += oxb_s[t].astype(F32) + oyb_s[t].astype(F32)

        @pl.when(t > z)
        def _():
            @pl.when(z > 0)
            def _():
                to_right(t).wait_recv()
                acc_s[0, t] = (own_s[t] + zl_s[t].astype(F32)).astype(BF)

            @pl.when(z == 0)
            def _():
                acc_s[0, t] = own_s[t].astype(BF)

            to_right(t).start()

        @pl.when(t < z)
        def _():
            @pl.when(z < z_count - 1)
            def _():
                to_left(t).wait_recv()
                acc_s[0, t] = (own_s[t] + zr_s[t].astype(F32)).astype(BF)

            @pl.when(z == z_count - 1)
            def _():
                acc_s[0, t] = own_s[t].astype(BF)

            to_left(t).start()

    @pl.when(z > 0)
    def _():
        to_right(z).wait_recv()
        own_s[z] += zl_s[z].astype(F32)

    @pl.when(z < z_count - 1)
    def _():
        to_left(z).wait_recv()
        own_s[z] += zr_s[z].astype(F32)

    rows = gw_ref.shape[1]
    gw_ref[0] = own_s[z, 0:rows]
    gw_ref[1] = own_s[z, rows : 2 * rows]
    gv_ref[...] = own_s[z, 2 * rows : 2 * rows + 2, 0 : gv_ref.shape[1]]

    for kind in range(4):
        to_core(kind).wait_send()
    for t in range(z_count):
        for one in (diag_top, diag_low, ycol_top, xcol_low, xcol_top, ycol_low):
            one(t).wait_send()

        @pl.when(t > z)
        def _():
            to_right(t).wait_send()

        @pl.when(t < z)
        def _():
            to_left(t).wait_send()


def gather(w, v, z_count, devices):
    rows, d = w.shape[1], w.shape[2]
    block = 2 * rows + 16
    return pl.pallas_call(
        partial(gather_kernel, z_count),
        in_specs=[pl.BlockSpec(memory_space=pltpu.VMEM)] * 2,
        out_specs=pl.BlockSpec(memory_space=pltpu.VMEM),
        out_shape=jax.ShapeDtypeStruct((devices, block, d), BF),
        scratch_shapes=[
            pltpu.SemaphoreType.DMA((devices, 2)),
            pltpu.SemaphoreType.DMA((devices, 2)),
            pltpu.SemaphoreType.DMA((devices, 2, 5)),
        ],
        compiler_params=pltpu.CompilerParams(
            collective_id=0, has_side_effects=True, vmem_limit_bytes=32 << 20
        ),
        name="gather",
    )(w, v)


def scatter(g, z_count, rows, vrow):
    devices, block, d = g.shape
    half = (block // 2 + 15) // 16 * 16
    low = block - half
    return pl.pallas_call(
        partial(scatter_kernel, z_count),
        in_specs=[pl.BlockSpec(memory_space=pltpu.VMEM)],
        out_specs=[pl.BlockSpec(memory_space=pltpu.VMEM)] * 2,
        out_shape=[
            jax.ShapeDtypeStruct((2, rows, d), F32),
            jax.ShapeDtypeStruct((2, vrow), F32),
        ],
        scratch_shapes=[
            pltpu.VMEM((4, z_count, block, d), BF),
            pltpu.VMEM((4, z_count, block, d), BF),
            pltpu.VMEM((z_count, block, d), F32),
            pltpu.VMEM((z_count, half, d), BF),
            pltpu.VMEM((z_count, low, d), BF),
            pltpu.VMEM((z_count, half, d), BF),
            pltpu.VMEM((z_count, low, d), BF),
            pltpu.VMEM((z_count, half, d), BF),
            pltpu.VMEM((z_count, low, d), BF),
            pltpu.VMEM((z_count, block, d), BF),
            pltpu.VMEM((z_count, block, d), BF),
            pltpu.SemaphoreType.DMA((4,)),
            pltpu.SemaphoreType.DMA((4,)),
            pltpu.SemaphoreType.DMA((6, z_count)),
            pltpu.SemaphoreType.DMA((6, z_count)),
            pltpu.SemaphoreType.DMA((2, z_count)),
            pltpu.SemaphoreType.DMA((2, z_count)),
        ],
        compiler_params=pltpu.CompilerParams(
            collective_id=1, has_side_effects=True, vmem_limit_bytes=48 << 20
        ),
        name="scatter",
    )(g)


def compute(x, cot, full, lengths, d, ff, vlen):
    n = lengths.shape[0]
    mrows = 4 * d + 2 * ff
    img = pl.BlockSpec((1, ROWS, NBLK, SUBL, d), lambda i: (i, 0, 0, 0, 0))
    whole = pl.BlockSpec(full.shape, lambda i: (0, 0, 0), pipeline_mode=pl.Buffered(1))
    shp = (n, ROWS, NBLK, SUBL, d)
    return pl.pallas_call(
        partial(kernel, (d, ff)),
        grid=(n,),
        in_specs=[pl.BlockSpec(memory_space=pltpu.SMEM), img, img, whole],
        out_specs=[img, img, whole],
        out_shape=[
            jax.ShapeDtypeStruct(shp, F32),
            jax.ShapeDtypeStruct(shp, F32),
            jax.ShapeDtypeStruct(full.shape, BF),
        ],
        scratch_shapes=[
            pltpu.VMEM((2, mrows, d), BF),
            pltpu.VMEM((2, 8, vlen), F32),
            pltpu.VMEM((2, d, mrows), F32),
            pltpu.VMEM((2, 8, vlen), F32),
            pltpu.VMEM((2, S, d), BF),
            pltpu.VMEM((2, S, 3 * d), BF),
            pltpu.VMEM((2, NBLK, HEADS, BLOCK, 128), BF),
            pltpu.VMEM((2, S, d), BF),
            pltpu.VMEM((2, S, d), F32),
            pltpu.VMEM((2, S, d), BF),
            pltpu.VMEM((2, S, ff), BF),
            pltpu.VMEM((2, S, ff), BF),
            pltpu.VMEM((NBLK, ROWS, SUBL, d), F32),
            pltpu.VMEM((ROWS, NBLK, SUBL, d), F32),
            pltpu.VMEM((S, d), BF),
            pltpu.VMEM((S, ff), BF),
            pltpu.VMEM((S, d), F32),
            pltpu.VMEM((S, d), BF),
            pltpu.VMEM((S, d), BF),
            pltpu.VMEM((S, 3 * d), BF),
        ],
        compiler_params=pltpu.CompilerParams(
            dimension_semantics=("arbitrary",), vmem_limit_bytes=63 << 20
        ),
        name="layers",
    )(lengths, x.reshape(shp), cot.reshape(shp), full)


def to_blocks(w, v):
    pad = jnp.pad(v[:, :], ((0, 0), (0, w.shape[2] - v.shape[1])))
    tail = jnp.pad(pad, ((0, 14), (0, 0)))
    return jnp.concatenate([w[0], w[1], tail], 0)


def body(z_count, dp_count, inputs, matrices, vectors, lengths, cotangent):
    d = inputs.shape[1]
    devices = z_count * dp_count
    rows, vrow = matrices.shape[1], vectors.shape[1]
    vlen = vrow * devices
    ff = (rows * devices - 4 * d) // 2
    own_kernels = dp_count == 8
    if own_kernels:
        full = gather(matrices, vectors, z_count, devices)
    else:
        full = lax.all_gather(to_blocks(matrices, vectors), ("dp", "sub"), axis=0)
    out, gin, gb = compute(inputs, cotangent, full, lengths, d, ff, vlen)
    if own_kernels:
        gw, gv = scatter(gb, z_count, rows, vrow)
    else:
        g = lax.psum_scatter(gb.astype(F32), ("dp", "sub"), scatter_dimension=0, tiled=True)[0]
        gw = g[: 2 * rows].reshape(2, rows, d)
        gv = g[2 * rows : 2 * rows + 2, :vrow]
    return (out.reshape(inputs.shape), gin.reshape(inputs.shape), gw, gv)


def solution(mesh):
    split = ("dp", "sub")
    return jax.shard_map(
        partial(body, mesh.shape["sub"], mesh.shape["dp"]),
        mesh=mesh,
        in_specs=(P(split, None), P(None, split, None), P(None, split), P(split), P(split, None)),
        out_specs=(P(split, None), P(split, None), P(None, split, None), P(None, split)),
        check_vma=False,
    )
```

```python
from functools import partial

import jax
import jax.numpy as jnp
from jax import lax
from jax.experimental import pallas as pl
from jax.experimental.pallas import tpu as pltpu
from jax.sharding import PartitionSpec as P

HEADS = 2
COLS = 96
ROWS = 12
SUBL = 8
BLOCK = 96
NBLK = 12
S = COLS * ROWS
LOG2E = 1.4426950408889634
BF = jnp.bfloat16
F32 = jnp.float32
STATIC = False
NB = (12,12,6,6,12,12)


def mm(a, b, ca, cb):
    return lax.dot_general(a, b, (((ca,), (cb,)), ((), ())), preferred_element_type=F32)


def standardize(v):
    c = v - jnp.mean(v, -1, keepdims=True)
    r = lax.rsqrt(jnp.mean(c * c, -1, keepdims=True) + 1e-05)
    return c * r, r


def rowsum8(v):
    return jnp.sum(v.reshape(v.shape[0] // 8, 8, v.shape[1]), axis=0)


def live_mask(length, slab, width):
    row = lax.broadcasted_iota(jnp.int32, (ROWS, SUBL, width), 0)
    col = lax.broadcasted_iota(jnp.int32, (ROWS, SUBL, width), 1)
    return row * COLS + col + slab * SUBL < length


def kernel(
    dims, len_ref, x_ref, cot_ref, full_ref,
    out_ref, gin_ref, gb_ref,
    w_ref, v_ref, gwt_ref, gv_ref,
    n1_s, pk_s, pt_s, mix_s, mid_s, n2_s, act_s, dact_s,
    x1_s, gy0_s, gy_s, gup_s, gmid_s, gmidl_s, gmix_s, gpk_s,
):
    d, ff = dims
    devices, block, _d = full_ref.shape
    rows_dev, vlen = w_ref.shape[1] // devices, v_ref.shape[2]
    vrow = vlen // devices
    hw = d // HEADS
    img = pl.program_id(0)
    length = len_ref[img]
    qs = hw ** -0.5

    @pl.when(img == 0)
    def _():
        gwt_ref[...] = jnp.zeros_like(gwt_ref)
        gv_ref[...] = jnp.zeros_like(gv_ref)
        v_ref[...] = jnp.zeros_like(v_ref)
        for i in range(devices):
            for l in range(2):
                w_ref[l, i * rows_dev : (i + 1) * rows_dev] = full_ref[
                    i, l * rows_dev : (l + 1) * rows_dev
                ]
            part = full_ref[i, 2 * rows_dev : block, 0:128].astype(F32)[0:8]
            at = i * vrow // 128 * 128
            wide = jnp.concatenate([part, jnp.zeros_like(part)], 1)
            if i * vrow > at:
                wide = pltpu.roll(wide, i * vrow - at, 1)
            n = min(256, vlen - at)
            for l in range(2):
                v_ref[l, 0:1, at : at + n] += wide[l : l + 1, 0:n]

    def wqkv(l):
        return w_ref[l, 0 : 3 * d, :]

    def wout(l):
        return w_ref[l, 3 * d : 4 * d, :]

    def vec(l, i, n=1):
        return v_ref[l, 0:1, i * d : (i + n) * d]

    tril_b = lax.broadcasted_iota(jnp.int32, (BLOCK, BLOCK), 0)
    tril_a = lax.broadcasted_iota(jnp.int32, (BLOCK, BLOCK), 1)
    masks = (
        tril_b <= tril_a,
        (tril_b <= tril_a) & ((tril_b & (SUBL - 1)) == (tril_a & (SUBL - 1))),
    )

    def load_x(l, c, nb):
        if l == 0:
            return x_ref[0, pl.ds(c * nb, nb)].reshape(nb * BLOCK, d)
        return x1_s[pl.ds(c * nb, nb)].reshape(nb * BLOCK, d)

    def store_perm(ref, c, nb, val, lead=()):
        v4 = val.reshape(nb, NBLK, SUBL, d)
        for b in range(nb):
            ref[lead + (slice(None), c * nb + b)] = v4[b]

    def rows(c, nb):
        if isinstance(c, int):
            return pl.ds(c * nb * BLOCK, nb * BLOCK)
        return pl.ds(pl.multiple_of(c * nb * BLOCK, BLOCK), nb * BLOCK)

    def loop(n, step):
        if STATIC or n == 1:
            for c in range(n):
                step(c, 0)
        else:
            lax.fori_loop(0, n, step, 0)

    def qkv_fwd(l, nb):
        def step(c, _):
            s = rows(c, nb)
            xh, _r = standardize(load_x(l, c, nb))
            n1 = (xh * vec(l, 0) + vec(l, 1)).astype(BF)
            n1_s[l, s, :] = n1
            pk_s[l, s, :] = mm(n1, wqkv(l), 1, 1).astype(BF)
            return 0

        loop(NBLK // nb, step)

    def heads_of(packed):
        return [
            tuple(packed[:, i * d + h * hw : i * d + (h + 1) * hw] for i in range(3))
            for h in range(HEADS)
        ]

    def attn_fwd(l, nb):
        mask = masks[l]

        def step(c, _):
            each = [(b, h) for b in range(nb) for h in range(HEADS)]
            qkv = []
            for b in range(nb):
                qkv += heads_of(pk_s[l, rows(c * nb + b, 1), :])
            scores = [mm(k, q, 1, 1) for q, k, v in qkv]
            ps = []
            for st in scores:
                st = jnp.where(mask, st, -1e30)
                p = jnp.exp2((st - jnp.max(st, 0, keepdims=True)) * (qs * LOG2E))
                ps.append((p * (1.0 / jnp.sum(p, 0, keepdims=True))).astype(BF))
            mixed = [mm(p, v, 0, 0).astype(BF) for p, (q, k, v) in zip(ps, qkv)]
            for (b, h), p, m in zip(each, ps, mixed):
                pt_s[l, c * nb + b, h, :, 0:BLOCK] = p
                mix_s[l, rows(c * nb + b, 1), h * hw : (h + 1) * hw] = m
            return 0

        loop(NBLK // nb, step)

    def ffn_fwd(l, nb):
        def step(c, _):
            s = rows(c, nb)
            mid = load_x(l, c, nb) + mm(mix_s[l, s, :], wout(l), 1, 1) + vec(l, 2)
            mid_s[l, s, :] = mid
            xh, _r = standardize(mid)
            n2 = (xh * vec(l, 3) + vec(l, 4)).astype(BF)
            n2_s[l, s, :] = n2
            y = mid + vec(l, 5)
            for f in range(ff // d):
                h = mm(n2, w_ref[l, (4 + f) * d : (5 + f) * d, :], 1, 1) + vec(l, 6 + f)
                phi = lax.erf(h * (2 ** -0.5)) * 0.5 + 0.5
                e = jnp.exp2(h * h * (-0.5 * LOG2E)) * 0.3989422804014327
                act = (h * phi).astype(BF)
                act_s[l, s, f * d : (f + 1) * d] = act
                dact_s[l, s, f * d : (f + 1) * d] = (phi + h * e).astype(BF)
            y = y + mm(act_s[l, s, :], w_ref[l, 4 * d + ff :, :], 1, 0)
            if l == 0:
                store_perm(x1_s, c, nb, y)
            else:
                y4 = y.reshape(nb, NBLK, SUBL, d)
                for b in range(nb):
                    live = live_mask(length, c * nb + b, d)
                    out_ref[0, :, c * nb + b] = jnp.where(live, y4[b], 0.0)
            return 0

        loop(NBLK // nb, step)

    def acc_vec(l, i, val, n=1):
        gv_ref[l, :, i * d : (i + n) * d] += rowsum8(val)

    def norm_back(l, gi, v, gn):
        xh, r = standardize(v)
        acc_vec(l, gi, gn * xh)
        acc_vec(l, gi + 1, gn)
        e = gn * vec(l, gi)
        me = jnp.mean(e, -1, keepdims=True)
        mx = jnp.mean(e * xh, -1, keepdims=True)
        return r * (e - me - xh * mx)

    def ffn_bwd(l, nb):
        def step(c, _):
            s = rows(c, nb)
            if l == 0:
                gy = gy0_s[pl.ds(c * nb, nb)].reshape(nb * BLOCK, d)
            else:
                parts = []
                for b in range(nb):
                    live = live_mask(length, c * nb + b, d)
                    part = jnp.where(live, cot_ref[0, :, c * nb + b], 0.0)
                    parts.append(part.reshape(BLOCK, d))
                gy = jnp.concatenate(parts, 0) if nb > 1 else parts[0]
            acc_vec(l, 5, gy)
            gyl = gy.astype(BF)
            gy_s[s, :] = gyl
            for f in range(ff // d):
                wd = w_ref[l, 4 * d + ff + f * d : 4 * d + ff + (f + 1) * d, :]
                gup = mm(gyl, wd, 1, 1) * dact_s[l, s, f * d : (f + 1) * d].astype(F32)
                acc_vec(l, 6 + f, gup)
                gupl = gup.astype(BF)
                gup_s[s, f * d : (f + 1) * d] = gupl
            gn2 = mm(gup_s[s, :], w_ref[l, 4 * d : 4 * d + ff, :], 1, 0)
            gmid = gy + norm_back(l, 3, mid_s[l, s, :], gn2)
            gmid_s[s, :] = gmid
            acc_vec(l, 2, gmid)
            gml = gmid.astype(BF)
            gmidl_s[s, :] = gml
            gmix_s[s, :] = mm(gml, wout(l), 1, 0).astype(BF)
            return 0

        loop(NBLK // nb, step)

    def attn_bwd(l, nb):
        def step(c, _):
            each = [(b, h) for b in range(nb) for h in range(HEADS)]
            qkv, gms = [], []
            for b in range(nb):
                at = rows(c * nb + b, 1)
                qkv += heads_of(pk_s[l, at, :])
                gm = gmix_s[at, :]
                gms += [gm[:, h * hw : (h + 1) * hw] for h in range(HEADS)]
            pts = [pt_s[l, c * nb + b, h, :, 0:BLOCK] for b, h in each]
            gps = [mm(v, gm, 1, 1) for (q, k, v), gm in zip(qkv, gms)]
            gss = []
            for pt, gp in zip(pts, gps):
                pf = pt.astype(F32)
                pg = pf * gp
                gss.append(((pg - pf * jnp.sum(pg, 0, keepdims=True)) * qs).astype(BF))
            gv = [mm(pt, gm, 1, 0).astype(BF) for pt, gm in zip(pts, gms)]
            gk = [mm(gs, q, 1, 0).astype(BF) for gs, (q, k, v) in zip(gss, qkv)]
            gq = [mm(gs, k, 0, 0).astype(BF) for gs, (q, k, v) in zip(gss, qkv)]
            for n, (b, h) in enumerate(each):
                for i, g in enumerate((gq, gk, gv)):
                    gpk_s[rows(c * nb + b, 1), i * d + h * hw : i * d + (h + 1) * hw] = g[n]
            return 0

        loop(NBLK // nb, step)

    def qkv_bwd(l, nb):
        def step(c, _):
            s = rows(c, nb)
            gn1 = mm(gpk_s[s, :], wqkv(l), 1, 0)
            gx = gmid_s[s, :] + norm_back(l, 0, load_x(l, c, nb), gn1)
            if l == 0:
                gin_ref[0, pl.ds(c * nb, nb)] = gx.reshape(nb, NBLK, SUBL, d)
            else:
                store_perm(gy0_s, c, nb, gx)
            return 0

        loop(NBLK // nb, step)

    def wgrads(l):
        gwt_ref[l, :, 0 : 3 * d] += mm(n1_s[l], gpk_s[...], 0, 0)
        gwt_ref[l, :, 3 * d : 4 * d] += mm(mix_s[l], gmidl_s[...], 0, 0)
        gwt_ref[l, :, 4 * d : 4 * d + ff] += mm(n2_s[l], gup_s[...], 0, 0)
        gwt_ref[l, :, 4 * d + ff :] += mm(gy_s[...], act_s[l], 0, 0)

    for l in range(2):
        qkv_fwd(l, NB[0])
        attn_fwd(l, NB[1])
        ffn_fwd(l, NB[2])
    for l in (1, 0):
        ffn_bwd(l, NB[3])
        attn_bwd(l, NB[4])
        qkv_bwd(l, NB[5])
        wgrads(l)

    @pl.when(img == pl.num_programs(0) - 1)
    def _():
        zeros = jnp.zeros((block - 2 * rows_dev, d), F32)
        for l in range(2):
            g = gwt_ref[l].T.astype(BF)
            for i in range(devices):
                gb_ref[i, l * rows_dev : (l + 1) * rows_dev] = g[i * rows_dev : (i + 1) * rows_dev]
        gv = jnp.concatenate([jnp.sum(gv_ref[l], 0, keepdims=True) for l in range(2)], 0)
        gv = jnp.concatenate([gv, jnp.zeros((6, vlen), F32)], 0)
        for i in range(devices):
            at = i * vrow // 128 * 128
            n = min(256, vlen - at)
            wide = gv[:, at : at + n]
            if n < 256:
                wide = jnp.concatenate([wide, jnp.zeros_like(wide)], 1)
            if i * vrow > at:
                wide = pltpu.roll(wide, 256 - (i * vrow - at), 1)
            wide = jnp.concatenate([wide, jnp.zeros_like(wide)], 0)
            gb_ref[i, 2 * rows_dev : block] = wide.astype(BF)


MESH = pl.DeviceIdType.MESH


def place(z_count):
    dp, z = lax.axis_index("dp"), lax.axis_index("sub")
    core = dp % 2
    x = (dp // 2) % 2
    y = dp // 4
    return y, x, core, z


def column(y, x, core):
    return (y * 2 + x) * 2 + core


def greet(z, z_count, partners):
    barrier = pltpu.get_barrier_semaphore()
    dp = lax.axis_index("dp")
    for p in partners:
        pl.semaphore_signal(barrier, inc=1, device_id=(p, z), device_id_type=MESH)

    @pl.when(z > 0)
    def _():
        pl.semaphore_signal(barrier, inc=1, device_id=(dp, z - 1), device_id_type=MESH)

    @pl.when(z < z_count - 1)
    def _():
        pl.semaphore_signal(barrier, inc=1, device_id=(dp, z + 1), device_id_type=MESH)

    ends = jnp.where(z > 0, 1, 0) + jnp.where(z < z_count - 1, 1, 0)
    pl.semaphore_wait(barrier, len(partners) + ends)


def gather_kernel(z_count, w_ref, v_ref, full_ref, link_sem, core_sem, send_sem):
    y, x, core, z = place(z_count)
    dp = lax.axis_index("dp")
    rows = w_ref.shape[1]
    block = full_ref.shape[1]
    half = (block // 2 + 15) // 16 * 16
    cut = (pl.ds(0, half), pl.ds(half, block - half))
    dp_x, dp_y, dp_c = column(y, 1 - x, core), column(1 - y, x, core), column(y, x, 1 - core)
    me = dp * z_count + z

    greet(z, z_count, (dp_x, dp_y, dp_c))
    full_ref[me, 0:rows] = w_ref[0]
    full_ref[me, rows : 2 * rows] = w_ref[1]
    pad = jnp.zeros((block - 2 * rows, full_ref.shape[2]), full_ref.dtype)
    full_ref[me, 2 * rows : block] = pad
    full_ref[me, 2 * rows : 2 * rows + 2, 0 : v_ref.shape[1]] = v_ref[...]

    def copy(i, h, slot, target, sem):
        ref = full_ref.at[i, cut[h], :]
        return pltpu.make_async_remote_copy(
            src_ref=ref, dst_ref=ref, send_sem=send_sem.at[i, h, slot], recv_sem=sem.at[i, h],
            device_id=target, device_id_type=MESH,
        )

    def to_right(i, h):
        return copy(i, h, 0, (dp, z + 1), link_sem)

    def to_left(i, h):
        return copy(i, h, 1, (dp, z - 1), link_sem)

    def to_x(i, h):
        return copy(i, h, 2, (dp_x, z), link_sem)

    def to_y(i, h):
        return copy(i, h, 3, (dp_y, z), link_sem)

    def to_core(i, h):
        return copy(i, h, 4, (dp_c, z), core_sem)

    def spread_column(i):
        to_x(i, 0).start()
        to_y(i, 1).start()
        to_core(i, 0).start()
        to_core(i, 1).start()
        to_x(i, 1).start()
        to_y(i, 0).start()

    def wait_link(i, h):
        pltpu.make_async_remote_copy(
            src_ref=full_ref.at[i, cut[h], :], dst_ref=full_ref.at[i, cut[h], :],
            send_sem=send_sem.at[i, h, 4], recv_sem=link_sem.at[i, h],
            device_id=(dp_c, z), device_id_type=MESH,
        ).wait_recv()

    @pl.when(z < z_count - 1)
    def _():
        for h in range(2):
            to_right(me, h).start()

    @pl.when(z > 0)
    def _():
        for h in range(2):
            to_left(me, h).start()

    spread_column(me)
    for k in range(1, z_count):

        @pl.when(z - k >= 0)
        def _():
            i = me - k
            for h in range(2):
                wait_link(i, h)

            @pl.when(z < z_count - 1)
            def _():
                for h in range(2):
                    to_right(i, h).start()

            spread_column(i)

        @pl.when(z + k < z_count)
        def _():
            i = me + k
            for h in range(2):
                wait_link(i, h)

            @pl.when(z > 0)
            def _():
                for h in range(2):
                    to_left(i, h).start()

            spread_column(i)

    order = []
    for k in range(z_count):
        order.append(lax.rem(z + k, z_count))
    for zz in order:
        i = dp_x * z_count + zz
        wait_link(i, 0)
        to_y(i, 0).start()
        to_core(i, 0).start()
        i = dp_y * z_count + zz
        wait_link(i, 1)
        to_x(i, 1).start()
        to_core(i, 1).start()
    for zz in order:
        i = dp_x * z_count + zz
        wait_link(i, 1)
        to_core(i, 1).start()
        i = dp_y * z_count + zz
        wait_link(i, 0)
        to_core(i, 0).start()
    dp_d = column(1 - y, 1 - x, core)
    for zz in order:
        i = dp_d * z_count + zz
        for h in range(2):
            wait_link(i, h)
            to_core(i, h).start()
    for yy in range(2):
        for xx in range(2):
            for zz in range(z_count):
                i = column(yy, xx, 1 - core) * z_count + zz
                for h in range(2):
                    to_core(i, h).wait_recv()
    for yy in range(2):
        for xx in range(2):
            for zz in range(z_count):
                i = column(yy, xx, core) * z_count + zz
                for h in range(2):
                    to_core(i, h).wait_send()
    for zz in range(z_count):
        i = dp * z_count + zz
        for h in range(2):
            to_x(i, h).wait_send()
            to_y(i, h).wait_send()

        @pl.when((zz <= z) & (z < z_count - 1))
        def _():
            for h in range(2):
                to_right(i, h).wait_send()

        @pl.when((zz >= z) & (z > 0))
        def _():
            for h in range(2):
                to_left(i, h).wait_send()

        to_y(dp_x * z_count + zz, 0).wait_send()
        to_x(dp_y * z_count + zz, 1).wait_send()


def scatter_kernel(
    z_count, g_ref, gw_ref, gv_ref,
    sib_s, acc_s, own_s, xa_s, yb_s, oya_s, oxb_s, oxa_s, oyb_s, zl_s, zr_s,
    sib_send, sib_recv, xy_send, xy_recv, z_send, z_recv,
):
    y, x, core, z = place(z_count)
    dp = lax.axis_index("dp")
    block, width = g_ref.shape[1], g_ref.shape[2]
    half = xa_s.shape[1]
    top, low = pl.ds(0, half), pl.ds(half, block - half)
    dp_x, dp_y, dp_c = column(y, 1 - x, core), column(1 - y, x, core), column(y, x, 1 - core)
    kinds = ((y, x), (y, 1 - x), (1 - y, x), (1 - y, 1 - x))
    order = []
    for k in range((z_count + 1) // 2):
        order.append(z_count - 1 - k)
        if k != z_count - 1 - k:
            order.append(k)

    greet(z, z_count, (dp_x, dp_y, dp_c))

    def to_core(kind):
        yy, xx = kinds[kind]
        return pltpu.make_async_remote_copy(
            src_ref=g_ref.at[pl.ds(column(yy, xx, 1 - core) * z_count, z_count)],
            dst_ref=sib_s.at[kind],
            send_sem=sib_send.at[kind], recv_sem=sib_recv.at[kind],
            device_id=(dp_c, z), device_id_type=MESH,
        )

    def across(kind, rows, dst, slot, target, t):
        return pltpu.make_async_remote_copy(
            src_ref=acc_s.at[kind, t, rows, :], dst_ref=dst.at[t],
            send_sem=xy_send.at[slot, t], recv_sem=xy_recv.at[slot, t],
            device_id=(target, z), device_id_type=MESH,
        )

    def diag_top(t):
        return across(3, top, xa_s, 0, dp_y, t)

    def diag_low(t):
        return across(3, low, yb_s, 1, dp_x, t)

    def ycol_top(t):
        return across(2, top, oya_s, 2, dp_y, t)

    def xcol_low(t):
        return across(1, low, oxb_s, 3, dp_x, t)

    def xcol_top(t):
        return across(1, top, oxa_s, 4, dp_x, t)

    def ycol_low(t):
        return across(2, low, oyb_s, 5, dp_y, t)

    def to_right(t):
        return pltpu.make_async_remote_copy(
            src_ref=acc_s.at[0, t], dst_ref=zl_s.at[t],
            send_sem=z_send.at[0, t], recv_sem=z_recv.at[0, t],
            device_id=(dp, z + 1), device_id_type=MESH,
        )

    def to_left(t):
        return pltpu.make_async_remote_copy(
            src_ref=acc_s.at[0, t], dst_ref=zr_s.at[t],
            send_sem=z_send.at[1, t], recv_sem=z_recv.at[1, t],
            device_id=(dp, z - 1), device_id_type=MESH,
        )

    def chip_sum(kind, t):
        yy, xx = kinds[kind]
        mine = g_ref[column(yy, xx, core) * z_count + t].astype(F32)
        return mine + sib_s[kind, t].astype(F32)

    for kind in (3, 1, 2, 0):
        to_core(kind).start()
    to_core(3).wait_recv()
    for t in order:
        acc_s[3, t] = chip_sum(3, t).astype(BF)
        diag_top(t).start()
        diag_low(t).start()
    to_core(1).wait_recv()
    for t in order:
        acc_s[1, t] = chip_sum(1, t).astype(BF)
        xcol_low(t).start()
    to_core(2).wait_recv()
    for t in order:
        acc_s[2, t] = chip_sum(2, t).astype(BF)
        ycol_top(t).start()
    to_core(0).wait_recv()
    for t in order:
        own_s[t] = chip_sum(0, t)
    for t in order:
        diag_top(t).wait_recv()
        acc_s[1, t, top] = (acc_s[1, t, top].astype(F32) + xa_s[t].astype(F32)).astype(BF)
        xcol_top(t).start()
        diag_low(t).wait_recv()
        acc_s[2, t, low] = (acc_s[2, t, low].astype(F32) + yb_s[t].astype(F32)).astype(BF)
        ycol_low(t).start()
    for t in order:
        xcol_low(t).wait_recv()
        ycol_top(t).wait_recv()
        xcol_top(t).wait_recv()
        ycol_low(t).wait_recv()
        own_s[t, top] += oya_s[t].astype(F32) + oxa_s[t].astype(F32)
        own_s[t, low] += oxb_s[t].astype(F32) + oyb_s[t].astype(F32)

        @pl.when(t > z)
        def _():
            @pl.when(z > 0)
            def _():
                to_right(t).wait_recv()
                acc_s[0, t] = (own_s[t] + zl_s[t].astype(F32)).astype(BF)

            @pl.when(z == 0)
            def _():
                acc_s[0, t] = own_s[t].astype(BF)

            to_right(t).start()

        @pl.when(t < z)
        def _():
            @pl.when(z < z_count - 1)
            def _():
                to_left(t).wait_recv()
                acc_s[0, t] = (own_s[t] + zr_s[t].astype(F32)).astype(BF)

            @pl.when(z == z_count - 1)
            def _():
                acc_s[0, t] = own_s[t].astype(BF)

            to_left(t).start()

    @pl.when(z > 0)
    def _():
        to_right(z).wait_recv()
        own_s[z] += zl_s[z].astype(F32)

    @pl.when(z < z_count - 1)
    def _():
        to_left(z).wait_recv()
        own_s[z] += zr_s[z].astype(F32)

    rows = gw_ref.shape[1]
    gw_ref[0] = own_s[z, 0:rows]
    gw_ref[1] = own_s[z, rows : 2 * rows]
    gv_ref[...] = own_s[z, 2 * rows : 2 * rows + 2, 0 : gv_ref.shape[1]]

    for kind in range(4):
        to_core(kind).wait_send()
    for t in range(z_count):
        for one in (diag_top, diag_low, ycol_top, xcol_low, xcol_top, ycol_low):
            one(t).wait_send()

        @pl.when(t > z)
        def _():
            to_right(t).wait_send()

        @pl.when(t < z)
        def _():
            to_left(t).wait_send()


def gather(w, v, z_count, devices):
    rows, d = w.shape[1], w.shape[2]
    block = 2 * rows + 16
    return pl.pallas_call(
        partial(gather_kernel, z_count),
        in_specs=[pl.BlockSpec(memory_space=pltpu.VMEM)] * 2,
        out_specs=pl.BlockSpec(memory_space=pltpu.VMEM),
        out_shape=jax.ShapeDtypeStruct((devices, block, d), BF),
        scratch_shapes=[
            pltpu.SemaphoreType.DMA((devices, 2)),
            pltpu.SemaphoreType.DMA((devices, 2)),
            pltpu.SemaphoreType.DMA((devices, 2, 5)),
        ],
        compiler_params=pltpu.CompilerParams(
            collective_id=0, has_side_effects=True, vmem_limit_bytes=32 << 20
        ),
        name="gather",
    )(w, v)


def scatter(g, z_count, rows, vrow):
    devices, block, d = g.shape
    half = (block // 2 + 15) // 16 * 16
    low = block - half
    return pl.pallas_call(
        partial(scatter_kernel, z_count),
        in_specs=[pl.BlockSpec(memory_space=pltpu.VMEM)],
        out_specs=[pl.BlockSpec(memory_space=pltpu.VMEM)] * 2,
        out_shape=[
            jax.ShapeDtypeStruct((2, rows, d), F32),
            jax.ShapeDtypeStruct((2, vrow), F32),
        ],
        scratch_shapes=[
            pltpu.VMEM((4, z_count, block, d), BF),
            pltpu.VMEM((4, z_count, block, d), BF),
            pltpu.VMEM((z_count, block, d), F32),
            pltpu.VMEM((z_count, half, d), BF),
            pltpu.VMEM((z_count, low, d), BF),
            pltpu.VMEM((z_count, half, d), BF),
            pltpu.VMEM((z_count, low, d), BF),
            pltpu.VMEM((z_count, half, d), BF),
            pltpu.VMEM((z_count, low, d), BF),
            pltpu.VMEM((z_count, block, d), BF),
            pltpu.VMEM((z_count, block, d), BF),
            pltpu.SemaphoreType.DMA((4,)),
            pltpu.SemaphoreType.DMA((4,)),
            pltpu.SemaphoreType.DMA((6, z_count)),
            pltpu.SemaphoreType.DMA((6, z_count)),
            pltpu.SemaphoreType.DMA((2, z_count)),
            pltpu.SemaphoreType.DMA((2, z_count)),
        ],
        compiler_params=pltpu.CompilerParams(
            collective_id=1, has_side_effects=True, vmem_limit_bytes=48 << 20
        ),
        name="scatter",
    )(g)


def compute(x, cot, full, lengths, d, ff, vlen):
    n = lengths.shape[0]
    mrows = 4 * d + 2 * ff
    img = pl.BlockSpec((1, ROWS, NBLK, SUBL, d), lambda i: (i, 0, 0, 0, 0))
    whole = pl.BlockSpec(full.shape, lambda i: (0, 0, 0), pipeline_mode=pl.Buffered(1))
    shp = (n, ROWS, NBLK, SUBL, d)
    return pl.pallas_call(
        partial(kernel, (d, ff)),
        grid=(n,),
        in_specs=[pl.BlockSpec(memory_space=pltpu.SMEM), img, img, whole],
        out_specs=[img, img, whole],
        out_shape=[
            jax.ShapeDtypeStruct(shp, F32),
            jax.ShapeDtypeStruct(shp, F32),
            jax.ShapeDtypeStruct(full.shape, BF),
        ],
        scratch_shapes=[
            pltpu.VMEM((2, mrows, d), BF),
            pltpu.VMEM((2, 8, vlen), F32),
            pltpu.VMEM((2, d, mrows), F32),
            pltpu.VMEM((2, 8, vlen), F32),
            pltpu.VMEM((2, S, d), BF),
            pltpu.VMEM((2, S, 3 * d), BF),
            pltpu.VMEM((2, NBLK, HEADS, BLOCK, 128), BF),
            pltpu.VMEM((2, S, d), BF),
            pltpu.VMEM((2, S, d), F32),
            pltpu.VMEM((2, S, d), BF),
            pltpu.VMEM((2, S, ff), BF),
            pltpu.VMEM((2, S, ff), BF),
            pltpu.VMEM((NBLK, ROWS, SUBL, d), F32),
            pltpu.VMEM((ROWS, NBLK, SUBL, d), F32),
            pltpu.VMEM((S, d), BF),
            pltpu.VMEM((S, ff), BF),
            pltpu.VMEM((S, d), F32),
            pltpu.VMEM((S, d), BF),
            pltpu.VMEM((S, d), BF),
            pltpu.VMEM((S, 3 * d), BF),
        ],
        compiler_params=pltpu.CompilerParams(
            dimension_semantics=("arbitrary",), vmem_limit_bytes=63 << 20
        ),
        name="layers",
    )(lengths, x.reshape(shp), cot.reshape(shp), full)


def to_blocks(w, v):
    pad = jnp.pad(v[:, :], ((0, 0), (0, w.shape[2] - v.shape[1])))
    tail = jnp.pad(pad, ((0, 14), (0, 0)))
    return jnp.concatenate([w[0], w[1], tail], 0)


def body(z_count, dp_count, inputs, matrices, vectors, lengths, cotangent):
    d = inputs.shape[1]
    devices = z_count * dp_count
    rows, vrow = matrices.shape[1], vectors.shape[1]
    vlen = vrow * devices
    ff = (rows * devices - 4 * d) // 2
    own_kernels = dp_count == 8
    if own_kernels:
        full = gather(matrices, vectors, z_count, devices)
    else:
        full = lax.all_gather(to_blocks(matrices, vectors), ("dp", "sub"), axis=0)
    out, gin, gb = compute(inputs, cotangent, full, lengths, d, ff, vlen)
    if own_kernels:
        gw, gv = scatter(gb, z_count, rows, vrow)
    else:
        g = lax.psum_scatter(gb.astype(F32), ("dp", "sub"), scatter_dimension=0, tiled=True)[0]
        gw = g[: 2 * rows].reshape(2, rows, d)
        gv = g[2 * rows : 2 * rows + 2, :vrow]
    return (out.reshape(inputs.shape), gin.reshape(inputs.shape), gw, gv)


def solution(mesh):
    split = ("dp", "sub")
    return jax.shard_map(
        partial(body, mesh.shape["sub"], mesh.shape["dp"]),
        mesh=mesh,
        in_specs=(P(split, None), P(None, split, None), P(None, split), P(split), P(split, None)),
        out_specs=(P(split, None), P(split, None), P(None, split, None), P(None, split)),
        check_vma=False,
    )
```

```python
from functools import partial

import jax
import jax.numpy as jnp
from jax import lax
from jax.experimental import pallas as pl
from jax.experimental.pallas import tpu as pltpu
from jax.sharding import PartitionSpec as P

HEADS = 2
COLS = 96
ROWS = 12
SUBL = 8
BLOCK = 96
NBLK = 12
S = COLS * ROWS
LOG2E = 1.4426950408889634
BF = jnp.bfloat16
F32 = jnp.float32
STATIC = False
NB = (12,12,6,6,12,12)


def mm(a, b, ca, cb):
    return lax.dot_general(a, b, (((ca,), (cb,)), ((), ())), preferred_element_type=F32)


def standardize(v):
    c = v - jnp.mean(v, -1, keepdims=True)
    r = lax.rsqrt(jnp.mean(c * c, -1, keepdims=True) + 1e-05)
    return c * r, r


def rowsum8(v):
    return jnp.sum(v.reshape(v.shape[0] // 8, 8, v.shape[1]), axis=0)


def live_mask(length, slab, width):
    row = lax.broadcasted_iota(jnp.int32, (ROWS, SUBL, width), 0)
    col = lax.broadcasted_iota(jnp.int32, (ROWS, SUBL, width), 1)
    return row * COLS + col + slab * SUBL < length


def kernel(dims, own, z_count, *refs):
    d, ff = dims
    len_ref, x_ref, cot_ref, w_ref, v_ref, out_ref, gin_ref, gw_ref, gvo_ref = refs[:9]
    (
        vs_s, gwt_ref, gv_ref, n1_s, pk_s, pt_s, mix_s, mid_s, n2_s, act_s, dact_s,
        x1_s, gy0_s, gy_s, gup_s, gmid_s, gmidl_s, gmix_s, gpk_s,
    ) = refs[9:28]
    img = pl.program_id(0)
    last = img == pl.num_programs(0) - 1
    length = len_ref[img]
    hw = d // HEADS
    qs = hw ** -0.5
    if own:
        move = Moves(z_count, w_ref, v_ref, gwt_ref, gv_ref, vs_s, gw_ref, gvo_ref, refs[28:])
        wpart = move.weights
    else:

        def wpart(l, a, b):
            return w_ref[l, a:b, :]

    @pl.when(img == 0)
    def _():
        gwt_ref[...] = jnp.zeros_like(gwt_ref)
        gv_ref[...] = jnp.zeros_like(gv_ref)
        if own:
            move.gather_first()
        else:
            vs_s[:, 0:1, :] = v_ref[...]

    def wqkv(l):
        return wpart(l, 0, 3 * d)

    def wout(l):
        return wpart(l, 3 * d, 4 * d)

    def vec(l, i, n=1):
        return vs_s[l, 0:1, i * d : (i + n) * d]

    tril_b = lax.broadcasted_iota(jnp.int32, (BLOCK, BLOCK), 0)
    tril_a = lax.broadcasted_iota(jnp.int32, (BLOCK, BLOCK), 1)
    masks = (
        tril_b <= tril_a,
        (tril_b <= tril_a) & ((tril_b & (SUBL - 1)) == (tril_a & (SUBL - 1))),
    )

    def load_x(l, c, nb):
        if l == 0:
            return x_ref[0, pl.ds(c * nb, nb)].reshape(nb * BLOCK, d)
        return x1_s[pl.ds(c * nb, nb)].reshape(nb * BLOCK, d)

    def store_perm(ref, c, nb, val, lead=()):
        v4 = val.reshape(nb, NBLK, SUBL, d)
        for b in range(nb):
            ref[lead + (slice(None), c * nb + b)] = v4[b]

    def rows(c, nb):
        if isinstance(c, int):
            return pl.ds(c * nb * BLOCK, nb * BLOCK)
        return pl.ds(pl.multiple_of(c * nb * BLOCK, BLOCK), nb * BLOCK)

    def loop(n, step):
        if STATIC or n == 1:
            for c in range(n):
                step(c, 0)
        else:
            lax.fori_loop(0, n, step, 0)

    def qkv_fwd(l, nb):
        def step(c, _):
            s = rows(c, nb)
            xh, _r = standardize(load_x(l, c, nb))
            n1 = (xh * vec(l, 0) + vec(l, 1)).astype(BF)
            n1_s[l, s, :] = n1
            pk_s[l, s, :] = mm(n1, wqkv(l), 1, 1).astype(BF)
            return 0

        loop(NBLK // nb, step)

    def heads_of(packed):
        return [
            tuple(packed[:, i * d + h * hw : i * d + (h + 1) * hw] for i in range(3))
            for h in range(HEADS)
        ]

    def attn_fwd(l, nb):
        mask = masks[l]

        def step(c, _):
            each = [(b, h) for b in range(nb) for h in range(HEADS)]
            qkv = []
            for b in range(nb):
                qkv += heads_of(pk_s[l, rows(c * nb + b, 1), :])
            scores = [mm(k, q, 1, 1) for q, k, v in qkv]
            ps = []
            for st in scores:
                st = jnp.where(mask, st, -1e30)
                p = jnp.exp2((st - jnp.max(st, 0, keepdims=True)) * (qs * LOG2E))
                ps.append((p * (1.0 / jnp.sum(p, 0, keepdims=True))).astype(BF))
            mixed = [mm(p, v, 0, 0).astype(BF) for p, (q, k, v) in zip(ps, qkv)]
            for (b, h), p, m in zip(each, ps, mixed):
                pt_s[l, c * nb + b, h, :, 0:BLOCK] = p
                mix_s[l, rows(c * nb + b, 1), h * hw : (h + 1) * hw] = m
            return 0

        loop(NBLK // nb, step)

    def ffn_fwd(l, nb):
        def step(c, _):
            s = rows(c, nb)
            mid = load_x(l, c, nb) + mm(mix_s[l, s, :], wout(l), 1, 1) + vec(l, 2)
            mid_s[l, s, :] = mid
            xh, _r = standardize(mid)
            n2 = (xh * vec(l, 3) + vec(l, 4)).astype(BF)
            n2_s[l, s, :] = n2
            y = mid + vec(l, 5)
            for f in range(ff // d):
                h = mm(n2, wpart(l, (4 + f) * d, (5 + f) * d), 1, 1) + vec(l, 6 + f)
                phi = lax.erf(h * (2 ** -0.5)) * 0.5 + 0.5
                e = jnp.exp2(h * h * (-0.5 * LOG2E)) * 0.3989422804014327
                act = (h * phi).astype(BF)
                act_s[l, s, f * d : (f + 1) * d] = act
                dact_s[l, s, f * d : (f + 1) * d] = (phi + h * e).astype(BF)
            y = y + mm(act_s[l, s, :], wpart(l, 4 * d + ff, 4 * d + 2 * ff), 1, 0)
            if l == 0:
                store_perm(x1_s, c, nb, y)
            else:
                y4 = y.reshape(nb, NBLK, SUBL, d)
                for b in range(nb):
                    live = live_mask(length, c * nb + b, d)
                    out_ref[0, :, c * nb + b] = jnp.where(live, y4[b], 0.0)
            return 0

        loop(NBLK // nb, step)

    def acc_vec(l, i, val, n=1):
        gv_ref[l, :, i * d : (i + n) * d] += rowsum8(val)

    def norm_back(l, gi, v, gn):
        xh, r = standardize(v)
        acc_vec(l, gi, gn * xh)
        acc_vec(l, gi + 1, gn)
        e = gn * vec(l, gi)
        me = jnp.mean(e, -1, keepdims=True)
        mx = jnp.mean(e * xh, -1, keepdims=True)
        return r * (e - me - xh * mx)

    def ffn_bwd(l, nb):
        def step(c, _):
            s = rows(c, nb)
            if l == 0:
                gy = gy0_s[pl.ds(c * nb, nb)].reshape(nb * BLOCK, d)
            else:
                parts = []
                for b in range(nb):
                    live = live_mask(length, c * nb + b, d)
                    part = jnp.where(live, cot_ref[0, :, c * nb + b], 0.0)
                    parts.append(part.reshape(BLOCK, d))
                gy = jnp.concatenate(parts, 0) if nb > 1 else parts[0]
            acc_vec(l, 5, gy)
            gyl = gy.astype(BF)
            gy_s[s, :] = gyl
            for f in range(ff // d):
                wd = wpart(l, 4 * d + ff + f * d, 4 * d + ff + (f + 1) * d)
                gup = mm(gyl, wd, 1, 1) * dact_s[l, s, f * d : (f + 1) * d].astype(F32)
                acc_vec(l, 6 + f, gup)
                gupl = gup.astype(BF)
                gup_s[s, f * d : (f + 1) * d] = gupl
            gn2 = mm(gup_s[s, :], wpart(l, 4 * d, 4 * d + ff), 1, 0)
            gmid = gy + norm_back(l, 3, mid_s[l, s, :], gn2)
            gmid_s[s, :] = gmid
            acc_vec(l, 2, gmid)
            gml = gmid.astype(BF)
            gmidl_s[s, :] = gml
            gmix_s[s, :] = mm(gml, wout(l), 1, 0).astype(BF)
            return 0

        loop(NBLK // nb, step)

    def attn_bwd(l, nb):
        def step(c, _):
            each = [(b, h) for b in range(nb) for h in range(HEADS)]
            qkv, gms = [], []
            for b in range(nb):
                at = rows(c * nb + b, 1)
                qkv += heads_of(pk_s[l, at, :])
                gm = gmix_s[at, :]
                gms += [gm[:, h * hw : (h + 1) * hw] for h in range(HEADS)]
            pts = [pt_s[l, c * nb + b, h, :, 0:BLOCK] for b, h in each]
            gps = [mm(v, gm, 1, 1) for (q, k, v), gm in zip(qkv, gms)]
            gss = []
            for pt, gp in zip(pts, gps):
                pf = pt.astype(F32)
                pg = pf * gp
                gss.append(((pg - pf * jnp.sum(pg, 0, keepdims=True)) * qs).astype(BF))
            gv = [mm(pt, gm, 1, 0).astype(BF) for pt, gm in zip(pts, gms)]
            gk = [mm(gs, q, 1, 0).astype(BF) for gs, (q, k, v) in zip(gss, qkv)]
            gq = [mm(gs, k, 0, 0).astype(BF) for gs, (q, k, v) in zip(gss, qkv)]
            for n, (b, h) in enumerate(each):
                for i, g in enumerate((gq, gk, gv)):
                    gpk_s[rows(c * nb + b, 1), i * d + h * hw : i * d + (h + 1) * hw] = g[n]
            return 0

        loop(NBLK // nb, step)

    def qkv_bwd(l, nb):
        def step(c, _):
            s = rows(c, nb)
            gn1 = mm(gpk_s[s, :], wqkv(l), 1, 0)
            gx = gmid_s[s, :] + norm_back(l, 0, load_x(l, c, nb), gn1)
            if l == 0:
                gin_ref[0, pl.ds(c * nb, nb)] = gx.reshape(nb, NBLK, SUBL, d)
            else:
                store_perm(gy0_s, c, nb, gx)
            return 0

        loop(NBLK // nb, step)

    def wgrads(l):
        gwt_ref[l, :, 0 : 3 * d] += mm(n1_s[l], gpk_s[...], 0, 0)
        gwt_ref[l, :, 3 * d : 4 * d] += mm(mix_s[l], gmidl_s[...], 0, 0)
        gwt_ref[l, :, 4 * d : 4 * d + ff] += mm(n2_s[l], gup_s[...], 0, 0)
        gwt_ref[l, :, 4 * d + ff :] += mm(gy_s[...], act_s[l], 0, 0)

    def between(first, step):
        if own:
            pl.when(img == 0 if first else last)(step)

    for l in range(2):
        qkv_fwd(l, NB[0])
        if l == 0:
            between(True, lambda: move.gather_across(1))
        attn_fwd(l, NB[1])
        if l == 0:
            between(True, lambda: move.gather_diagonal(1))
        ffn_fwd(l, NB[2])
        if l == 0:
            between(True, lambda: move.gather_end(1))
    for l in (1, 0):
        ffn_bwd(l, NB[3])
        if l == 0:
            between(False, lambda: move.sum_chip(1))
        attn_bwd(l, NB[4])
        if l == 0:
            between(False, lambda: move.sum_across(1))
        qkv_bwd(l, NB[5])
        if l == 0:
            between(False, lambda: move.sum_column(1))
        wgrads(l)
        between(False, lambda: move.sum_start(l))

    @pl.when(last)
    def _():
        if own:
            move.sum_chip(0)
            move.sum_end(1)
            move.sum_across(0)
            move.sum_column(0)
            move.sum_end(0)
            move.drain()
        else:
            for l in range(2):
                gw_ref[l] = gwt_ref[l].T
                gvo_ref[l] = jnp.sum(gv_ref[l], 0, keepdims=True)


MESH = pl.DeviceIdType.MESH


def column(y, x, core):
    return (y * 2 + x) * 2 + core


class Moves:
    def __init__(self, z_count, w_ref, v_ref, gwt_ref, gv_ref, vs_s, gw_ref, gvo_ref, refs):
        self.z_count = z_count
        self.w_ref, self.v_ref, self.gwt_ref, self.gv_ref = w_ref, v_ref, gwt_ref, gv_ref
        self.vs_s, self.gw_ref, self.gvo_ref = vs_s, gw_ref, gvo_ref
        (
            self.full_s, self.gb_s, self.sib_s, self.own_s, self.diag_top_s, self.diag_low_s,
            self.cols_s, self.zr_s,
            self.ag_link, self.ag_core, self.ag_z, self.ag_x, self.ag_y, self.ag_c,
            self.rs_core_send, self.rs_core_recv, self.rs_send, self.rs_recv,
            self.rs_z_send, self.rs_z_recv,
        ) = refs
        self.rows, self.d = w_ref.shape[1], w_ref.shape[2]
        self.block = self.full_s.shape[2]
        self.half = self.diag_top_s.shape[2]
        self.devices = self.full_s.shape[1]
        self.vrow = v_ref.shape[1]
        self.vlen = self.vrow * self.devices
        dp, z = lax.axis_index("dp"), lax.axis_index("sub")
        self.dp, self.z = dp, z
        self.core = dp % 2
        self.x = dp // 2 % 2
        self.y = dp // 4
        y, x = self.y, self.x
        self.chips = ((y, x), (y, 1 - x), (1 - y, x), (1 - y, 1 - x))
        self.dp_x = column(y, 1 - x, self.core)
        self.dp_y = column(1 - y, x, self.core)
        self.dp_c = column(y, x, 1 - self.core)
        self.cut = (pl.ds(0, self.half), pl.ds(self.half, self.block - self.half))
        near = [0]
        for k in range(1, z_count // 2 + 1):
            near.append(k)
            if z_count - k != k:
                near.append(z_count - k)
        self.near = near

    def zz(self, k):
        return lax.rem(self.z + k, self.z_count)

    def index(self, kind, t, core=None):
        yy, xx = self.chips[kind]
        return column(yy, xx, self.core if core is None else core) * self.z_count + t

    def slot(self, kind, t):
        yy, xx = self.chips[kind]
        return (yy * 2 + xx) * self.z_count + t

    def weights(self, l, a, b):
        parts, rows = [], self.rows
        while a < b:
            i = a // rows
            e = min(b, (i + 1) * rows)
            parts.append(self.full_s[l, i, a - i * rows : e - i * rows, :])
            a = e
        return jnp.concatenate(parts, 0)

    def remote(self, src, dst, send, recv, target):
        return pltpu.make_async_remote_copy(
            src_ref=src, dst_ref=dst, send_sem=send, recv_sem=recv,
            device_id=target, device_id_type=MESH,
        )

    def ag_copy(self, l, kind, t, way, part=None):
        i, s = self.index(kind, t), self.slot(kind, t)
        ref = self.full_s.at[l, i] if part is None else self.full_s.at[l, i, self.cut[part], :]
        if way == "c":
            return self.remote(
                ref, ref, self.ag_c.at[l, s], self.ag_core.at[l, s], (self.dp_c, self.z)
            )
        send = self.ag_x if way == "x" else self.ag_y
        target = (self.dp_x if way == "x" else self.dp_y, self.z)
        return self.remote(ref, ref, send.at[l, s], self.ag_link.at[l, 1 if part else 0, s], target)

    def ag_along(self, l, k):
        ref = self.full_s.at[l, self.index(0, self.z)]
        s = self.slot(0, self.z)
        return self.remote(
            ref, ref, self.ag_z.at[l, k], self.ag_link.at[l, 0, s], (self.dp, self.zz(k))
        )

    def ag_wait(self, l, kind, t, part=None):
        i, s = self.index(kind, t), self.slot(kind, t)
        ref = self.full_s.at[l, i] if part is None else self.full_s.at[l, i, self.cut[part], :]
        self.remote(
            ref, ref, self.ag_c.at[l, s], self.ag_link.at[l, 1 if part else 0, s],
            (self.dp_c, self.z),
        ).wait_recv()

    def gather_along(self, l):
        for k in self.near[1:]:
            self.ag_along(l, k).start()

    def gather_spread(self, l):
        for k in self.near:
            t = self.zz(k)
            if k:
                self.ag_wait(l, 0, t)
            for way in "xyc":
                self.ag_copy(l, 0, t, way).start()

    def gather_across(self, l):
        for k in self.near:
            t = self.zz(k)
            self.ag_wait(l, 1, t)
            self.ag_copy(l, 1, t, "y", 0).start()
            self.ag_copy(l, 1, t, "c").start()
            self.ag_wait(l, 2, t)
            self.ag_copy(l, 2, t, "x", 1).start()
            self.ag_copy(l, 2, t, "c").start()

    def gather_diagonal(self, l):
        for k in self.near:
            t = self.zz(k)
            self.ag_wait(l, 3, t, 0)
            self.ag_wait(l, 3, t, 1)
            self.ag_copy(l, 3, t, "c").start()

    def gather_end(self, l):
        for kind in range(4):
            for t in range(self.z_count):
                i, s = self.index(kind, t, 1 - self.core), self.slot(kind, t)
                ref = self.full_s.at[l, i]
                self.remote(
                    ref, ref, self.ag_c.at[l, s], self.ag_core.at[l, s], (self.dp_c, self.z)
                ).wait_recv()
        vrow, vlen, rows = self.vrow, self.vlen, self.rows
        self.vs_s[l] = jnp.zeros((8, vlen), F32)
        for i in range(self.devices):
            part = self.full_s[l, i, rows : self.block, 0:128].astype(F32)[0:8]
            at = i * vrow // 128 * 128
            wide = jnp.concatenate([part, jnp.zeros_like(part)], 1)
            if i * vrow > at:
                wide = pltpu.roll(wide, i * vrow - at, 1)
            n = min(256, vlen - at)
            self.vs_s[l, 0:1, at : at + n] += wide[0:1, 0:n]

    def gather_first(self):
        barrier = pltpu.get_barrier_semaphore()
        partners = [(p, self.z) for p in (self.dp_x, self.dp_y, self.dp_c)]
        partners += [(self.dp, self.zz(k)) for k in self.near[1:]]
        for p in partners:
            pl.semaphore_signal(barrier, inc=1, device_id=p, device_id_type=MESH)
        me, rows = self.index(0, self.z), self.rows
        for l in range(2):
            self.full_s[l, me, 0:rows] = self.w_ref[l]
            tail = jnp.zeros((self.block - rows, self.d - self.vrow), BF)
            v = self.v_ref[l : l + 1, :].astype(F32)
            v = jnp.concatenate([v, jnp.zeros((self.block - rows - 1, self.vrow), F32)], 0)
            self.full_s[l, me, rows : self.block, :] = jnp.concatenate([v.astype(BF), tail], 1)
        pl.semaphore_wait(barrier, len(partners))
        self.gather_along(0)
        self.gather_spread(0)
        self.gather_along(1)
        self.gather_across(0)
        self.gather_spread(1)
        self.gather_diagonal(0)
        self.gather_end(0)

    def rs_core(self, l, kind):
        i = self.index(kind, 0, 1 - self.core)
        return self.remote(
            self.gb_s.at[l, pl.ds(i, self.z_count)], self.sib_s.at[l, kind],
            self.rs_core_send.at[l, kind], self.rs_core_recv.at[l, kind], (self.dp_c, self.z),
        )

    def rs_across(self, l, slot, t):
        kind, half, target, dst = (
            (3, 0, self.dp_y, self.diag_top_s.at[l, t]),
            (3, 1, self.dp_x, self.diag_low_s.at[l, t]),
            (2, 0, self.dp_y, self.cols_s.at[l, 0, t, self.cut[0], :]),
            (1, 1, self.dp_x, self.cols_s.at[l, 0, t, self.cut[1], :]),
            (1, 0, self.dp_x, self.cols_s.at[l, 1, t, self.cut[0], :]),
            (2, 1, self.dp_y, self.cols_s.at[l, 1, t, self.cut[1], :]),
        )[slot]
        return self.remote(
            self.gb_s.at[l, self.index(kind, t), self.cut[half], :], dst,
            self.rs_send.at[l, slot, t], self.rs_recv.at[l, slot, t], (target, self.z),
        )

    def rs_along(self, l, k):
        return self.remote(
            self.gb_s.at[l, self.index(0, self.zz(k))], self.zr_s.at[l, k - 1],
            self.rs_z_send.at[l, k], self.rs_z_recv.at[l, k], (self.dp, self.zz(k)),
        )

    def sum_start(self, l):
        rows, vrow, vlen = self.rows, self.vrow, self.vlen
        g = self.gwt_ref[l].T.astype(BF)
        gv = jnp.sum(self.gv_ref[l], 0, keepdims=True)
        gv = jnp.concatenate([gv, jnp.zeros((7, vlen), F32)], 0)
        for i in range(self.devices):
            self.gb_s[l, i, 0:rows] = g[i * rows : (i + 1) * rows]
            at = i * vrow // 128 * 128
            n = min(256, vlen - at)
            wide = gv[:, at : at + n]
            if n < 256:
                wide = jnp.concatenate([wide, jnp.zeros_like(wide)], 1)
            if i * vrow > at:
                wide = pltpu.roll(wide, 256 - (i * vrow - at), 1)
            wide = jnp.concatenate([wide, jnp.zeros_like(wide)], 0)
            self.gb_s[l, i, rows : self.block] = wide.astype(BF)
        for kind in (3, 1, 2, 0):
            self.rs_core(l, kind).start()

    def sum_chip(self, l):
        for kind, slots in ((3, (0, 1)), (1, (3,)), (2, (2,)), (0, ())):
            self.rs_core(l, kind).wait_recv()
            for t in range(self.z_count):
                i = self.index(kind, t)
                both = self.gb_s[l, i].astype(F32) + self.sib_s[l, kind, t].astype(F32)
                if kind == 0:
                    self.own_s[l, t] = both
                else:
                    self.gb_s[l, i] = both.astype(BF)
                for slot in slots:
                    self.rs_across(l, slot, t).start()

    def sum_across(self, l):
        for t in range(self.z_count):
            for slot, kind, half, ref in (
                (0, 1, 0, self.diag_top_s), (1, 2, 1, self.diag_low_s),
            ):
                self.rs_across(l, slot, t).wait_recv()
                i, cut = self.index(kind, t), self.cut[half]
                both = self.gb_s[l, i, cut].astype(F32) + ref[l, t].astype(F32)
                self.gb_s[l, i, cut] = both.astype(BF)
                self.rs_across(l, 4 if half == 0 else 5, t).start()

    def sum_column(self, l):
        for k in self.near[1:] + [0]:
            t = self.zz(k)
            for slot in (2, 3, 4, 5):
                self.rs_across(l, slot, t).wait_recv()
            total = self.own_s[l, t]
            for a in range(2):
                total = total + self.cols_s[l, a, t].astype(F32)
            if k:
                self.gb_s[l, self.index(0, t)] = total.astype(BF)
                self.rs_along(l, k).start()
            else:
                self.own_s[l, t] = total

    def sum_end(self, l):
        for k in self.near[1:]:
            self.rs_along(l, k).wait_recv()
        total = self.own_s[l, self.z]
        for k in self.near[1:]:
            total = total + self.zr_s[l, k - 1].astype(F32)
        self.gw_ref[l] = total[0 : self.rows]
        self.gvo_ref[l : l + 1, :] = total[self.rows : self.rows + 1, 0 : self.vrow]

    def drain(self):
        for l in range(2):
            for k in self.near[1:]:
                self.ag_along(l, k).wait_send()
                self.rs_along(l, k).wait_send()
            for t in range(self.z_count):
                for kind in range(4):
                    self.ag_copy(l, kind, t, "c").wait_send()
                self.ag_copy(l, 0, t, "x").wait_send()
                self.ag_copy(l, 0, t, "y").wait_send()
                self.ag_copy(l, 1, t, "y", 0).wait_send()
                self.ag_copy(l, 2, t, "x", 1).wait_send()
                for slot in range(6):
                    self.rs_across(l, slot, t).wait_send()
            for kind in range(4):
                self.rs_core(l, kind).wait_send()


def compute(x, cot, w, v, lengths, dims, own, z_count):
    d, ff = dims
    n = lengths.shape[0]
    mrows, vlen = 4 * d + 2 * ff, 6 * d + ff
    img = pl.BlockSpec((1, ROWS, NBLK, SUBL, d), lambda i: (i, 0, 0, 0, 0))
    shp = (n, ROWS, NBLK, SUBL, d)

    def whole(shape):
        zero = (0,) * len(shape)
        return pl.BlockSpec(shape, lambda i: zero, pipeline_mode=pl.Buffered(1))

    scratch = [
        pltpu.VMEM((2, 8, vlen), F32),
        pltpu.VMEM((2, d, mrows), F32),
        pltpu.VMEM((2, 8, vlen), F32),
        pltpu.VMEM((2, S, d), BF),
        pltpu.VMEM((2, S, 3 * d), BF),
        pltpu.VMEM((2, NBLK, HEADS, BLOCK, 128), BF),
        pltpu.VMEM((2, S, d), BF),
        pltpu.VMEM((2, S, d), F32),
        pltpu.VMEM((2, S, d), BF),
        pltpu.VMEM((2, S, ff), BF),
        pltpu.VMEM((2, S, ff), BF),
        pltpu.VMEM((NBLK, ROWS, SUBL, d), F32),
        pltpu.VMEM((ROWS, NBLK, SUBL, d), F32),
        pltpu.VMEM((S, d), BF),
        pltpu.VMEM((S, ff), BF),
        pltpu.VMEM((S, d), F32),
        pltpu.VMEM((S, d), BF),
        pltpu.VMEM((S, d), BF),
        pltpu.VMEM((S, 3 * d), BF),
    ]
    if own:
        rows, vrow = w.shape[1], v.shape[1]
        devices = mrows // rows
        block = rows + 16
        half = (block // 2 + 15) // 16 * 16
        zc = z_count
        dma = pltpu.SemaphoreType.DMA
        scratch += [
            pltpu.VMEM((2, devices, block, d), BF),
            pltpu.VMEM((2, devices, block, d), BF),
            pltpu.VMEM((2, 4, zc, block, d), BF),
            pltpu.VMEM((2, zc, block, d), F32),
            pltpu.VMEM((2, zc, half, d), BF),
            pltpu.VMEM((2, zc, block - half, d), BF),
            pltpu.VMEM((2, 2, zc, block, d), BF),
            pltpu.VMEM((2, zc - 1, block, d), BF),
            dma((2, 2, 4 * zc)), dma((2, 4 * zc)), dma((2, zc)),
            dma((2, 4 * zc)), dma((2, 4 * zc)), dma((2, 4 * zc)),
            dma((2, 4)), dma((2, 4)), dma((2, 6, zc)), dma((2, 6, zc)),
            dma((2, zc)), dma((2, zc)),
        ]
        gw_shape, gv_shape = (2, rows, d), (2, vrow)
    else:
        gw_shape, gv_shape = (2, mrows, d), (2, 1, vlen)
    return pl.pallas_call(
        partial(kernel, dims, own, z_count),
        grid=(n,),
        in_specs=[pl.BlockSpec(memory_space=pltpu.SMEM), img, img, whole(w.shape), whole(v.shape)],
        out_specs=[img, img, whole(gw_shape), whole(gv_shape)],
        out_shape=[
            jax.ShapeDtypeStruct(shp, F32),
            jax.ShapeDtypeStruct(shp, F32),
            jax.ShapeDtypeStruct(gw_shape, F32),
            jax.ShapeDtypeStruct(gv_shape, F32),
        ],
        scratch_shapes=scratch,
        compiler_params=pltpu.CompilerParams(
            dimension_semantics=("arbitrary",),
            vmem_limit_bytes=63 << 20,
            collective_id=0 if own else None,
            has_side_effects=own,
        ),
        name="layers",
    )(lengths, x.reshape(shp), cot.reshape(shp), w, v)


def body(z_count, dp_count, inputs, matrices, vectors, lengths, cotangent):
    d = inputs.shape[1]
    devices = z_count * dp_count
    ff = (matrices.shape[1] * devices - 4 * d) // 2
    own = dp_count == 8
    split = ("dp", "sub")
    if own:
        w, v = matrices, vectors
    else:
        w = lax.all_gather(matrices, split, axis=1, tiled=True)
        v = lax.all_gather(vectors, split, axis=1, tiled=True).astype(F32)[:, None, :]
    out, gin, gw, gv = compute(inputs, cotangent, w, v, lengths, (d, ff), own, z_count)
    if not own:
        gw = lax.psum_scatter(gw, split, scatter_dimension=1, tiled=True)
        gv = lax.psum_scatter(gv[:, 0], split, scatter_dimension=1, tiled=True)
    return (out.reshape(inputs.shape), gin.reshape(inputs.shape), gw, gv)


def solution(mesh):
    split = ("dp", "sub")
    return jax.shard_map(
        partial(body, mesh.shape["sub"], mesh.shape["dp"]),
        mesh=mesh,
        in_specs=(P(split, None), P(None, split, None), P(None, split), P(split), P(split, None)),
        out_specs=(P(split, None), P(split, None), P(None, split, None), P(None, split)),
        check_vma=False,
    )
```

```python
from functools import partial

import jax
import jax.numpy as jnp
from jax import lax
from jax.experimental import pallas as pl
from jax.experimental.pallas import tpu as pltpu
from jax.sharding import PartitionSpec as P

HEADS = 2
COLS = 96
ROWS = 12
SUBL = 8
BLOCK = 96
NBLK = 12
S = COLS * ROWS
LOG2E = 1.4426950408889634
BF = jnp.bfloat16
F32 = jnp.float32
STATIC = False
SIZE = (288, 576, 576, 576)


def mm(a, b, ca, cb):
    return lax.dot_general(a, b, (((ca,), (cb,)), ((), ())), preferred_element_type=F32)


def standardize(v):
    c = v - jnp.mean(v, -1, keepdims=True)
    r = lax.rsqrt(jnp.mean(c * c, -1, keepdims=True) + 1e-05)
    return c * r, r


def rowsum8(v):
    return jnp.sum(v.reshape(v.shape[0] // 8, 8, v.shape[1]), axis=0)


def live_mask(length, slab, width):
    row = lax.broadcasted_iota(jnp.int32, (ROWS, SUBL, width), 0)
    col = lax.broadcasted_iota(jnp.int32, (ROWS, SUBL, width), 1)
    return row * COLS + col + slab * SUBL < length


def kernel(dims, own, z_count, *refs):
    d, ff = dims
    len_ref, x_ref, cot_ref, w_ref, v_ref, out_ref, gin_ref, gw_ref, gvo_ref = refs[:9]
    (
        vs_s, gwt_ref, gv_ref, n1_s, pk_s, pt_s, mix_s, mid_s, n2_s, act_s, dact_s,
        x1_s, gy0_s, gy_s, gup_s, gmid_s, gmidl_s, gmix_s, gpk_s,
    ) = refs[9:28]
    img = pl.program_id(0)
    last = img == pl.num_programs(0) - 1
    length = len_ref[img]
    hw = d // HEADS
    qs = hw ** -0.5
    if own:
        move = Moves(z_count, w_ref, v_ref, gwt_ref, gv_ref, vs_s, gw_ref, gvo_ref, refs[28:])
        wpart = move.weights
    else:

        def wpart(l, a, b):
            return w_ref[l, a:b, :]

    @pl.when(img == 0)
    def _():
        gwt_ref[...] = jnp.zeros_like(gwt_ref)
        gv_ref[...] = jnp.zeros_like(gv_ref)
        if own:
            move.gather_first()
        else:
            vs_s[:, 0:1, :] = v_ref[...]

    def wqkv(l):
        return wpart(l, 0, 3 * d)

    def wout(l):
        return wpart(l, 3 * d, 4 * d)

    def vec(l, i, n=1):
        return vs_s[l, 0:1, i * d : (i + n) * d]

    tril_b = lax.broadcasted_iota(jnp.int32, (BLOCK, BLOCK), 0)
    tril_a = lax.broadcasted_iota(jnp.int32, (BLOCK, BLOCK), 1)
    masks = (
        tril_b <= tril_a,
        (tril_b <= tril_a) & ((tril_b & (SUBL - 1)) == (tril_a & (SUBL - 1))),
    )

    def load_x(l, c, nb):
        if l == 0:
            return x_ref[0, pl.ds(c * nb, nb)].reshape(nb * BLOCK, d)
        return x1_s[pl.ds(c * nb, nb)].reshape(nb * BLOCK, d)

    def store_perm(ref, c, nb, val, lead=()):
        v4 = val.reshape(nb, NBLK, SUBL, d)
        for b in range(nb):
            ref[lead + (slice(None), c * nb + b)] = v4[b]

    def rows(c, nb):
        if isinstance(c, int):
            return pl.ds(c * nb * BLOCK, nb * BLOCK)
        return pl.ds(pl.multiple_of(c * nb * BLOCK, BLOCK), nb * BLOCK)

    def loop(n, step):
        if STATIC or n == 1:
            for c in range(n):
                step(c, 0)
        else:
            lax.fori_loop(0, n, step, 0)

    def qkv_fwd(l, nb):
        def step(c, _):
            s = rows(c, nb)
            xh, _r = standardize(load_x(l, c, nb))
            n1 = (xh * vec(l, 0) + vec(l, 1)).astype(BF)
            n1_s[l, s, :] = n1
            pk_s[l, s, :] = mm(n1, wqkv(l), 1, 1).astype(BF)
            return 0

        loop(NBLK // nb, step)

    def heads_of(packed):
        return [
            tuple(packed[:, i * d + h * hw : i * d + (h + 1) * hw] for i in range(3))
            for h in range(HEADS)
        ]

    def attn_fwd(l, nb):
        mask = masks[l]

        def step(c, _):
            each = [(b, h) for b in range(nb) for h in range(HEADS)]
            qkv = []
            for b in range(nb):
                qkv += heads_of(pk_s[l, rows(c * nb + b, 1), :])
            scores = [mm(k, q, 1, 1) for q, k, v in qkv]
            ps = []
            for st in scores:
                st = jnp.where(mask, st, -1e30)
                p = jnp.exp2((st - jnp.max(st, 0, keepdims=True)) * (qs * LOG2E))
                ps.append((p * (1.0 / jnp.sum(p, 0, keepdims=True))).astype(BF))
            mixed = [mm(p, v, 0, 0).astype(BF) for p, (q, k, v) in zip(ps, qkv)]
            for (b, h), p, m in zip(each, ps, mixed):
                pt_s[l, c * nb + b, h, :, 0:BLOCK] = p
                mix_s[l, rows(c * nb + b, 1), h * hw : (h + 1) * hw] = m
            return 0

        loop(NBLK // nb, step)

    def wup(l, f):
        return wpart(l, (4 + f) * d, (5 + f) * d)

    def wdown(l, f):
        return wpart(l, 4 * d + ff + f * d, 4 * d + ff + (f + 1) * d)

    def cols(f):
        return slice(f * d, (f + 1) * d)

    def mid_stage(l):
        mid = load_x(l, 0, NBLK) + mm(mix_s[l], wout(l), 1, 1) + vec(l, 2)
        mid_s[l] = mid
        xh, _r = standardize(mid)
        n2_s[l] = (xh * vec(l, 3) + vec(l, 4)).astype(BF)

    def gelu_parts(h):
        t = lax.erf(h * (2 ** -0.5)) + 1.0
        act = ((0.5 * h) * t).astype(BF)
        hb = h.astype(BF)
        e = jnp.exp2(hb * hb * BF(-0.5 * LOG2E))
        return act, t.astype(BF) + hb * e * BF(2 * 0.3989422804014327)

    def chunks(size):
        return [slice(r, r + size) for r in range(0, S, size)]

    def ffn_fwd0():
        l = 0
        h = mm(n2_s[l], wup(l, 0), 1, 1)
        for f in range(ff // d):
            ahead = mm(n2_s[l], wup(l, f + 1), 1, 1) if f + 1 < ff // d else None
            act, dact = gelu_parts(h + vec(l, 6 + f))
            act_s[l, :, cols(f)] = act
            dact_s[:, cols(f)] = dact
            h = ahead
        y = mid_s[l] + vec(l, 5) + mm(act_s[l], wpart(l, 4 * d + ff, 4 * d + 2 * ff), 1, 0)
        store_perm(x1_s, 0, NBLK, y)

    def load_gy1():
        for b in range(NBLK):
            live = live_mask(length, b, d)
            part = jnp.where(live, cot_ref[0, :, b], 0.0).reshape(BLOCK, d)
            acc_vec(1, 5, part)
            gy_s[b * BLOCK : (b + 1) * BLOCK] = (0.5 * part).astype(BF)

    def ffn_both1(size):
        l, n = 1, ff // d

        def products(f, s):
            return mm(n2_s[l, s], wup(l, f), 1, 1), mm(gy_s[s], wdown(l, f), 1, 1)

        ahead = {s.start: products(0, s) for s in chunks(size)}
        for f in range(n + 1):
            for i, s in enumerate(chunks(size)):
                if f < n:
                    h, ga = ahead[s.start]
                    if f + 1 < n:
                        ahead[s.start] = products(f + 1, s)
                    act, dact = gelu_parts(h + vec(l, 6 + f))
                    act_s[l, s, cols(f)] = act
                    gup = ga * dact.astype(F32)
                    acc_vec(l, 6 + f, gup)
                    gup_s[s, cols(f)] = gup.astype(BF)
                if f > 0 and i == 0:
                    wgrad(l, 4 * d + ff + (f - 1) * d, gy_s[...], act_s[l, :, cols(f - 1)])
                if f > 0 and i == min(1, S // size - 1):
                    wgrad(l, 4 * d + (f - 1) * d, n2_s[l], gup_s[:, cols(f - 1)])

    def ffn_end1():
        l = 1
        y = mid_s[l] + vec(l, 5) + mm(act_s[l], wpart(l, 4 * d + ff, 4 * d + 2 * ff), 1, 0)
        y4 = y.reshape(NBLK, NBLK, SUBL, d)
        for b in range(NBLK):
            out_ref[0, :, b] = jnp.where(live_mask(length, b, d), y4[b], 0.0)

    def ffn_bwd0(size):
        l, n = 0, ff // d
        for s in chunks(size):
            gy = gy0_s[s.start // BLOCK : s.stop // BLOCK].reshape(size, d)
            acc_vec(l, 5, gy)
            gy_s[s] = (0.5 * gy).astype(BF)
        ahead = {s.start: mm(gy_s[s], wdown(l, 0), 1, 1) for s in chunks(size)}
        for f in range(n + 1):
            for i, s in enumerate(chunks(size)):
                if f < n:
                    ga = ahead[s.start]
                    if f + 1 < n:
                        ahead[s.start] = mm(gy_s[s], wdown(l, f + 1), 1, 1)
                    gup = ga * dact_s[s, cols(f)].astype(F32)
                    acc_vec(l, 6 + f, gup)
                    gup_s[s, cols(f)] = gup.astype(BF)
                if f > 0 and i == 0:
                    wgrad(l, 4 * d + ff + (f - 1) * d, gy_s[...], act_s[l, :, cols(f - 1)])
                if f > 0 and i == min(1, S // size - 1):
                    wgrad(l, 4 * d + (f - 1) * d, n2_s[l], gup_s[:, cols(f - 1)])

    def mid_bwd(l, size):
        for s in chunks(size):
            gn2 = mm(gup_s[s], wpart(l, 4 * d, 4 * d + ff), 1, 0)
            if l == 0:
                gy = gy0_s[s.start // BLOCK : s.stop // BLOCK].reshape(size, d)
            else:
                parts = []
                for b in range(s.start // BLOCK, s.stop // BLOCK):
                    live = live_mask(length, b, d)
                    parts.append(jnp.where(live, cot_ref[0, :, b], 0.0).reshape(BLOCK, d))
                gy = jnp.concatenate(parts, 0)
            gmid = gy + norm_back(l, 3, mid_s[l, s], gn2)
            gmid_s[s] = gmid
            acc_vec(l, 2, gmid)
            gml = gmid.astype(BF)
            gmidl_s[s] = gml
            gmix_s[s] = mm(gml, wout(l), 1, 0).astype(BF)

    def acc_vec(l, i, val, n=1):
        gv_ref[l, :, i * d : (i + n) * d] += rowsum8(val)

    def norm_back(l, gi, v, gn):
        xh, r = standardize(v)
        acc_vec(l, gi, gn * xh)
        acc_vec(l, gi + 1, gn)
        e = gn * vec(l, gi)
        me = jnp.mean(e, -1, keepdims=True)
        mx = jnp.mean(e * xh, -1, keepdims=True)
        return r * (e - me - xh * mx)

    def attn_bwd(l, nb):
        def step(c, _):
            each = [(b, h) for b in range(nb) for h in range(HEADS)]
            qkv, gms = [], []
            for b in range(nb):
                at = rows(c * nb + b, 1)
                qkv += heads_of(pk_s[l, at, :])
                gm = gmix_s[at, :]
                gms += [gm[:, h * hw : (h + 1) * hw] for h in range(HEADS)]
            pts = [pt_s[l, c * nb + b, h, :, 0:BLOCK] for b, h in each]
            gps = [mm(v, gm, 1, 1) for (q, k, v), gm in zip(qkv, gms)]
            gss = []
            for pt, gp in zip(pts, gps):
                pf = pt.astype(F32)
                pg = pf * gp
                gss.append(((pg - pf * jnp.sum(pg, 0, keepdims=True)) * qs).astype(BF))
            gv = [mm(pt, gm, 1, 0).astype(BF) for pt, gm in zip(pts, gms)]
            gk = [mm(gs, q, 1, 0).astype(BF) for gs, (q, k, v) in zip(gss, qkv)]
            gq = [mm(gs, k, 0, 0).astype(BF) for gs, (q, k, v) in zip(gss, qkv)]
            for n, (b, h) in enumerate(each):
                for i, g in enumerate((gq, gk, gv)):
                    gpk_s[rows(c * nb + b, 1), i * d + h * hw : i * d + (h + 1) * hw] = g[n]
            return 0

        loop(NBLK // nb, step)

    def qkv_bwd(l, nb):
        def step(c, _):
            s = rows(c, nb)
            gn1 = mm(gpk_s[s, :], wqkv(l), 1, 0)
            gx = gmid_s[s, :] + norm_back(l, 0, load_x(l, c, nb), gn1)
            if l == 0:
                gin_ref[0, pl.ds(c * nb, nb)] = gx.reshape(nb, NBLK, SUBL, d)
            else:
                store_perm(gy0_s, c, nb, gx)
            return 0

        loop(NBLK // nb, step)

    def wgrad(l, at, a, b):
        gwt_ref[l, :, at : at + b.shape[1]] += mm(a, b, 0, 0)

    def wgrads(l):
        wgrad(l, 0, n1_s[l], gpk_s[...])
        wgrad(l, 3 * d, mix_s[l], gmidl_s[...])

    def region(step):
        pl.when(img >= 0)(step)

    def between(first, step):
        if own:
            pl.when(img == 0 if first else last)(step)

    region(lambda: qkv_fwd(0, NBLK))
    between(True, lambda: move.gather_across(1))
    region(lambda: attn_fwd(0, NBLK))
    between(True, lambda: move.gather_diagonal(1))
    region(lambda: mid_stage(0))
    region(ffn_fwd0)
    between(True, lambda: move.gather_end(1))
    region(lambda: qkv_fwd(1, NBLK))
    region(lambda: attn_fwd(1, NBLK))
    region(lambda: mid_stage(1))
    region(load_gy1)
    region(lambda: ffn_both1(SIZE[0]))
    region(ffn_end1)
    region(lambda: mid_bwd(1, SIZE[1]))
    region(lambda: attn_bwd(1, NBLK))
    region(lambda: qkv_bwd(1, NBLK))
    region(lambda: wgrads(1))
    between(False, lambda: move.sum_start(1))
    region(lambda: ffn_bwd0(SIZE[2]))
    between(False, lambda: move.sum_chip(1))
    region(lambda: mid_bwd(0, SIZE[3]))
    between(False, lambda: move.sum_across(1))
    region(lambda: attn_bwd(0, NBLK))
    between(False, lambda: move.sum_column(1))
    region(lambda: qkv_bwd(0, NBLK))
    region(lambda: wgrads(0))
    between(False, lambda: move.sum_start(0))

    @pl.when(last)
    def _():
        if own:
            move.sum_chip(0)
            move.sum_end(1)
            move.sum_across(0)
            move.sum_column(0)
            move.sum_end(0)
            move.drain()
        else:
            for l in range(2):
                gw_ref[l] = whole_grad(gwt_ref, l, 4 * d + ff)
                gvo_ref[l] = jnp.sum(gv_ref[l], 0, keepdims=True)


def whole_grad(gwt_ref, l, cut):
    return jnp.concatenate([gwt_ref[l, :, :cut], 2.0 * gwt_ref[l, :, cut:]], 1).T


MESH = pl.DeviceIdType.MESH


def column(y, x, core):
    return (y * 2 + x) * 2 + core


class Moves:
    def __init__(self, z_count, w_ref, v_ref, gwt_ref, gv_ref, vs_s, gw_ref, gvo_ref, refs):
        self.z_count = z_count
        self.w_ref, self.v_ref, self.gwt_ref, self.gv_ref = w_ref, v_ref, gwt_ref, gv_ref
        self.vs_s, self.gw_ref, self.gvo_ref = vs_s, gw_ref, gvo_ref
        (
            self.full_s, self.gb_s, self.sib_s, self.own_s, self.diag_top_s, self.diag_low_s,
            self.cols_s, self.zr_s,
            self.ag_link, self.ag_core, self.ag_z, self.ag_x, self.ag_y, self.ag_c,
            self.rs_core_send, self.rs_core_recv, self.rs_send, self.rs_recv,
            self.rs_z_send, self.rs_z_recv,
        ) = refs
        self.rows, self.d = w_ref.shape[1], w_ref.shape[2]
        self.block = self.full_s.shape[2]
        self.half = self.diag_top_s.shape[2]
        self.devices = self.full_s.shape[1]
        self.vrow = v_ref.shape[1]
        self.vlen = self.vrow * self.devices
        dp, z = lax.axis_index("dp"), lax.axis_index("sub")
        self.dp, self.z = dp, z
        self.core = dp % 2
        self.x = dp // 2 % 2
        self.y = dp // 4
        y, x = self.y, self.x
        self.chips = ((y, x), (y, 1 - x), (1 - y, x), (1 - y, 1 - x))
        self.dp_x = column(y, 1 - x, self.core)
        self.dp_y = column(1 - y, x, self.core)
        self.dp_c = column(y, x, 1 - self.core)
        self.cut = (pl.ds(0, self.half), pl.ds(self.half, self.block - self.half))
        near = [0]
        for k in range(1, z_count // 2 + 1):
            near.append(k)
            if z_count - k != k:
                near.append(z_count - k)
        self.near = near

    def zz(self, k):
        return lax.rem(self.z + k, self.z_count)

    def index(self, kind, t, core=None):
        yy, xx = self.chips[kind]
        return column(yy, xx, self.core if core is None else core) * self.z_count + t

    def slot(self, kind, t):
        yy, xx = self.chips[kind]
        return (yy * 2 + xx) * self.z_count + t

    def weights(self, l, a, b):
        parts, rows = [], self.rows
        while a < b:
            i = a // rows
            e = min(b, (i + 1) * rows)
            parts.append(self.full_s[l, i, a - i * rows : e - i * rows, :])
            a = e
        return jnp.concatenate(parts, 0)

    def remote(self, src, dst, send, recv, target):
        return pltpu.make_async_remote_copy(
            src_ref=src, dst_ref=dst, send_sem=send, recv_sem=recv,
            device_id=target, device_id_type=MESH,
        )

    def ag_copy(self, l, kind, t, way, part=None):
        i, s = self.index(kind, t), self.slot(kind, t)
        ref = self.full_s.at[l, i] if part is None else self.full_s.at[l, i, self.cut[part], :]
        if way == "c":
            return self.remote(
                ref, ref, self.ag_c.at[l, s], self.ag_core.at[l, s], (self.dp_c, self.z)
            )
        send = self.ag_x if way == "x" else self.ag_y
        target = (self.dp_x if way == "x" else self.dp_y, self.z)
        return self.remote(ref, ref, send.at[l, s], self.ag_link.at[l, 1 if part else 0, s], target)

    def ag_along(self, l, k):
        ref = self.full_s.at[l, self.index(0, self.z)]
        s = self.slot(0, self.z)
        return self.remote(
            ref, ref, self.ag_z.at[l, k], self.ag_link.at[l, 0, s], (self.dp, self.zz(k))
        )

    def ag_wait(self, l, kind, t, part=None):
        i, s = self.index(kind, t), self.slot(kind, t)
        ref = self.full_s.at[l, i] if part is None else self.full_s.at[l, i, self.cut[part], :]
        self.remote(
            ref, ref, self.ag_c.at[l, s], self.ag_link.at[l, 1 if part else 0, s],
            (self.dp_c, self.z),
        ).wait_recv()

    def gather_along(self, l):
        for k in self.near[1:]:
            self.ag_along(l, k).start()

    def gather_spread(self, l):
        for k in self.near:
            t = self.zz(k)
            if k:
                self.ag_wait(l, 0, t)
            for way in "xyc":
                self.ag_copy(l, 0, t, way).start()

    def gather_across(self, l):
        for k in self.near:
            t = self.zz(k)
            self.ag_wait(l, 1, t)
            self.ag_copy(l, 1, t, "y", 0).start()
            self.ag_copy(l, 1, t, "c").start()
            self.ag_wait(l, 2, t)
            self.ag_copy(l, 2, t, "x", 1).start()
            self.ag_copy(l, 2, t, "c").start()

    def gather_diagonal(self, l):
        for k in self.near:
            t = self.zz(k)
            self.ag_wait(l, 3, t, 0)
            self.ag_wait(l, 3, t, 1)
            self.ag_copy(l, 3, t, "c").start()

    def gather_end(self, l):
        for kind in range(4):
            for t in range(self.z_count):
                i, s = self.index(kind, t, 1 - self.core), self.slot(kind, t)
                ref = self.full_s.at[l, i]
                self.remote(
                    ref, ref, self.ag_c.at[l, s], self.ag_core.at[l, s], (self.dp_c, self.z)
                ).wait_recv()
        vrow, vlen, rows = self.vrow, self.vlen, self.rows
        self.vs_s[l] = jnp.zeros((8, vlen), F32)
        for i in range(self.devices):
            part = self.full_s[l, i, rows : self.block, 0:128].astype(F32)[0:8]
            at = i * vrow // 128 * 128
            wide = jnp.concatenate([part, jnp.zeros_like(part)], 1)
            if i * vrow > at:
                wide = pltpu.roll(wide, i * vrow - at, 1)
            n = min(256, vlen - at)
            self.vs_s[l, 0:1, at : at + n] += wide[0:1, 0:n]

    def gather_first(self):
        barrier = pltpu.get_barrier_semaphore()
        partners = [(p, self.z) for p in (self.dp_x, self.dp_y, self.dp_c)]
        partners += [(self.dp, self.zz(k)) for k in self.near[1:]]
        for p in partners:
            pl.semaphore_signal(barrier, inc=1, device_id=p, device_id_type=MESH)
        me, rows = self.index(0, self.z), self.rows
        for l in range(2):
            self.full_s[l, me, 0:rows] = self.w_ref[l]
            tail = jnp.zeros((self.block - rows, self.d - self.vrow), BF)
            v = self.v_ref[l : l + 1, :].astype(F32)
            v = jnp.concatenate([v, jnp.zeros((self.block - rows - 1, self.vrow), F32)], 0)
            self.full_s[l, me, rows : self.block, :] = jnp.concatenate([v.astype(BF), tail], 1)
        pl.semaphore_wait(barrier, len(partners))
        self.gather_along(0)
        self.gather_spread(0)
        self.gather_along(1)
        self.gather_across(0)
        self.gather_spread(1)
        self.gather_diagonal(0)
        self.gather_end(0)

    def rs_core(self, l, kind):
        i = self.index(kind, 0, 1 - self.core)
        return self.remote(
            self.gb_s.at[l, pl.ds(i, self.z_count)], self.sib_s.at[l, kind],
            self.rs_core_send.at[l, kind], self.rs_core_recv.at[l, kind], (self.dp_c, self.z),
        )

    def rs_across(self, l, slot, t):
        kind, half, target, dst = (
            (3, 0, self.dp_y, self.diag_top_s.at[l, t]),
            (3, 1, self.dp_x, self.diag_low_s.at[l, t]),
            (2, 0, self.dp_y, self.cols_s.at[l, 0, t, self.cut[0], :]),
            (1, 1, self.dp_x, self.cols_s.at[l, 0, t, self.cut[1], :]),
            (1, 0, self.dp_x, self.cols_s.at[l, 1, t, self.cut[0], :]),
            (2, 1, self.dp_y, self.cols_s.at[l, 1, t, self.cut[1], :]),
        )[slot]
        return self.remote(
            self.gb_s.at[l, self.index(kind, t), self.cut[half], :], dst,
            self.rs_send.at[l, slot, t], self.rs_recv.at[l, slot, t], (target, self.z),
        )

    def rs_along(self, l, k):
        return self.remote(
            self.gb_s.at[l, self.index(0, self.zz(k))], self.zr_s.at[l, k - 1],
            self.rs_z_send.at[l, k], self.rs_z_recv.at[l, k], (self.dp, self.zz(k)),
        )

    def sum_start(self, l):
        rows, vrow, vlen = self.rows, self.vrow, self.vlen
        g = whole_grad(self.gwt_ref, l, (rows * self.devices) // 2 + 2 * self.d).astype(BF)
        gv = jnp.sum(self.gv_ref[l], 0, keepdims=True)
        gv = jnp.concatenate([gv, jnp.zeros((7, vlen), F32)], 0)
        for i in range(self.devices):
            self.gb_s[l, i, 0:rows] = g[i * rows : (i + 1) * rows]
            at = i * vrow // 128 * 128
            n = min(256, vlen - at)
            wide = gv[:, at : at + n]
            if n < 256:
                wide = jnp.concatenate([wide, jnp.zeros_like(wide)], 1)
            if i * vrow > at:
                wide = pltpu.roll(wide, 256 - (i * vrow - at), 1)
            wide = jnp.concatenate([wide, jnp.zeros_like(wide)], 0)
            self.gb_s[l, i, rows : self.block] = wide.astype(BF)
        for kind in (3, 1, 2, 0):
            self.rs_core(l, kind).start()

    def sum_chip(self, l):
        for kind, slots in ((3, (0, 1)), (1, (3,)), (2, (2,)), (0, ())):
            self.rs_core(l, kind).wait_recv()
            for t in range(self.z_count):
                i = self.index(kind, t)
                both = self.gb_s[l, i].astype(F32) + self.sib_s[l, kind, t].astype(F32)
                if kind == 0:
                    self.own_s[l, t] = both
                else:
                    self.gb_s[l, i] = both.astype(BF)
                for slot in slots:
                    self.rs_across(l, slot, t).start()

    def sum_across(self, l):
        for t in range(self.z_count):
            for slot, kind, half, ref in (
                (0, 1, 0, self.diag_top_s), (1, 2, 1, self.diag_low_s),
            ):
                self.rs_across(l, slot, t).wait_recv()
                i, cut = self.index(kind, t), self.cut[half]
                both = self.gb_s[l, i, cut].astype(F32) + ref[l, t].astype(F32)
                self.gb_s[l, i, cut] = both.astype(BF)
                self.rs_across(l, 4 if half == 0 else 5, t).start()

    def sum_column(self, l):
        for k in self.near[1:] + [0]:
            t = self.zz(k)
            for slot in (2, 3, 4, 5):
                self.rs_across(l, slot, t).wait_recv()
            total = self.own_s[l, t]
            for a in range(2):
                total = total + self.cols_s[l, a, t].astype(F32)
            if k:
                self.gb_s[l, self.index(0, t)] = total.astype(BF)
                self.rs_along(l, k).start()
            else:
                self.own_s[l, t] = total

    def sum_end(self, l):
        for k in self.near[1:]:
            self.rs_along(l, k).wait_recv()
        total = self.own_s[l, self.z]
        for k in self.near[1:]:
            total = total + self.zr_s[l, k - 1].astype(F32)
        self.gw_ref[l] = total[0 : self.rows]
        self.gvo_ref[l : l + 1, :] = total[self.rows : self.rows + 1, 0 : self.vrow]

    def drain(self):
        for l in range(2):
            for k in self.near[1:]:
                self.ag_along(l, k).wait_send()
                self.rs_along(l, k).wait_send()
            for t in range(self.z_count):
                for kind in range(4):
                    self.ag_copy(l, kind, t, "c").wait_send()
                self.ag_copy(l, 0, t, "x").wait_send()
                self.ag_copy(l, 0, t, "y").wait_send()
                self.ag_copy(l, 1, t, "y", 0).wait_send()
                self.ag_copy(l, 2, t, "x", 1).wait_send()
                for slot in range(6):
                    self.rs_across(l, slot, t).wait_send()
            for kind in range(4):
                self.rs_core(l, kind).wait_send()


def compute(x, cot, w, v, lengths, dims, own, z_count):
    d, ff = dims
    n = lengths.shape[0]
    mrows, vlen = 4 * d + 2 * ff, 6 * d + ff
    img = pl.BlockSpec((1, ROWS, NBLK, SUBL, d), lambda i: (i, 0, 0, 0, 0))
    shp = (n, ROWS, NBLK, SUBL, d)

    def whole(shape):
        zero = (0,) * len(shape)
        return pl.BlockSpec(shape, lambda i: zero, pipeline_mode=pl.Buffered(1))

    scratch = [
        pltpu.VMEM((2, 8, vlen), F32),
        pltpu.VMEM((2, d, mrows), F32),
        pltpu.VMEM((2, 8, vlen), F32),
        pltpu.VMEM((2, S, d), BF),
        pltpu.VMEM((2, S, 3 * d), BF),
        pltpu.VMEM((2, NBLK, HEADS, BLOCK, 128), BF),
        pltpu.VMEM((2, S, d), BF),
        pltpu.VMEM((2, S, d), F32),
        pltpu.VMEM((2, S, d), BF),
        pltpu.VMEM((2, S, ff), BF),
        pltpu.VMEM((S, ff), BF),
        pltpu.VMEM((NBLK, ROWS, SUBL, d), F32),
        pltpu.VMEM((ROWS, NBLK, SUBL, d), F32),
        pltpu.VMEM((S, d), BF),
        pltpu.VMEM((S, ff), BF),
        pltpu.VMEM((S, d), F32),
        pltpu.VMEM((S, d), BF),
        pltpu.VMEM((S, d), BF),
        pltpu.VMEM((S, 3 * d), BF),
    ]
    if own:
        rows, vrow = w.shape[1], v.shape[1]
        devices = mrows // rows
        block = rows + 16
        half = (block // 2 + 15) // 16 * 16
        zc = z_count
        dma = pltpu.SemaphoreType.DMA
        scratch += [
            pltpu.VMEM((2, devices, block, d), BF),
            pltpu.VMEM((2, devices, block, d), BF),
            pltpu.VMEM((2, 4, zc, block, d), BF),
            pltpu.VMEM((2, zc, block, d), F32),
            pltpu.VMEM((2, zc, half, d), BF),
            pltpu.VMEM((2, zc, block - half, d), BF),
            pltpu.VMEM((2, 2, zc, block, d), BF),
            pltpu.VMEM((2, zc - 1, block, d), BF),
            dma((2, 2, 4 * zc)), dma((2, 4 * zc)), dma((2, zc)),
            dma((2, 4 * zc)), dma((2, 4 * zc)), dma((2, 4 * zc)),
            dma((2, 4)), dma((2, 4)), dma((2, 6, zc)), dma((2, 6, zc)),
            dma((2, zc)), dma((2, zc)),
        ]
        gw_shape, gv_shape = (2, rows, d), (2, vrow)
    else:
        gw_shape, gv_shape = (2, mrows, d), (2, 1, vlen)
    return pl.pallas_call(
        partial(kernel, dims, own, z_count),
        grid=(n,),
        in_specs=[pl.BlockSpec(memory_space=pltpu.SMEM), img, img, whole(w.shape), whole(v.shape)],
        out_specs=[img, img, whole(gw_shape), whole(gv_shape)],
        out_shape=[
            jax.ShapeDtypeStruct(shp, F32),
            jax.ShapeDtypeStruct(shp, F32),
            jax.ShapeDtypeStruct(gw_shape, F32),
            jax.ShapeDtypeStruct(gv_shape, F32),
        ],
        scratch_shapes=scratch,
        compiler_params=pltpu.CompilerParams(
            dimension_semantics=("arbitrary",),
            vmem_limit_bytes=63 << 20,
            collective_id=0 if own else None,
            has_side_effects=own,
        ),
        name="layers",
    )(lengths, x.reshape(shp), cot.reshape(shp), w, v)


def body(z_count, dp_count, inputs, matrices, vectors, lengths, cotangent):
    d = inputs.shape[1]
    devices = z_count * dp_count
    ff = (matrices.shape[1] * devices - 4 * d) // 2
    own = dp_count == 8
    split = ("dp", "sub")
    if own:
        w, v = matrices, vectors
    else:
        w = lax.all_gather(matrices, split, axis=1, tiled=True)
        v = lax.all_gather(vectors, split, axis=1, tiled=True).astype(F32)[:, None, :]
    out, gin, gw, gv = compute(inputs, cotangent, w, v, lengths, (d, ff), own, z_count)
    if not own:
        gw = lax.psum_scatter(gw, split, scatter_dimension=1, tiled=True)
        gv = lax.psum_scatter(gv[:, 0], split, scatter_dimension=1, tiled=True)
    return (out.reshape(inputs.shape), gin.reshape(inputs.shape), gw, gv)


def solution(mesh):
    split = ("dp", "sub")
    return jax.shard_map(
        partial(body, mesh.shape["sub"], mesh.shape["dp"]),
        mesh=mesh,
        in_specs=(P(split, None), P(None, split, None), P(None, split), P(split), P(split, None)),
        out_specs=(P(split, None), P(split, None), P(None, split, None), P(None, split)),
        check_vma=False,
    )
```

```python
from functools import partial

import jax
import jax.numpy as jnp
from jax import lax
from jax.experimental import pallas as pl
from jax.experimental.pallas import tpu as pltpu
from jax.sharding import PartitionSpec as P

HEADS = 2
COLS = 96
ROWS = 12
SUBL = 8
BLOCK = 96
NBLK = 12
S = COLS * ROWS
LOG2E = 1.4426950408889634
BF = jnp.bfloat16
F32 = jnp.float32
STATIC = False
SIZE = (288, 576, 576, 576, 576)


def mm(a, b, ca, cb):
    return lax.dot_general(a, b, (((ca,), (cb,)), ((), ())), preferred_element_type=F32)


def standardize(v):
    c = v - jnp.mean(v, -1, keepdims=True)
    r = lax.rsqrt(jnp.mean(c * c, -1, keepdims=True) + 1e-05)
    return c * r, r


def rowsum8(v):
    return jnp.sum(v.reshape(v.shape[0] // 8, 8, v.shape[1]), axis=0)


def live_mask(length, slab, width):
    row = lax.broadcasted_iota(jnp.int32, (ROWS, SUBL, width), 0)
    col = lax.broadcasted_iota(jnp.int32, (ROWS, SUBL, width), 1)
    return row * COLS + col + slab * SUBL < length


def kernel(dims, own, z_count, *refs):
    d, ff = dims
    len_ref, x_ref, cot_ref, w_ref, v_ref, out_ref, gin_ref, gw_ref, gvo_ref = refs[:9]
    (
        vs_s, gwt_ref, gv_ref, n1_s, pk_s, pt_s, mix_s, mid_s, n2_s, act_s, dact_s,
        x1_s, gy0_s, gy_s, gup_s, gmid_s, gmidl_s, gmix_s, gpk_s,
    ) = refs[9:28]
    img = pl.program_id(0)
    last = img == pl.num_programs(0) - 1
    length = len_ref[img]
    hw = d // HEADS
    qs = hw ** -0.5
    if own:
        move = Moves(z_count, w_ref, v_ref, gwt_ref, gv_ref, vs_s, gw_ref, gvo_ref, refs[28:])
        wpart = move.weights
    else:

        def wpart(l, a, b):
            return w_ref[l, a:b, :]

    @pl.when(img == 0)
    def _():
        def clear():
            gwt_ref[...] = jnp.zeros_like(gwt_ref)
            gv_ref[...] = jnp.zeros_like(gv_ref)

        if own:
            move.gather_first(clear)
        else:
            clear()
            vs_s[:, 0:1, :] = v_ref[...]

    def wqkv(l):
        return wpart(l, 0, 3 * d)

    def wout(l):
        return wpart(l, 3 * d, 4 * d)

    def vec(l, i, n=1):
        return vs_s[l, 0:1, i * d : (i + n) * d]

    tril_b = lax.broadcasted_iota(jnp.int32, (BLOCK, BLOCK), 0)
    tril_a = lax.broadcasted_iota(jnp.int32, (BLOCK, BLOCK), 1)
    masks = (
        tril_b <= tril_a,
        (tril_b <= tril_a) & ((tril_b & (SUBL - 1)) == (tril_a & (SUBL - 1))),
    )

    def load_x(l, c, nb):
        if l == 0:
            return x_ref[0, pl.ds(c * nb, nb)].reshape(nb * BLOCK, d)
        return x1_s[pl.ds(c * nb, nb)].reshape(nb * BLOCK, d)

    def store_perm(ref, c, nb, val, lead=()):
        v4 = val.reshape(nb, NBLK, SUBL, d)
        for b in range(nb):
            ref[lead + (slice(None), c * nb + b)] = v4[b]

    def rows(c, nb):
        if isinstance(c, int):
            return pl.ds(c * nb * BLOCK, nb * BLOCK)
        return pl.ds(pl.multiple_of(c * nb * BLOCK, BLOCK), nb * BLOCK)

    def loop(n, step):
        if STATIC or n == 1:
            for c in range(n):
                step(c, 0)
        else:
            lax.fori_loop(0, n, step, 0)

    def qkv_fwd(l, nb):
        def step(c, _):
            s = rows(c, nb)
            xh, _r = standardize(load_x(l, c, nb))
            n1 = (xh * vec(l, 0) + vec(l, 1)).astype(BF)
            n1_s[l, s, :] = n1
            pk_s[l, s, :] = mm(n1, wqkv(l), 1, 1).astype(BF)
            return 0

        loop(NBLK // nb, step)

    def heads_of(packed):
        return [
            tuple(packed[:, i * d + h * hw : i * d + (h + 1) * hw] for i in range(3))
            for h in range(HEADS)
        ]

    def attn_fwd(l, nb):
        mask = masks[l]

        def step(c, _):
            each = [(b, h) for b in range(nb) for h in range(HEADS)]
            qkv = []
            for b in range(nb):
                qkv += heads_of(pk_s[l, rows(c * nb + b, 1), :])
            scores = [mm(k, q, 1, 1) for q, k, v in qkv]
            ps = []
            for st in scores:
                st = jnp.where(mask, st, -1e30)
                p = jnp.exp2((st - jnp.max(st, 0, keepdims=True)) * (qs * LOG2E))
                ps.append((p * (1.0 / jnp.sum(p, 0, keepdims=True))).astype(BF))
            mixed = [mm(p, v, 0, 0).astype(BF) for p, (q, k, v) in zip(ps, qkv)]
            for (b, h), p, m in zip(each, ps, mixed):
                pt_s[l, c * nb + b, h, :, 0:BLOCK] = p
                mix_s[l, rows(c * nb + b, 1), h * hw : (h + 1) * hw] = m
            return 0

        loop(NBLK // nb, step)

    def wup(l, f):
        return wpart(l, (4 + f) * d, (5 + f) * d)

    def wdown(l, f):
        return wpart(l, 4 * d + ff + f * d, 4 * d + ff + (f + 1) * d)

    def cols(f):
        return slice(f * d, (f + 1) * d)

    def mid_stage(l):
        mid = load_x(l, 0, NBLK) + mm(mix_s[l], wout(l), 1, 1) + vec(l, 2)
        mid_s[l] = mid
        xh, _r = standardize(mid)
        n2_s[l] = (xh * vec(l, 3) + vec(l, 4)).astype(BF)

    def gelu_parts(h):
        t = lax.erf(h * (2 ** -0.5)) + 1.0
        act = ((0.5 * h) * t).astype(BF)
        hb = h.astype(BF)
        e = jnp.exp2(hb * hb * BF(-0.5 * LOG2E))
        return act, t.astype(BF) + hb * e * BF(2 * 0.3989422804014327)

    def chunks(size):
        return [slice(r, r + size) for r in range(0, S, size)]

    def ffn_fwd0(size):
        l, n = 0, ff // d
        ahead = {s.start: mm(n2_s[l, s], wup(l, 0), 1, 1) for s in chunks(size)}
        for f in range(n):
            for s in chunks(size):
                h = ahead[s.start]
                if f + 1 < n:
                    ahead[s.start] = mm(n2_s[l, s], wup(l, f + 1), 1, 1)
                act, dact = gelu_parts(h + vec(l, 6 + f))
                act_s[l, s, cols(f)] = act
                dact_s[s, cols(f)] = dact
        y = mid_s[l] + vec(l, 5) + mm(act_s[l], wpart(l, 4 * d + ff, 4 * d + 2 * ff), 1, 0)
        store_perm(x1_s, 0, NBLK, y)

    def load_gy1():
        for b in range(NBLK):
            live = live_mask(length, b, d)
            part = jnp.where(live, cot_ref[0, :, b], 0.0).reshape(BLOCK, d)
            acc_vec(1, 5, part)
            gy_s[b * BLOCK : (b + 1) * BLOCK] = (0.5 * part).astype(BF)

    def ffn_both1(size):
        l, n = 1, ff // d

        def products(f, s):
            return mm(n2_s[l, s], wup(l, f), 1, 1), mm(gy_s[s], wdown(l, f), 1, 1)

        ahead = {s.start: products(0, s) for s in chunks(size)}
        for f in range(n + 1):
            for i, s in enumerate(chunks(size)):
                if f < n:
                    h, ga = ahead[s.start]
                    if f + 1 < n:
                        ahead[s.start] = products(f + 1, s)
                    act, dact = gelu_parts(h + vec(l, 6 + f))
                    act_s[l, s, cols(f)] = act
                    gup = ga * dact.astype(F32)
                    acc_vec(l, 6 + f, gup)
                    gup_s[s, cols(f)] = gup.astype(BF)
                if f > 0 and i == 0:
                    wgrad(l, 4 * d + ff + (f - 1) * d, gy_s[...], act_s[l, :, cols(f - 1)])
                if f > 0 and i == min(1, S // size - 1):
                    wgrad(l, 4 * d + (f - 1) * d, n2_s[l], gup_s[:, cols(f - 1)])

    def ffn_end1():
        l = 1
        y = mid_s[l] + vec(l, 5) + mm(act_s[l], wpart(l, 4 * d + ff, 4 * d + 2 * ff), 1, 0)
        y4 = y.reshape(NBLK, NBLK, SUBL, d)
        for b in range(NBLK):
            out_ref[0, :, b] = jnp.where(live_mask(length, b, d), y4[b], 0.0)

    def ffn_bwd0(size):
        l, n = 0, ff // d
        for s in chunks(size):
            gy = gy0_s[s.start // BLOCK : s.stop // BLOCK].reshape(size, d)
            acc_vec(l, 5, gy)
            gy_s[s] = (0.5 * gy).astype(BF)
        ahead = {s.start: mm(gy_s[s], wdown(l, 0), 1, 1) for s in chunks(size)}
        for f in range(n + 1):
            for i, s in enumerate(chunks(size)):
                if f < n:
                    ga = ahead[s.start]
                    if f + 1 < n:
                        ahead[s.start] = mm(gy_s[s], wdown(l, f + 1), 1, 1)
                    gup = ga * dact_s[s, cols(f)].astype(F32)
                    acc_vec(l, 6 + f, gup)
                    gup_s[s, cols(f)] = gup.astype(BF)
                if f > 0 and i == 0:
                    wgrad(l, 4 * d + ff + (f - 1) * d, gy_s[...], act_s[l, :, cols(f - 1)])
                if f > 0 and i == min(1, S // size - 1):
                    wgrad(l, 4 * d + (f - 1) * d, n2_s[l], gup_s[:, cols(f - 1)])

    def mid_bwd(l, size):
        for s in chunks(size):
            gn2 = mm(gup_s[s], wpart(l, 4 * d, 4 * d + ff), 1, 0)
            if l == 0:
                gy = gy0_s[s.start // BLOCK : s.stop // BLOCK].reshape(size, d)
            else:
                parts = []
                for b in range(s.start // BLOCK, s.stop // BLOCK):
                    live = live_mask(length, b, d)
                    parts.append(jnp.where(live, cot_ref[0, :, b], 0.0).reshape(BLOCK, d))
                gy = jnp.concatenate(parts, 0)
            gmid = gy + norm_back(l, 3, mid_s[l, s], gn2)
            gmid_s[s] = gmid
            acc_vec(l, 2, gmid)
            gml = gmid.astype(BF)
            gmidl_s[s] = gml
            gmix_s[s] = mm(gml, wout(l), 1, 0).astype(BF)

    def acc_vec(l, i, val, n=1):
        gv_ref[l, :, i * d : (i + n) * d] += rowsum8(val)

    def norm_back(l, gi, v, gn):
        xh, r = standardize(v)
        acc_vec(l, gi, gn * xh)
        acc_vec(l, gi + 1, gn)
        e = gn * vec(l, gi)
        me = jnp.mean(e, -1, keepdims=True)
        mx = jnp.mean(e * xh, -1, keepdims=True)
        return r * (e - me - xh * mx)

    def attn_bwd(l, nb):
        def step(c, _):
            each = [(b, h) for b in range(nb) for h in range(HEADS)]
            qkv, gms = [], []
            for b in range(nb):
                at = rows(c * nb + b, 1)
                qkv += heads_of(pk_s[l, at, :])
                gm = gmix_s[at, :]
                gms += [gm[:, h * hw : (h + 1) * hw] for h in range(HEADS)]
            pts = [pt_s[l, c * nb + b, h, :, 0:BLOCK] for b, h in each]
            gps = [mm(v, gm, 1, 1) for (q, k, v), gm in zip(qkv, gms)]
            gss = []
            for pt, gp in zip(pts, gps):
                pf = pt.astype(F32)
                pg = pf * gp
                gss.append(((pg - pf * jnp.sum(pg, 0, keepdims=True)) * qs).astype(BF))
            gv = [mm(pt, gm, 1, 0).astype(BF) for pt, gm in zip(pts, gms)]
            gk = [mm(gs, q, 1, 0).astype(BF) for gs, (q, k, v) in zip(gss, qkv)]
            gq = [mm(gs, k, 0, 0).astype(BF) for gs, (q, k, v) in zip(gss, qkv)]
            for n, (b, h) in enumerate(each):
                for i, g in enumerate((gq, gk, gv)):
                    gpk_s[rows(c * nb + b, 1), i * d + h * hw : i * d + (h + 1) * hw] = g[n]
            return 0

        loop(NBLK // nb, step)

    def qkv_bwd(l, nb):
        def step(c, _):
            s = rows(c, nb)
            gn1 = mm(gpk_s[s, :], wqkv(l), 1, 0)
            gx = gmid_s[s, :] + norm_back(l, 0, load_x(l, c, nb), gn1)
            if l == 0:
                gin_ref[0, pl.ds(c * nb, nb)] = gx.reshape(nb, NBLK, SUBL, d)
            else:
                store_perm(gy0_s, c, nb, gx)
            return 0

        loop(NBLK // nb, step)

    def wgrad(l, at, a, b):
        gwt_ref[l, :, at : at + b.shape[1]] += mm(a, b, 0, 0)

    def wgrads(l):
        wgrad(l, 0, n1_s[l], gpk_s[...])
        wgrad(l, 3 * d, mix_s[l], gmidl_s[...])

    def region(step):
        pl.when(img >= 0)(step)

    def between(first, step):
        if own:
            pl.when(img == 0 if first else last)(step)

    region(lambda: qkv_fwd(0, NBLK))
    region(lambda: attn_fwd(0, NBLK))
    between(True, lambda: move.gather_diagonal(1))
    region(lambda: mid_stage(0))
    region(lambda: ffn_fwd0(SIZE[4]))
    between(True, lambda: move.gather_end(1))
    region(lambda: qkv_fwd(1, NBLK))
    region(lambda: attn_fwd(1, NBLK))
    region(lambda: mid_stage(1))
    region(load_gy1)
    region(lambda: ffn_both1(SIZE[0]))
    region(ffn_end1)
    region(lambda: mid_bwd(1, SIZE[1]))
    region(lambda: attn_bwd(1, NBLK))
    region(lambda: qkv_bwd(1, NBLK))
    region(lambda: wgrads(1))
    between(False, lambda: move.sum_start(1))
    region(lambda: ffn_bwd0(SIZE[2]))
    between(False, lambda: move.sum_chip(1))
    region(lambda: mid_bwd(0, SIZE[3]))
    region(lambda: attn_bwd(0, NBLK))
    region(lambda: qkv_bwd(0, NBLK))
    region(lambda: wgrads(0))
    between(False, lambda: move.sum_start(0))
    between(False, lambda: move.sum_across(1))

    @pl.when(last)
    def _():
        if own:
            move.sum_chip(0)
            move.sum_column(1)
            move.sum_across(0)
            move.sum_end(1)
            move.sum_column(0)
            move.sum_end(0)
            move.drain()
        else:
            for l in range(2):
                gw_ref[l] = whole_grad(gwt_ref, l, 4 * d + ff)
                gvo_ref[l] = jnp.sum(gv_ref[l], 0, keepdims=True)


def whole_grad(gwt_ref, l, cut):
    return jnp.concatenate([gwt_ref[l, :, :cut], 2.0 * gwt_ref[l, :, cut:]], 1).T


MESH = pl.DeviceIdType.MESH


def column(y, x, core):
    return (y * 2 + x) * 2 + core


class Moves:
    def __init__(self, z_count, w_ref, v_ref, gwt_ref, gv_ref, vs_s, gw_ref, gvo_ref, refs):
        self.z_count = z_count
        self.w_ref, self.v_ref, self.gwt_ref, self.gv_ref = w_ref, v_ref, gwt_ref, gv_ref
        self.vs_s, self.gw_ref, self.gvo_ref = vs_s, gw_ref, gvo_ref
        (
            self.full_s, self.gb_s, self.sib_s, self.own_s, self.diag_top_s, self.diag_low_s,
            self.cols_s, self.zr_s,
            self.ag_link, self.ag_core, self.ag_z, self.ag_x, self.ag_y, self.ag_c,
            self.rs_core_send, self.rs_core_recv, self.rs_send, self.rs_recv,
            self.rs_z_send, self.rs_z_recv,
        ) = refs
        self.rows, self.d = w_ref.shape[1], w_ref.shape[2]
        self.block = self.full_s.shape[2]
        self.half = self.diag_top_s.shape[2]
        self.devices = self.full_s.shape[1]
        self.vrow = v_ref.shape[1]
        self.vlen = self.vrow * self.devices
        dp, z = lax.axis_index("dp"), lax.axis_index("sub")
        self.dp, self.z = dp, z
        self.core = dp % 2
        self.x = dp // 2 % 2
        self.y = dp // 4
        y, x = self.y, self.x
        self.chips = ((y, x), (y, 1 - x), (1 - y, x), (1 - y, 1 - x))
        self.dp_x = column(y, 1 - x, self.core)
        self.dp_y = column(1 - y, x, self.core)
        self.dp_c = column(y, x, 1 - self.core)
        self.cut = (pl.ds(0, self.half), pl.ds(self.half, self.block - self.half))
        near = [0]
        for k in range(1, z_count // 2 + 1):
            near.append(k)
            if z_count - k != k:
                near.append(z_count - k)
        self.near = near

    def zz(self, k):
        return lax.rem(self.z + k, self.z_count)

    def index(self, kind, t, core=None):
        yy, xx = self.chips[kind]
        return column(yy, xx, self.core if core is None else core) * self.z_count + t

    def slot(self, kind, t):
        yy, xx = self.chips[kind]
        return (yy * 2 + xx) * self.z_count + t

    def weights(self, l, a, b):
        parts, rows = [], self.rows
        while a < b:
            i = a // rows
            e = min(b, (i + 1) * rows)
            parts.append(self.full_s[l, i, a - i * rows : e - i * rows, :])
            a = e
        return jnp.concatenate(parts, 0)

    def remote(self, src, dst, send, recv, target):
        return pltpu.make_async_remote_copy(
            src_ref=src, dst_ref=dst, send_sem=send, recv_sem=recv,
            device_id=target, device_id_type=MESH,
        )

    def ag_copy(self, l, kind, t, way, part=None):
        i, s = self.index(kind, t), self.slot(kind, t)
        ref = self.full_s.at[l, i] if part is None else self.full_s.at[l, i, self.cut[part], :]
        if way == "c":
            return self.remote(
                ref, ref, self.ag_c.at[l, s], self.ag_core.at[l, s], (self.dp_c, self.z)
            )
        send = self.ag_x if way == "x" else self.ag_y
        target = (self.dp_x if way == "x" else self.dp_y, self.z)
        return self.remote(ref, ref, send.at[l, s], self.ag_link.at[l, 1 if part else 0, s], target)

    def ag_along(self, l, k):
        ref = self.full_s.at[l, self.index(0, self.z)]
        s = self.slot(0, self.z)
        return self.remote(
            ref, ref, self.ag_z.at[l, k], self.ag_link.at[l, 0, s], (self.dp, self.zz(k))
        )

    def ag_wait(self, l, kind, t, part=None):
        i, s = self.index(kind, t), self.slot(kind, t)
        ref = self.full_s.at[l, i] if part is None else self.full_s.at[l, i, self.cut[part], :]
        self.remote(
            ref, ref, self.ag_c.at[l, s], self.ag_link.at[l, 1 if part else 0, s],
            (self.dp_c, self.z),
        ).wait_recv()

    def gather_along(self, l):
        for k in self.near[1:]:
            self.ag_along(l, k).start()

    def gather_spread(self, l, steps):
        for k in steps:
            t = self.zz(k)
            if k:
                self.ag_wait(l, 0, t)
            for way in "xyc":
                self.ag_copy(l, 0, t, way).start()

    def gather_across(self, l):
        for k in self.near:
            t = self.zz(k)
            self.ag_wait(l, 1, t)
            self.ag_copy(l, 1, t, "y", 0).start()
            self.ag_copy(l, 1, t, "c").start()
            self.ag_wait(l, 2, t)
            self.ag_copy(l, 2, t, "x", 1).start()
            self.ag_copy(l, 2, t, "c").start()

    def gather_diagonal(self, l):
        for k in self.near:
            t = self.zz(k)
            self.ag_wait(l, 3, t, 0)
            self.ag_wait(l, 3, t, 1)
            self.ag_copy(l, 3, t, "c").start()

    def gather_end(self, l):
        for kind in range(4):
            for t in range(self.z_count):
                i, s = self.index(kind, t, 1 - self.core), self.slot(kind, t)
                ref = self.full_s.at[l, i]
                self.remote(
                    ref, ref, self.ag_c.at[l, s], self.ag_core.at[l, s], (self.dp_c, self.z)
                ).wait_recv()
        vrow, vlen, rows = self.vrow, self.vlen, self.rows
        self.vs_s[l] = jnp.zeros((8, vlen), F32)
        for i in range(self.devices):
            part = self.full_s[l, i, rows : self.block, 0:128].astype(F32)[0:8]
            at = i * vrow // 128 * 128
            wide = jnp.concatenate([part, jnp.zeros_like(part)], 1)
            if i * vrow > at:
                wide = pltpu.roll(wide, i * vrow - at, 1)
            n = min(256, vlen - at)
            self.vs_s[l, 0:1, at : at + n] += wide[0:1, 0:n]

    def gather_first(self, meanwhile):
        barrier = pltpu.get_barrier_semaphore()
        partners = [(p, self.z) for p in (self.dp_x, self.dp_y, self.dp_c)]
        partners += [(self.dp, self.zz(k)) for k in self.near[1:]]
        for p in partners:
            pl.semaphore_signal(barrier, inc=1, device_id=p, device_id_type=MESH)
        me, rows = self.index(0, self.z), self.rows
        for l in range(2):
            self.full_s[l, me, 0:rows] = self.w_ref[l]
            tail = jnp.zeros((self.block - rows, self.d - self.vrow), BF)
            v = self.v_ref[l : l + 1, :].astype(F32)
            v = jnp.concatenate([v, jnp.zeros((self.block - rows - 1, self.vrow), F32)], 0)
            self.full_s[l, me, rows : self.block, :] = jnp.concatenate([v.astype(BF), tail], 1)
        pl.semaphore_wait(barrier, len(partners))
        self.gather_along(0)
        self.gather_spread(0, (0,))
        self.gather_along(1)
        self.gather_spread(1, (0,))
        meanwhile()
        self.gather_spread(0, self.near[1:])
        self.gather_spread(1, self.near[1:])
        self.gather_across(0)
        self.gather_across(1)
        self.gather_diagonal(0)
        self.gather_end(0)

    def rs_core(self, l, kind):
        i = self.index(kind, 0, 1 - self.core)
        return self.remote(
            self.gb_s.at[l, pl.ds(i, self.z_count)], self.sib_s.at[l, kind],
            self.rs_core_send.at[l, kind], self.rs_core_recv.at[l, kind], (self.dp_c, self.z),
        )

    def rs_across(self, l, slot, t):
        kind, half, target, dst = (
            (3, 0, self.dp_y, self.diag_top_s.at[l, t]),
            (3, 1, self.dp_x, self.diag_low_s.at[l, t]),
            (2, 0, self.dp_y, self.cols_s.at[l, 0, t, self.cut[0], :]),
            (1, 1, self.dp_x, self.cols_s.at[l, 0, t, self.cut[1], :]),
            (1, 0, self.dp_x, self.cols_s.at[l, 1, t, self.cut[0], :]),
            (2, 1, self.dp_y, self.cols_s.at[l, 1, t, self.cut[1], :]),
        )[slot]
        return self.remote(
            self.gb_s.at[l, self.index(kind, t), self.cut[half], :], dst,
            self.rs_send.at[l, slot, t], self.rs_recv.at[l, slot, t], (target, self.z),
        )

    def rs_along(self, l, k):
        return self.remote(
            self.gb_s.at[l, self.index(0, self.zz(k))], self.zr_s.at[l, k - 1],
            self.rs_z_send.at[l, k], self.rs_z_recv.at[l, k], (self.dp, self.zz(k)),
        )

    def sum_start(self, l):
        rows, vrow, vlen = self.rows, self.vrow, self.vlen
        g = whole_grad(self.gwt_ref, l, (rows * self.devices) // 2 + 2 * self.d).astype(BF)
        gv = jnp.sum(self.gv_ref[l], 0, keepdims=True)
        gv = jnp.concatenate([gv, jnp.zeros((7, vlen), F32)], 0)
        for i in range(self.devices):
            self.gb_s[l, i, 0:rows] = g[i * rows : (i + 1) * rows]
            at = i * vrow // 128 * 128
            n = min(256, vlen - at)
            wide = gv[:, at : at + n]
            if n < 256:
                wide = jnp.concatenate([wide, jnp.zeros_like(wide)], 1)
            if i * vrow > at:
                wide = pltpu.roll(wide, 256 - (i * vrow - at), 1)
            wide = jnp.concatenate([wide, jnp.zeros_like(wide)], 0)
            self.gb_s[l, i, rows : self.block] = wide.astype(BF)
        for kind in (3, 1, 2, 0):
            self.rs_core(l, kind).start()

    def sum_chip(self, l):
        for kind, slots in ((3, (0, 1)), (1, (3,)), (2, (2,)), (0, ())):
            self.rs_core(l, kind).wait_recv()
            for t in range(self.z_count):
                i = self.index(kind, t)
                both = self.gb_s[l, i].astype(F32) + self.sib_s[l, kind, t].astype(F32)
                if kind == 0:
                    self.own_s[l, t] = both
                else:
                    self.gb_s[l, i] = both.astype(BF)
                for slot in slots:
                    self.rs_across(l, slot, t).start()

    def sum_across(self, l):
        for t in range(self.z_count):
            for slot, kind, half, ref in (
                (0, 1, 0, self.diag_top_s), (1, 2, 1, self.diag_low_s),
            ):
                self.rs_across(l, slot, t).wait_recv()
                i, cut = self.index(kind, t), self.cut[half]
                both = self.gb_s[l, i, cut].astype(F32) + ref[l, t].astype(F32)
                self.gb_s[l, i, cut] = both.astype(BF)
                self.rs_across(l, 4 if half == 0 else 5, t).start()

    def sum_column(self, l):
        for k in self.near[1:] + [0]:
            t = self.zz(k)
            for slot in (2, 3, 4, 5):
                self.rs_across(l, slot, t).wait_recv()
            total = self.own_s[l, t]
            for a in range(2):
                total = total + self.cols_s[l, a, t].astype(F32)
            if k:
                self.gb_s[l, self.index(0, t)] = total.astype(BF)
                self.rs_along(l, k).start()
            else:
                self.own_s[l, t] = total

    def sum_end(self, l):
        for k in self.near[1:]:
            self.rs_along(l, k).wait_recv()
        total = self.own_s[l, self.z]
        for k in self.near[1:]:
            total = total + self.zr_s[l, k - 1].astype(F32)
        self.gw_ref[l] = total[0 : self.rows]
        self.gvo_ref[l : l + 1, :] = total[self.rows : self.rows + 1, 0 : self.vrow]

    def drain(self):
        for l in range(2):
            for k in self.near[1:]:
                self.ag_along(l, k).wait_send()
                self.rs_along(l, k).wait_send()
            for t in range(self.z_count):
                for kind in range(4):
                    self.ag_copy(l, kind, t, "c").wait_send()
                self.ag_copy(l, 0, t, "x").wait_send()
                self.ag_copy(l, 0, t, "y").wait_send()
                self.ag_copy(l, 1, t, "y", 0).wait_send()
                self.ag_copy(l, 2, t, "x", 1).wait_send()
                for slot in range(6):
                    self.rs_across(l, slot, t).wait_send()
            for kind in range(4):
                self.rs_core(l, kind).wait_send()


def compute(x, cot, w, v, lengths, dims, own, z_count):
    d, ff = dims
    n = lengths.shape[0]
    mrows, vlen = 4 * d + 2 * ff, 6 * d + ff
    img = pl.BlockSpec((1, ROWS, NBLK, SUBL, d), lambda i: (i, 0, 0, 0, 0))
    shp = (n, ROWS, NBLK, SUBL, d)

    def whole(shape):
        zero = (0,) * len(shape)
        return pl.BlockSpec(shape, lambda i: zero, pipeline_mode=pl.Buffered(1))

    scratch = [
        pltpu.VMEM((2, 8, vlen), F32),
        pltpu.VMEM((2, d, mrows), F32),
        pltpu.VMEM((2, 8, vlen), F32),
        pltpu.VMEM((2, S, d), BF),
        pltpu.VMEM((2, S, 3 * d), BF),
        pltpu.VMEM((2, NBLK, HEADS, BLOCK, 128), BF),
        pltpu.VMEM((2, S, d), BF),
        pltpu.VMEM((2, S, d), F32),
        pltpu.VMEM((2, S, d), BF),
        pltpu.VMEM((2, S, ff), BF),
        pltpu.VMEM((S, ff), BF),
        pltpu.VMEM((NBLK, ROWS, SUBL, d), F32),
        pltpu.VMEM((ROWS, NBLK, SUBL, d), F32),
        pltpu.VMEM((S, d), BF),
        pltpu.VMEM((S, ff), BF),
        pltpu.VMEM((S, d), F32),
        pltpu.VMEM((S, d), BF),
        pltpu.VMEM((S, d), BF),
        pltpu.VMEM((S, 3 * d), BF),
    ]
    if own:
        rows, vrow = w.shape[1], v.shape[1]
        devices = mrows // rows
        block = rows + 16
        half = (block // 2 + 15) // 16 * 16
        zc = z_count
        dma = pltpu.SemaphoreType.DMA
        scratch += [
            pltpu.VMEM((2, devices, block, d), BF),
            pltpu.VMEM((2, devices, block, d), BF),
            pltpu.VMEM((2, 4, zc, block, d), BF),
            pltpu.VMEM((2, zc, block, d), F32),
            pltpu.VMEM((2, zc, half, d), BF),
            pltpu.VMEM((2, zc, block - half, d), BF),
            pltpu.VMEM((2, 2, zc, block, d), BF),
            pltpu.VMEM((2, zc - 1, block, d), BF),
            dma((2, 2, 4 * zc)), dma((2, 4 * zc)), dma((2, zc)),
            dma((2, 4 * zc)), dma((2, 4 * zc)), dma((2, 4 * zc)),
            dma((2, 4)), dma((2, 4)), dma((2, 6, zc)), dma((2, 6, zc)),
            dma((2, zc)), dma((2, zc)),
        ]
        gw_shape, gv_shape = (2, rows, d), (2, vrow)
    else:
        gw_shape, gv_shape = (2, mrows, d), (2, 1, vlen)
    return pl.pallas_call(
        partial(kernel, dims, own, z_count),
        grid=(n,),
        in_specs=[pl.BlockSpec(memory_space=pltpu.SMEM), img, img, whole(w.shape), whole(v.shape)],
        out_specs=[img, img, whole(gw_shape), whole(gv_shape)],
        out_shape=[
            jax.ShapeDtypeStruct(shp, F32),
            jax.ShapeDtypeStruct(shp, F32),
            jax.ShapeDtypeStruct(gw_shape, F32),
            jax.ShapeDtypeStruct(gv_shape, F32),
        ],
        scratch_shapes=scratch,
        compiler_params=pltpu.CompilerParams(
            dimension_semantics=("arbitrary",),
            vmem_limit_bytes=63 << 20,
            collective_id=0 if own else None,
            has_side_effects=own,
        ),
        name="layers",
    )(lengths, x.reshape(shp), cot.reshape(shp), w, v)


def body(z_count, dp_count, inputs, matrices, vectors, lengths, cotangent):
    d = inputs.shape[1]
    devices = z_count * dp_count
    ff = (matrices.shape[1] * devices - 4 * d) // 2
    own = dp_count == 8
    split = ("dp", "sub")
    if own:
        w, v = matrices, vectors
    else:
        w = lax.all_gather(matrices, split, axis=1, tiled=True)
        v = lax.all_gather(vectors, split, axis=1, tiled=True).astype(F32)[:, None, :]
    out, gin, gw, gv = compute(inputs, cotangent, w, v, lengths, (d, ff), own, z_count)
    if not own:
        gw = lax.psum_scatter(gw, split, scatter_dimension=1, tiled=True)
        gv = lax.psum_scatter(gv[:, 0], split, scatter_dimension=1, tiled=True)
    return (out.reshape(inputs.shape), gin.reshape(inputs.shape), gw, gv)


def solution(mesh):
    split = ("dp", "sub")
    return jax.shard_map(
        partial(body, mesh.shape["sub"], mesh.shape["dp"]),
        mesh=mesh,
        in_specs=(P(split, None), P(None, split, None), P(None, split), P(split), P(split, None)),
        out_specs=(P(split, None), P(split, None), P(None, split, None), P(None, split)),
        check_vma=False,
    )
```

```python
from functools import partial

import jax
import jax.numpy as jnp
from jax import lax
from jax.experimental import pallas as pl
from jax.experimental.pallas import tpu as pltpu
from jax.sharding import PartitionSpec as P

HEADS = 2
COLS = 96
ROWS = 12
SUBL = 8
BLOCK = 96
NBLK = 12
S = COLS * ROWS
LOG2E = 1.4426950408889634
BF = jnp.bfloat16
F32 = jnp.float32
STATIC = False
SIZE = (288, 576, 576, 576, 576)
NB = (4, 4, 4, 4)


def mm(a, b, ca, cb):
    return lax.dot_general(a, b, (((ca,), (cb,)), ((), ())), preferred_element_type=F32)


def standardize(v):
    c = v - jnp.mean(v, -1, keepdims=True)
    r = lax.rsqrt(jnp.mean(c * c, -1, keepdims=True) + 1e-05)
    return c * r, r


def rowsum8(v):
    return jnp.sum(v.reshape(v.shape[0] // 8, 8, v.shape[1]), axis=0)


def live_mask(length, slab, width):
    row = lax.broadcasted_iota(jnp.int32, (ROWS, SUBL, width), 0)
    col = lax.broadcasted_iota(jnp.int32, (ROWS, SUBL, width), 1)
    return row * COLS + col + slab * SUBL < length


def kernel(dims, own, z_count, *refs):
    d, ff = dims
    len_ref, x_ref, cot_ref, w_ref, v_ref, out_ref, gin_ref, gw_ref, gvo_ref = refs[:9]
    (
        vs_s, gwt_ref, gv_ref, n1_s, pk_s, pt_s, mix_s, mid_s, n2_s, act_s, dact_s,
        x1_s, gy0_s, gy_s, gup_s, gmid_s, gmidl_s, gmix_s, gpk_s,
    ) = refs[9:28]
    img = pl.program_id(0)
    last = img == pl.num_programs(0) - 1
    length = len_ref[img]
    hw = d // HEADS
    qs = hw ** -0.5
    if own:
        move = Moves(z_count, w_ref, v_ref, gwt_ref, gv_ref, vs_s, gw_ref, gvo_ref, refs[28:])
        wpart = move.weights
    else:

        def wpart(l, a, b):
            return w_ref[l, a:b, :]

    @pl.when(img == 0)
    def _():
        def clear():
            gwt_ref[...] = jnp.zeros_like(gwt_ref)
            gv_ref[...] = jnp.zeros_like(gv_ref)

        if own:
            move.gather_first(clear)
        else:
            clear()
            vs_s[:, 0:1, :] = v_ref[...]

    def wqkv(l):
        return wpart(l, 0, 3 * d)

    def wout(l):
        return wpart(l, 3 * d, 4 * d)

    def vec(l, i, n=1):
        return vs_s[l, 0:1, i * d : (i + n) * d]

    tril_b = lax.broadcasted_iota(jnp.int32, (BLOCK, BLOCK), 0)
    tril_a = lax.broadcasted_iota(jnp.int32, (BLOCK, BLOCK), 1)
    masks = (
        tril_b <= tril_a,
        (tril_b <= tril_a) & ((tril_b & (SUBL - 1)) == (tril_a & (SUBL - 1))),
    )

    def load_x(l, c, nb):
        if l == 0:
            return x_ref[0, pl.ds(c * nb, nb)].reshape(nb * BLOCK, d)
        return x1_s[pl.ds(c * nb, nb)].reshape(nb * BLOCK, d)

    def store_perm(ref, c, nb, val, lead=()):
        v4 = val.reshape(nb, NBLK, SUBL, d)
        for b in range(nb):
            ref[lead + (slice(None), c * nb + b)] = v4[b]

    def rows(c, nb):
        if isinstance(c, int):
            return pl.ds(c * nb * BLOCK, nb * BLOCK)
        return pl.ds(pl.multiple_of(c * nb * BLOCK, BLOCK), nb * BLOCK)

    def loop(n, step):
        if STATIC or n == 1:
            for c in range(n):
                step(c, 0)
        else:
            lax.fori_loop(0, n, step, 0)

    def heads_of(packed):
        return [
            tuple(packed[:, i * d + h * hw : i * d + (h + 1) * hw] for i in range(3))
            for h in range(HEADS)
        ]

    def pipeline(stages, n):
        for i in range(n + len(stages) - 1):
            for j in reversed(range(len(stages))):
                if 0 <= i - j < n:
                    stages[j](i - j)

    def front(l, nb):
        mask = masks[l]
        qkv, scores, ps = {}, {}, {}

        def each(c):
            return [(c * nb + b, h) for b in range(nb) for h in range(HEADS)]

        def normed(c):
            xh, _r = standardize(load_x(l, c, nb))
            n1_s[l, rows(c, nb), :] = (xh * vec(l, 0) + vec(l, 1)).astype(BF)

        def project(c):
            pk_s[l, rows(c, nb), :] = mm(n1_s[l, rows(c, nb), :], wqkv(l), 1, 1).astype(BF)

        def score(c):
            qkv[c] = []
            for b in range(nb):
                qkv[c] += heads_of(pk_s[l, rows(c * nb + b, 1), :])
            scores[c] = [mm(k, q, 1, 1) for q, k, v in qkv[c]]

        def soft(c):
            ps[c] = []
            for st, (b, h) in zip(scores.pop(c), each(c)):
                st = jnp.where(mask, st, -1e30)
                p = jnp.exp2((st - jnp.max(st, 0, keepdims=True)) * (qs * LOG2E))
                p = (p * (1.0 / jnp.sum(p, 0, keepdims=True))).astype(BF)
                pt_s[l, b, h, :, 0:BLOCK] = p
                ps[c].append(p)

        def mix(c):
            for p, (q, k, v), (b, h) in zip(ps.pop(c), qkv.pop(c), each(c)):
                mix_s[l, rows(b, 1), h * hw : (h + 1) * hw] = mm(p, v, 0, 0).astype(BF)

        def middle(c):
            r = rows(c, nb)
            mid = load_x(l, c, nb) + mm(mix_s[l, r, :], wout(l), 1, 1) + vec(l, 2)
            mid_s[l, r, :] = mid
            xh, _r = standardize(mid)
            n2_s[l, r, :] = (xh * vec(l, 3) + vec(l, 4)).astype(BF)

        pipeline([normed, project, score, soft, mix, middle], NBLK // nb)

    def wup(l, f):
        return wpart(l, (4 + f) * d, (5 + f) * d)

    def wdown(l, f):
        return wpart(l, 4 * d + ff + f * d, 4 * d + ff + (f + 1) * d)

    def cols(f):
        return slice(f * d, (f + 1) * d)

    def gelu_parts(h):
        t = lax.erf(h * (2 ** -0.5)) + 1.0
        act = ((0.5 * h) * t).astype(BF)
        hb = h.astype(BF)
        e = jnp.exp2(hb * hb * BF(-0.5 * LOG2E))
        return act, t.astype(BF) + hb * e * BF(2 * 0.3989422804014327)

    def chunks(size):
        return [slice(r, r + size) for r in range(0, S, size)]

    def ffn_fwd0(size):
        l, n = 0, ff // d
        ahead = {s.start: mm(n2_s[l, s], wup(l, 0), 1, 1) for s in chunks(size)}
        for f in range(n):
            for s in chunks(size):
                h = ahead[s.start]
                if f + 1 < n:
                    ahead[s.start] = mm(n2_s[l, s], wup(l, f + 1), 1, 1)
                act, dact = gelu_parts(h + vec(l, 6 + f))
                act_s[l, s, cols(f)] = act
                dact_s[s, cols(f)] = dact
        y = mid_s[l] + vec(l, 5) + mm(act_s[l], wpart(l, 4 * d + ff, 4 * d + 2 * ff), 1, 0)
        store_perm(x1_s, 0, NBLK, y)

    def load_gy1():
        for b in range(NBLK):
            live = live_mask(length, b, d)
            part = jnp.where(live, cot_ref[0, :, b], 0.0).reshape(BLOCK, d)
            acc_vec(1, 5, part)
            gy_s[b * BLOCK : (b + 1) * BLOCK] = (0.5 * part).astype(BF)

    def ffn_both1(size):
        l, n = 1, ff // d

        def products(f, s):
            return mm(n2_s[l, s], wup(l, f), 1, 1), mm(gy_s[s], wdown(l, f), 1, 1)

        ahead = {s.start: products(0, s) for s in chunks(size)}
        for f in range(n + 1):
            for i, s in enumerate(chunks(size)):
                if f < n:
                    h, ga = ahead[s.start]
                    if f + 1 < n:
                        ahead[s.start] = products(f + 1, s)
                    act, dact = gelu_parts(h + vec(l, 6 + f))
                    act_s[l, s, cols(f)] = act
                    gup = ga * dact.astype(F32)
                    acc_vec(l, 6 + f, gup)
                    gup_s[s, cols(f)] = gup.astype(BF)
                if f > 0 and i == 0:
                    wgrad(l, 4 * d + ff + (f - 1) * d, gy_s[...], act_s[l, :, cols(f - 1)])
                if f > 0 and i == min(1, S // size - 1):
                    wgrad(l, 4 * d + (f - 1) * d, n2_s[l], gup_s[:, cols(f - 1)])

    def ffn_end1():
        l = 1
        y = mid_s[l] + vec(l, 5) + mm(act_s[l], wpart(l, 4 * d + ff, 4 * d + 2 * ff), 1, 0)
        y4 = y.reshape(NBLK, NBLK, SUBL, d)
        for b in range(NBLK):
            out_ref[0, :, b] = jnp.where(live_mask(length, b, d), y4[b], 0.0)

    def ffn_bwd0(size):
        l, n = 0, ff // d
        for s in chunks(size):
            gy = gy0_s[s.start // BLOCK : s.stop // BLOCK].reshape(size, d)
            acc_vec(l, 5, gy)
            gy_s[s] = (0.5 * gy).astype(BF)
        ahead = {s.start: mm(gy_s[s], wdown(l, 0), 1, 1) for s in chunks(size)}
        for f in range(n + 1):
            for i, s in enumerate(chunks(size)):
                if f < n:
                    ga = ahead[s.start]
                    if f + 1 < n:
                        ahead[s.start] = mm(gy_s[s], wdown(l, f + 1), 1, 1)
                    gup = ga * dact_s[s, cols(f)].astype(F32)
                    acc_vec(l, 6 + f, gup)
                    gup_s[s, cols(f)] = gup.astype(BF)
                if f > 0 and i == 0:
                    wgrad(l, 4 * d + ff + (f - 1) * d, gy_s[...], act_s[l, :, cols(f - 1)])
                if f > 0 and i == min(1, S // size - 1):
                    wgrad(l, 4 * d + (f - 1) * d, n2_s[l], gup_s[:, cols(f - 1)])

    def acc_vec(l, i, val, n=1):
        gv_ref[l, :, i * d : (i + n) * d] += rowsum8(val)

    def norm_back(l, gi, v, gn):
        xh, r = standardize(v)
        acc_vec(l, gi, gn * xh)
        acc_vec(l, gi + 1, gn)
        e = gn * vec(l, gi)
        me = jnp.mean(e, -1, keepdims=True)
        mx = jnp.mean(e * xh, -1, keepdims=True)
        return r * (e - me - xh * mx)

    def back(l, nb):
        gn2, gn1, qkv, gms, pts, gps, gss = {}, {}, {}, {}, {}, {}, {}

        def each(c):
            return [(c * nb + b, h) for b in range(nb) for h in range(HEADS)]

        def up(c):
            gn2[c] = mm(gup_s[rows(c, nb), :], wpart(l, 4 * d, 4 * d + ff), 1, 0)

        def middle(c):
            r = rows(c, nb)
            if l == 0:
                gy = gy0_s[c * nb : (c + 1) * nb].reshape(nb * BLOCK, d)
            else:
                parts = []
                for b in range(c * nb, (c + 1) * nb):
                    live = live_mask(length, b, d)
                    parts.append(jnp.where(live, cot_ref[0, :, b], 0.0).reshape(BLOCK, d))
                gy = jnp.concatenate(parts, 0)
            gmid = gy + norm_back(l, 3, mid_s[l, r, :], gn2.pop(c))
            gmid_s[r, :] = gmid
            acc_vec(l, 2, gmid)
            gmidl_s[r, :] = gmid.astype(BF)

        def out(c):
            r = rows(c, nb)
            gmix_s[r, :] = mm(gmidl_s[r, :], wout(l), 1, 0).astype(BF)

        def probs(c):
            qkv[c], gms[c] = [], []
            for b in range(c * nb, (c + 1) * nb):
                qkv[c] += heads_of(pk_s[l, rows(b, 1), :])
                gm = gmix_s[rows(b, 1), :]
                gms[c] += [gm[:, h * hw : (h + 1) * hw] for h in range(HEADS)]
            gps[c] = [mm(v, gm, 1, 1) for (q, k, v), gm in zip(qkv[c], gms[c])]

        def store(c, i, grads):
            for (b, h), g in zip(each(c), grads):
                gpk_s[rows(b, 1), i * d + h * hw : i * d + (h + 1) * hw] = g.astype(BF)

        def soft(c):
            pts = [pt_s[l, b, h, :, 0:BLOCK] for b, h in each(c)]
            gss[c] = []
            for pt, gp in zip(pts, gps.pop(c)):
                pf = pt.astype(F32)
                pg = pf * gp
                gss[c].append(((pg - pf * jnp.sum(pg, 0, keepdims=True)) * qs).astype(BF))
            store(c, 2, [mm(pt, gm, 1, 0) for pt, gm in zip(pts, gms.pop(c))])

        def heads(c):
            gs, both = gss.pop(c), qkv.pop(c)
            store(c, 1, [mm(g, q, 1, 0) for g, (q, k, v) in zip(gs, both)])
            store(c, 0, [mm(g, k, 0, 0) for g, (q, k, v) in zip(gs, both)])

        def project(c):
            gn1[c] = mm(gpk_s[rows(c, nb), :], wqkv(l), 1, 0)

        def first(c):
            r = rows(c, nb)
            gx = gmid_s[r, :] + norm_back(l, 0, load_x(l, c, nb), gn1.pop(c))
            if l == 0:
                gin_ref[0, pl.ds(c * nb, nb)] = gx.reshape(nb, NBLK, SUBL, d)
            else:
                store_perm(gy0_s, c, nb, gx)

        pipeline([up, middle, out, probs, soft, heads, project, first], NBLK // nb)

    def wgrad(l, at, a, b):
        gwt_ref[l, :, at : at + b.shape[1]] += mm(a, b, 0, 0)

    def wgrads(l):
        wgrad(l, 0, n1_s[l], gpk_s[...])
        wgrad(l, 3 * d, mix_s[l], gmidl_s[...])

    def region(step):
        pl.when(img >= 0)(step)

    def between(first, step):
        if own:
            pl.when(img == 0 if first else last)(step)

    region(lambda: front(0, NB[0]))
    between(True, lambda: move.gather_diagonal(1))
    region(lambda: ffn_fwd0(SIZE[4]))
    between(True, lambda: move.gather_end(1))
    region(lambda: front(1, NB[1]))
    region(load_gy1)
    region(lambda: ffn_both1(SIZE[0]))
    region(ffn_end1)
    region(lambda: back(1, NB[2]))
    region(lambda: wgrads(1))
    between(False, lambda: move.sum_start(1))
    region(lambda: ffn_bwd0(SIZE[2]))
    between(False, lambda: move.sum_chip(1))
    region(lambda: back(0, NB[3]))
    region(lambda: wgrads(0))
    between(False, lambda: move.sum_start(0))
    between(False, lambda: move.sum_across(1))

    @pl.when(last)
    def _():
        if own:
            move.sum_tail(0, lambda: move.sum_column(1))
            move.sum_end(1)
            move.sum_end(0)
            move.drain()
        else:
            for l in range(2):
                gw_ref[l] = whole_grad(gwt_ref, l, 4 * d + ff)
                gvo_ref[l] = jnp.sum(gv_ref[l], 0, keepdims=True)


def whole_grad(gwt_ref, l, cut):
    return jnp.concatenate([gwt_ref[l, :, :cut], 2.0 * gwt_ref[l, :, cut:]], 1).T


MESH = pl.DeviceIdType.MESH


def column(y, x, core):
    return (y * 2 + x) * 2 + core


class Moves:
    def __init__(self, z_count, w_ref, v_ref, gwt_ref, gv_ref, vs_s, gw_ref, gvo_ref, refs):
        self.z_count = z_count
        self.w_ref, self.v_ref, self.gwt_ref, self.gv_ref = w_ref, v_ref, gwt_ref, gv_ref
        self.vs_s, self.gw_ref, self.gvo_ref = vs_s, gw_ref, gvo_ref
        (
            self.full_s, self.gb_s, self.sib_s, self.own_s, self.diag_top_s, self.diag_low_s,
            self.cols_s, self.zr_s,
            self.ag_link, self.ag_core, self.ag_z, self.ag_x, self.ag_y, self.ag_c,
            self.rs_core_send, self.rs_core_recv, self.rs_send, self.rs_recv,
            self.rs_z_send, self.rs_z_recv,
        ) = refs
        self.rows, self.d = w_ref.shape[1], w_ref.shape[2]
        self.block = self.full_s.shape[2]
        self.half = self.diag_top_s.shape[2]
        self.devices = self.full_s.shape[1]
        self.vrow = v_ref.shape[1]
        self.vlen = self.vrow * self.devices
        dp, z = lax.axis_index("dp"), lax.axis_index("sub")
        self.dp, self.z = dp, z
        self.core = dp % 2
        self.x = dp // 2 % 2
        self.y = dp // 4
        y, x = self.y, self.x
        self.chips = ((y, x), (y, 1 - x), (1 - y, x), (1 - y, 1 - x))
        self.dp_x = column(y, 1 - x, self.core)
        self.dp_y = column(1 - y, x, self.core)
        self.dp_c = column(y, x, 1 - self.core)
        self.cut = (pl.ds(0, self.half), pl.ds(self.half, self.block - self.half))
        self.near = list(range(z_count))
        self.order = self.near[1:] + [0]

    def zz(self, k):
        return self.z ^ k

    def index(self, kind, t, core=None):
        yy, xx = self.chips[kind]
        return column(yy, xx, self.core if core is None else core) * self.z_count + t

    def slot(self, kind, t):
        yy, xx = self.chips[kind]
        return (yy * 2 + xx) * self.z_count + t

    def weights(self, l, a, b):
        parts, rows = [], self.rows
        while a < b:
            i = a // rows
            e = min(b, (i + 1) * rows)
            parts.append(self.full_s[l, i, a - i * rows : e - i * rows, :])
            a = e
        return jnp.concatenate(parts, 0)

    def remote(self, src, dst, send, recv, target):
        return pltpu.make_async_remote_copy(
            src_ref=src, dst_ref=dst, send_sem=send, recv_sem=recv,
            device_id=target, device_id_type=MESH,
        )

    def ag_copy(self, l, kind, t, way, part=None):
        i, s = self.index(kind, t), self.slot(kind, t)
        ref = self.full_s.at[l, i] if part is None else self.full_s.at[l, i, self.cut[part], :]
        if way == "c":
            return self.remote(
                ref, ref, self.ag_c.at[l, s], self.ag_core.at[l, s], (self.dp_c, self.z)
            )
        send = self.ag_x if way == "x" else self.ag_y
        target = (self.dp_x if way == "x" else self.dp_y, self.z)
        return self.remote(ref, ref, send.at[l, s], self.ag_link.at[l, 1 if part else 0, s], target)

    def ag_along(self, l, k):
        ref = self.full_s.at[l, self.index(0, self.z)]
        s = self.slot(0, self.z)
        return self.remote(
            ref, ref, self.ag_z.at[l, k], self.ag_link.at[l, 0, s], (self.dp, self.zz(k))
        )

    def ag_wait(self, l, kind, t, part=None):
        i, s = self.index(kind, t), self.slot(kind, t)
        ref = self.full_s.at[l, i] if part is None else self.full_s.at[l, i, self.cut[part], :]
        self.remote(
            ref, ref, self.ag_c.at[l, s], self.ag_link.at[l, 1 if part else 0, s],
            (self.dp_c, self.z),
        ).wait_recv()

    def gather_along(self, l):
        for k in self.near[1:]:
            self.ag_along(l, k).start()

    def gather_spread(self, l, steps):
        for k in steps:
            t = self.zz(k)
            if k:
                self.ag_wait(l, 0, t)
            for way in "xyc":
                self.ag_copy(l, 0, t, way).start()

    def gather_across(self, l):
        for k in self.near:
            t = self.zz(k)
            self.ag_wait(l, 1, t)
            self.ag_copy(l, 1, t, "y", 0).start()
            self.ag_copy(l, 1, t, "c").start()
            self.ag_wait(l, 2, t)
            self.ag_copy(l, 2, t, "x", 1).start()
            self.ag_copy(l, 2, t, "c").start()

    def gather_diagonal(self, l):
        for k in self.near:
            t = self.zz(k)
            self.ag_wait(l, 3, t, 0)
            self.ag_wait(l, 3, t, 1)
            self.ag_copy(l, 3, t, "c").start()

    def gather_end(self, l):
        for kind in range(4):
            for t in range(self.z_count):
                i, s = self.index(kind, t, 1 - self.core), self.slot(kind, t)
                ref = self.full_s.at[l, i]
                self.remote(
                    ref, ref, self.ag_c.at[l, s], self.ag_core.at[l, s], (self.dp_c, self.z)
                ).wait_recv()
        vrow, vlen, rows = self.vrow, self.vlen, self.rows
        tiles = [jnp.zeros((8, 128), F32)] * (vlen // 128 + 1)
        for i in range(self.devices):
            part = self.full_s[l, i, rows : self.block, 0:128].astype(F32)[0:8]
            at = i * vrow // 128
            wide = jnp.concatenate([part, jnp.zeros_like(part)], 1)
            if i * vrow > at * 128:
                wide = pltpu.roll(wide, i * vrow - at * 128, 1)
            tiles[at] += wide[:, 0:128]
            tiles[at + 1] += wide[:, 128:256]
        self.vs_s[l] = jnp.concatenate(tiles[:-1], 1)

    def gather_first(self, meanwhile):
        barrier = pltpu.get_barrier_semaphore()
        partners = [(p, self.z) for p in (self.dp_x, self.dp_y, self.dp_c)]
        partners += [(self.dp, self.zz(k)) for k in self.near[1:]]
        for p in partners:
            pl.semaphore_signal(barrier, inc=1, device_id=p, device_id_type=MESH)
        me, rows = self.index(0, self.z), self.rows
        for l in range(2):
            self.full_s[l, me, 0:rows] = self.w_ref[l]
            tail = jnp.zeros((self.block - rows, self.d - self.vrow), BF)
            v = self.v_ref[l : l + 1, :].astype(F32)
            v = jnp.concatenate([v, jnp.zeros((self.block - rows - 1, self.vrow), F32)], 0)
            self.full_s[l, me, rows : self.block, :] = jnp.concatenate([v.astype(BF), tail], 1)
        pl.semaphore_wait(barrier, len(partners))
        self.gather_along(0)
        self.gather_spread(0, (0,))
        self.gather_along(1)
        self.gather_spread(1, (0,))
        meanwhile()
        self.gather_spread(0, self.near[1:])
        self.gather_spread(1, self.near[1:])
        self.gather_across(0)
        self.gather_across(1)
        self.gather_diagonal(0)
        self.gather_end(0)

    def rs_core(self, l, kind):
        i = self.index(kind, 0, 1 - self.core)
        return self.remote(
            self.gb_s.at[l, pl.ds(i, self.z_count)], self.sib_s.at[l, kind],
            self.rs_core_send.at[l, kind], self.rs_core_recv.at[l, kind], (self.dp_c, self.z),
        )

    def rs_across(self, l, slot, t):
        kind, half, target, dst = (
            (3, 0, self.dp_y, self.diag_top_s.at[l, t]),
            (3, 1, self.dp_x, self.diag_low_s.at[l, t]),
            (2, 0, self.dp_y, self.cols_s.at[l, 0, t, self.cut[0], :]),
            (1, 1, self.dp_x, self.cols_s.at[l, 0, t, self.cut[1], :]),
            (1, 0, self.dp_x, self.cols_s.at[l, 1, t, self.cut[0], :]),
            (2, 1, self.dp_y, self.cols_s.at[l, 1, t, self.cut[1], :]),
        )[slot]
        return self.remote(
            self.gb_s.at[l, self.index(kind, t), self.cut[half], :], dst,
            self.rs_send.at[l, slot, t], self.rs_recv.at[l, slot, t], (target, self.z),
        )

    def rs_along(self, l, k):
        return self.remote(
            self.gb_s.at[l, self.index(0, self.zz(k))], self.zr_s.at[l, k - 1],
            self.rs_z_send.at[l, k], self.rs_z_recv.at[l, k], (self.dp, self.zz(k)),
        )

    def sum_start(self, l):
        rows, vrow, vlen = self.rows, self.vrow, self.vlen
        g = whole_grad(self.gwt_ref, l, (rows * self.devices) // 2 + 2 * self.d).astype(BF)
        gv = jnp.sum(self.gv_ref[l], 0, keepdims=True)
        gv = jnp.concatenate([gv, jnp.zeros((7, vlen), F32)], 0)
        for i in range(self.devices):
            self.gb_s[l, i, 0:rows] = g[i * rows : (i + 1) * rows]
            at = i * vrow // 128 * 128
            n = min(256, vlen - at)
            wide = gv[:, at : at + n]
            if n < 256:
                wide = jnp.concatenate([wide, jnp.zeros_like(wide)], 1)
            if i * vrow > at:
                wide = pltpu.roll(wide, 256 - (i * vrow - at), 1)
            wide = jnp.concatenate([wide, jnp.zeros_like(wide)], 0)
            self.gb_s[l, i, rows : self.block] = wide.astype(BF)
        for kind in (3, 1, 2, 0):
            self.rs_core(l, kind).start()

    def chip_step(self, l, k):
        t = self.zz(k)
        for kind, slots in ((3, (0, 1)), (1, (3,)), (2, (2,)), (0, ())):
            i = self.index(kind, t)
            mine, other = self.gb_s[l, i], self.sib_s[l, kind, t]
            if kind == 0:
                self.own_s[l, t] = mine.astype(F32) + other.astype(F32)
            else:
                self.gb_s[l, i] = mine + other
            for slot in slots:
                self.rs_across(l, slot, t).start()

    def across_step(self, l, k):
        t = self.zz(k)
        for slot, kind, half, ref in (
            (0, 1, 0, self.diag_top_s), (1, 2, 1, self.diag_low_s),
        ):
            self.rs_across(l, slot, t).wait_recv()
            i, cut = self.index(kind, t), self.cut[half]
            self.gb_s[l, i, cut] = self.gb_s[l, i, cut] + ref[l, t]
            self.rs_across(l, 4 if half == 0 else 5, t).start()

    def column_step(self, l, k):
        t = self.zz(k)
        for slot in (2, 3, 4, 5):
            self.rs_across(l, slot, t).wait_recv()
        total = self.own_s[l, t]
        for a in range(2):
            total = total + self.cols_s[l, a, t].astype(F32)
        if k:
            self.gb_s[l, self.index(0, t)] = total.astype(BF)
            self.rs_along(l, k).start()
        else:
            self.own_s[l, t] = total

    def sum_core(self, l):
        for kind in (3, 1, 2, 0):
            self.rs_core(l, kind).wait_recv()

    def sum_chip(self, l):
        self.sum_core(l)
        for k in self.order:
            self.chip_step(l, k)

    def sum_across(self, l):
        for k in self.order:
            self.across_step(l, k)

    def sum_column(self, l):
        for k in self.order:
            self.column_step(l, k)

    def sum_tail(self, l, meanwhile):
        order = self.order
        self.sum_core(l)
        self.chip_step(l, order[0])
        self.chip_step(l, order[1])
        meanwhile()
        for n in range(len(order) + 2):
            if n < len(order):
                self.across_step(l, order[n])
            if 1 <= n <= len(order):
                self.column_step(l, order[n - 1])
            if n + 2 < len(order):
                self.chip_step(l, order[n + 2])

    def sum_end(self, l):
        for k in self.near[1:]:
            self.rs_along(l, k).wait_recv()
        total = self.own_s[l, self.z]
        for k in self.near[1:]:
            total = total + self.zr_s[l, k - 1].astype(F32)
        self.gw_ref[l] = total[0 : self.rows]
        self.gvo_ref[l : l + 1, :] = total[self.rows : self.rows + 1, 0 : self.vrow]

    def drain(self):
        for l in range(2):
            for k in self.near[1:]:
                self.ag_along(l, k).wait_send()
                self.rs_along(l, k).wait_send()
            for t in range(self.z_count):
                for kind in range(4):
                    self.ag_copy(l, kind, t, "c").wait_send()
                self.ag_copy(l, 0, t, "x").wait_send()
                self.ag_copy(l, 0, t, "y").wait_send()
                self.ag_copy(l, 1, t, "y", 0).wait_send()
                self.ag_copy(l, 2, t, "x", 1).wait_send()
                for slot in range(6):
                    self.rs_across(l, slot, t).wait_send()
            for kind in range(4):
                self.rs_core(l, kind).wait_send()


def compute(x, cot, w, v, lengths, dims, own, z_count):
    d, ff = dims
    n = lengths.shape[0]
    mrows, vlen = 4 * d + 2 * ff, 6 * d + ff
    img = pl.BlockSpec((1, ROWS, NBLK, SUBL, d), lambda i: (i, 0, 0, 0, 0))
    shp = (n, ROWS, NBLK, SUBL, d)

    def whole(shape):
        zero = (0,) * len(shape)
        return pl.BlockSpec(shape, lambda i: zero, pipeline_mode=pl.Buffered(1))

    scratch = [
        pltpu.VMEM((2, 8, vlen), F32),
        pltpu.VMEM((2, d, mrows), F32),
        pltpu.VMEM((2, 8, vlen), F32),
        pltpu.VMEM((2, S, d), BF),
        pltpu.VMEM((2, S, 3 * d), BF),
        pltpu.VMEM((2, NBLK, HEADS, BLOCK, 128), BF),
        pltpu.VMEM((2, S, d), BF),
        pltpu.VMEM((2, S, d), F32),
        pltpu.VMEM((2, S, d), BF),
        pltpu.VMEM((2, S, ff), BF),
        pltpu.VMEM((S, ff), BF),
        pltpu.VMEM((NBLK, ROWS, SUBL, d), F32),
        pltpu.VMEM((ROWS, NBLK, SUBL, d), F32),
        pltpu.VMEM((S, d), BF),
        pltpu.VMEM((S, ff), BF),
        pltpu.VMEM((S, d), F32),
        pltpu.VMEM((S, d), BF),
        pltpu.VMEM((S, d), BF),
        pltpu.VMEM((S, 3 * d), BF),
    ]
    if own:
        rows, vrow = w.shape[1], v.shape[1]
        devices = mrows // rows
        block = rows + 16
        half = (block // 2 + 15) // 16 * 16
        zc = z_count
        dma = pltpu.SemaphoreType.DMA
        scratch += [
            pltpu.VMEM((2, devices, block, d), BF),
            pltpu.VMEM((2, devices, block, d), BF),
            pltpu.VMEM((2, 4, zc, block, d), BF),
            pltpu.VMEM((2, zc, block, d), F32),
            pltpu.VMEM((2, zc, half, d), BF),
            pltpu.VMEM((2, zc, block - half, d), BF),
            pltpu.VMEM((2, 2, zc, block, d), BF),
            pltpu.VMEM((2, zc - 1, block, d), BF),
            dma((2, 2, 4 * zc)), dma((2, 4 * zc)), dma((2, zc)),
            dma((2, 4 * zc)), dma((2, 4 * zc)), dma((2, 4 * zc)),
            dma((2, 4)), dma((2, 4)), dma((2, 6, zc)), dma((2, 6, zc)),
            dma((2, zc)), dma((2, zc)),
        ]
        gw_shape, gv_shape = (2, rows, d), (2, vrow)
    else:
        gw_shape, gv_shape = (2, mrows, d), (2, 1, vlen)
    return pl.pallas_call(
        partial(kernel, dims, own, z_count),
        grid=(n,),
        in_specs=[pl.BlockSpec(memory_space=pltpu.SMEM), img, img, whole(w.shape), whole(v.shape)],
        out_specs=[img, img, whole(gw_shape), whole(gv_shape)],
        out_shape=[
            jax.ShapeDtypeStruct(shp, F32),
            jax.ShapeDtypeStruct(shp, F32),
            jax.ShapeDtypeStruct(gw_shape, F32),
            jax.ShapeDtypeStruct(gv_shape, F32),
        ],
        scratch_shapes=scratch,
        compiler_params=pltpu.CompilerParams(
            dimension_semantics=("arbitrary",),
            vmem_limit_bytes=63 << 20,
            collective_id=0 if own else None,
            has_side_effects=own,
        ),
        name="layers",
    )(lengths, x.reshape(shp), cot.reshape(shp), w, v)


def body(z_count, dp_count, inputs, matrices, vectors, lengths, cotangent):
    d = inputs.shape[1]
    devices = z_count * dp_count
    ff = (matrices.shape[1] * devices - 4 * d) // 2
    own = dp_count == 8 and z_count & (z_count - 1) == 0
    split = ("dp", "sub")
    if own:
        w, v = matrices, vectors
    else:
        w = lax.all_gather(matrices, split, axis=1, tiled=True)
        v = lax.all_gather(vectors, split, axis=1, tiled=True).astype(F32)[:, None, :]
    out, gin, gw, gv = compute(inputs, cotangent, w, v, lengths, (d, ff), own, z_count)
    if not own:
        gw = lax.psum_scatter(gw, split, scatter_dimension=1, tiled=True)
        gv = lax.psum_scatter(gv[:, 0], split, scatter_dimension=1, tiled=True)
    return (out.reshape(inputs.shape), gin.reshape(inputs.shape), gw, gv)


def solution(mesh):
    split = ("dp", "sub")
    return jax.shard_map(
        partial(body, mesh.shape["sub"], mesh.shape["dp"]),
        mesh=mesh,
        in_specs=(P(split, None), P(None, split, None), P(None, split), P(split), P(split, None)),
        out_specs=(P(split, None), P(split, None), P(None, split, None), P(None, split)),
        check_vma=False,
    )
```

```python
from functools import partial

import jax
import jax.numpy as jnp
from jax import lax
from jax.experimental import pallas as pl
from jax.experimental.pallas import tpu as pltpu
from jax.sharding import PartitionSpec as P

HEADS = 2
COLS = 96
ROWS = 12
SUBL = 8
BLOCK = 96
NBLK = 12
S = COLS * ROWS
LOG2E = 1.4426950408889634
BF = jnp.bfloat16
F32 = jnp.float32
STATIC = False
SIZE = (288, 576, 576, 576, 576)
NB = (4, 4, 4, 4)
FLAGS = (True, True)


def mm(a, b, ca, cb):
    return lax.dot_general(a, b, (((ca,), (cb,)), ((), ())), preferred_element_type=F32)


def standardize(v):
    c = v - jnp.mean(v, -1, keepdims=True)
    r = lax.rsqrt(jnp.mean(c * c, -1, keepdims=True) + 1e-05)
    return c * r, r


def rowsum8(v):
    return jnp.sum(v.reshape(v.shape[0] // 8, 8, v.shape[1]), axis=0)


def live_mask(length, slab, width):
    row = lax.broadcasted_iota(jnp.int32, (ROWS, SUBL, width), 0)
    col = lax.broadcasted_iota(jnp.int32, (ROWS, SUBL, width), 1)
    return row * COLS + col + slab * SUBL < length


def kernel(dims, own, z_count, *refs):
    d, ff = dims
    len_ref, x_ref, cot_ref, w_ref, v_ref, out_ref, gin_ref, gw_ref, gvo_ref = refs[:9]
    (
        vs_s, gwt_ref, gv_ref, n1_s, pk_s, pt_s, mix_s, mid_s, n2_s, act_s, dact_s,
        x1_s, gy0_s, gy_s, gup_s, gmid_s, gmidl_s, gmix_s, gpk_s,
    ) = refs[9:28]
    img = pl.program_id(0)
    last = img == pl.num_programs(0) - 1
    length = len_ref[img]
    hw = d // HEADS
    qs = hw ** -0.5
    if own:
        move = Moves(z_count, w_ref, v_ref, gwt_ref, gv_ref, vs_s, gw_ref, gvo_ref, refs[28:])
        wpart = move.weights
    else:

        def wpart(l, a, b):
            return w_ref[l, a:b, :]

    @pl.when(img == 0)
    def _():
        def clear():
            gwt_ref[...] = jnp.zeros_like(gwt_ref)
            gv_ref[...] = jnp.zeros_like(gv_ref)

        if own:
            move.gather_first(clear)
        else:
            clear()
            vs_s[:, 0:1, :] = v_ref[...]

    def wqkv(l):
        return wpart(l, 0, 3 * d)

    def wout(l):
        return wpart(l, 3 * d, 4 * d)

    def vec(l, i, n=1):
        return vs_s[l, 0:1, i * d : (i + n) * d]

    tril_b = lax.broadcasted_iota(jnp.int32, (BLOCK, BLOCK), 0)
    tril_a = lax.broadcasted_iota(jnp.int32, (BLOCK, BLOCK), 1)
    masks = (
        tril_b <= tril_a,
        (tril_b <= tril_a) & ((tril_b & (SUBL - 1)) == (tril_a & (SUBL - 1))),
    )

    def load_x(l, c, nb):
        if l == 0:
            return x_ref[0, pl.ds(c * nb, nb)].reshape(nb * BLOCK, d)
        return x1_s[pl.ds(c * nb, nb)].reshape(nb * BLOCK, d)

    def store_perm(ref, c, nb, val, lead=()):
        v4 = val.reshape(nb, NBLK, SUBL, d)
        for b in range(nb):
            ref[lead + (slice(None), c * nb + b)] = v4[b]

    def rows(c, nb):
        if isinstance(c, int):
            return pl.ds(c * nb * BLOCK, nb * BLOCK)
        return pl.ds(pl.multiple_of(c * nb * BLOCK, BLOCK), nb * BLOCK)

    def loop(n, step):
        if STATIC or n == 1:
            for c in range(n):
                step(c, 0)
        else:
            lax.fori_loop(0, n, step, 0)

    def heads_of(packed):
        return [
            tuple(packed[:, i * d + h * hw : i * d + (h + 1) * hw] for i in range(3))
            for h in range(HEADS)
        ]

    def pipeline(stages, n):
        for i in range(n + len(stages) - 1):
            for j in reversed(range(len(stages))):
                if 0 <= i - j < n:
                    stages[j](i - j)

    def front(l, nb):
        mask = masks[l]
        qkv, scores, ps = {}, {}, {}

        def each(c):
            return [(c * nb + b, h) for b in range(nb) for h in range(HEADS)]

        def normed(c):
            xh, _r = standardize(load_x(l, c, nb))
            n1_s[l, rows(c, nb), :] = (xh * vec(l, 0) + vec(l, 1)).astype(BF)

        def project(c):
            pk_s[l, rows(c, nb), :] = mm(n1_s[l, rows(c, nb), :], wqkv(l), 1, 1).astype(BF)

        def score(c):
            qkv[c] = []
            for b in range(nb):
                qkv[c] += heads_of(pk_s[l, rows(c * nb + b, 1), :])
            scores[c] = [mm(k, q, 1, 1) for q, k, v in qkv[c]]

        def soft(c):
            ps[c] = []
            for st, (b, h) in zip(scores.pop(c), each(c)):
                st = jnp.where(mask, st, -1e30)
                p = jnp.exp2((st - jnp.max(st, 0, keepdims=True)) * (qs * LOG2E))
                p = (p * (1.0 / jnp.sum(p, 0, keepdims=True))).astype(BF)
                pt_s[l, b, h, :, 0:BLOCK] = p
                ps[c].append(p)

        def mix(c):
            for p, (q, k, v), (b, h) in zip(ps.pop(c), qkv.pop(c), each(c)):
                mix_s[l, rows(b, 1), h * hw : (h + 1) * hw] = mm(p, v, 0, 0).astype(BF)

        def middle(c):
            r = rows(c, nb)
            mid = load_x(l, c, nb) + mm(mix_s[l, r, :], wout(l), 1, 1) + vec(l, 2)
            mid_s[l, r, :] = mid
            xh, _r = standardize(mid)
            n2_s[l, r, :] = (xh * vec(l, 3) + vec(l, 4)).astype(BF)

        def hidden(c):
            r = rows(c, nb)
            n = ff // d
            h = mm(n2_s[l, r, :], wup(l, 0), 1, 1)
            for f in range(n):
                ahead = mm(n2_s[l, r, :], wup(l, f + 1), 1, 1) if f + 1 < n else None
                act, dact = gelu_parts(h + vec(l, 6 + f))
                act_s[l, r, cols(f)] = act
                dact_s[r, cols(f)] = dact
                h = ahead

        def result(c):
            r = rows(c, nb)
            y = mm(act_s[l, r, :], wpart(l, 4 * d + ff, 4 * d + 2 * ff), 1, 0)
            store_perm(x1_s, c, nb, y + mid_s[l, r, :] + vec(l, 5))

        stages = [normed, project, score, soft, mix, middle]
        if l == 0 and FLAGS[1]:
            stages += [hidden, result]
        pipeline(stages, NBLK // nb)

    def wup(l, f):
        return wpart(l, (4 + f) * d, (5 + f) * d)

    def wdown(l, f):
        return wpart(l, 4 * d + ff + f * d, 4 * d + ff + (f + 1) * d)

    def cols(f):
        return slice(f * d, (f + 1) * d)

    def gelu_parts(h):
        t = lax.erf(h * (2 ** -0.5)) + 1.0
        act = ((0.5 * h) * t).astype(BF)
        hb = h.astype(BF)
        e = jnp.exp2(hb * hb * BF(-0.5 * LOG2E))
        return act, t.astype(BF) + hb * e * BF(2 * 0.3989422804014327)

    def chunks(size):
        return [slice(r, r + size) for r in range(0, S, size)]

    def ffn_fwd0(size):
        l, n = 0, ff // d
        ahead = {s.start: mm(n2_s[l, s], wup(l, 0), 1, 1) for s in chunks(size)}
        for f in range(n):
            for s in chunks(size):
                h = ahead[s.start]
                if f + 1 < n:
                    ahead[s.start] = mm(n2_s[l, s], wup(l, f + 1), 1, 1)
                act, dact = gelu_parts(h + vec(l, 6 + f))
                act_s[l, s, cols(f)] = act
                dact_s[s, cols(f)] = dact
        y = mid_s[l] + vec(l, 5) + mm(act_s[l], wpart(l, 4 * d + ff, 4 * d + 2 * ff), 1, 0)
        store_perm(x1_s, 0, NBLK, y)

    def load_gy1():
        for b in range(NBLK):
            live = live_mask(length, b, d)
            part = jnp.where(live, cot_ref[0, :, b], 0.0).reshape(BLOCK, d)
            acc_vec(1, 5, part)
            gy_s[b * BLOCK : (b + 1) * BLOCK] = (0.5 * part).astype(BF)

    def ffn_both1(size):
        l, n = 1, ff // d

        def products(f, s):
            return mm(n2_s[l, s], wup(l, f), 1, 1), mm(gy_s[s], wdown(l, f), 1, 1)

        ahead = {s.start: products(0, s) for s in chunks(size)}
        for f in range(n + 1):
            for i, s in enumerate(chunks(size)):
                if f < n:
                    h, ga = ahead[s.start]
                    if f + 1 < n:
                        ahead[s.start] = products(f + 1, s)
                    act, dact = gelu_parts(h + vec(l, 6 + f))
                    act_s[l, s, cols(f)] = act
                    gup = ga * dact.astype(F32)
                    acc_vec(l, 6 + f, gup)
                    gup_s[s, cols(f)] = gup.astype(BF)
                if f > 0 and i == 0:
                    wgrad(l, 4 * d + ff + (f - 1) * d, gy_s[...], act_s[l, :, cols(f - 1)])
                if f > 0 and i == min(1, S // size - 1):
                    wgrad(l, 4 * d + (f - 1) * d, n2_s[l], gup_s[:, cols(f - 1)])

    def ffn_end1():
        l = 1
        y = mid_s[l] + vec(l, 5) + mm(act_s[l], wpart(l, 4 * d + ff, 4 * d + 2 * ff), 1, 0)
        y4 = y.reshape(NBLK, NBLK, SUBL, d)
        for b in range(NBLK):
            out_ref[0, :, b] = jnp.where(live_mask(length, b, d), y4[b], 0.0)

    def ffn_bwd0(size):
        l, n = 0, ff // d
        for s in chunks(size):
            gy = gy0_s[s.start // BLOCK : s.stop // BLOCK].reshape(size, d)
            acc_vec(l, 5, gy)
            gy_s[s] = (0.5 * gy).astype(BF)
        ahead = {s.start: mm(gy_s[s], wdown(l, 0), 1, 1) for s in chunks(size)}
        for f in range(n + 1):
            for i, s in enumerate(chunks(size)):
                if f < n:
                    ga = ahead[s.start]
                    if f + 1 < n:
                        ahead[s.start] = mm(gy_s[s], wdown(l, f + 1), 1, 1)
                    gup = ga * dact_s[s, cols(f)].astype(F32)
                    acc_vec(l, 6 + f, gup)
                    gup_s[s, cols(f)] = gup.astype(BF)
                if f > 0 and i == 0:
                    wgrad(l, 4 * d + ff + (f - 1) * d, gy_s[...], act_s[l, :, cols(f - 1)])
                if f > 0 and i == min(1, S // size - 1):
                    wgrad(l, 4 * d + (f - 1) * d, n2_s[l], gup_s[:, cols(f - 1)])

    def acc_vec(l, i, val, n=1):
        gv_ref[l, :, i * d : (i + n) * d] += rowsum8(val)

    def norm_back(l, gi, v, gn):
        xh, r = standardize(v)
        acc_vec(l, gi, gn * xh)
        acc_vec(l, gi + 1, gn)
        e = gn * vec(l, gi)
        me = jnp.mean(e, -1, keepdims=True)
        mx = jnp.mean(e * xh, -1, keepdims=True)
        return r * (e - me - xh * mx)

    def back(l, nb):
        gn2, gn1, qkv, gms, pts, gps, gss = {}, {}, {}, {}, {}, {}, {}

        def each(c):
            return [(c * nb + b, h) for b in range(nb) for h in range(HEADS)]

        def up(c):
            gn2[c] = mm(gup_s[rows(c, nb), :], wpart(l, 4 * d, 4 * d + ff), 1, 0)

        def middle(c):
            r = rows(c, nb)
            if l == 0:
                gy = gy0_s[c * nb : (c + 1) * nb].reshape(nb * BLOCK, d)
            else:
                parts = []
                for b in range(c * nb, (c + 1) * nb):
                    live = live_mask(length, b, d)
                    parts.append(jnp.where(live, cot_ref[0, :, b], 0.0).reshape(BLOCK, d))
                gy = jnp.concatenate(parts, 0)
            gmid = gy + norm_back(l, 3, mid_s[l, r, :], gn2.pop(c))
            gmid_s[r, :] = gmid
            acc_vec(l, 2, gmid)
            gmidl_s[r, :] = gmid.astype(BF)

        def out(c):
            r = rows(c, nb)
            gmix_s[r, :] = mm(gmidl_s[r, :], wout(l), 1, 0).astype(BF)

        def probs(c):
            qkv[c], gms[c] = [], []
            for b in range(c * nb, (c + 1) * nb):
                qkv[c] += heads_of(pk_s[l, rows(b, 1), :])
                gm = gmix_s[rows(b, 1), :]
                gms[c] += [gm[:, h * hw : (h + 1) * hw] for h in range(HEADS)]
            gps[c] = [mm(v, gm, 1, 1) for (q, k, v), gm in zip(qkv[c], gms[c])]

        def store(c, i, grads):
            for (b, h), g in zip(each(c), grads):
                gpk_s[rows(b, 1), i * d + h * hw : i * d + (h + 1) * hw] = g.astype(BF)

        def soft(c):
            pts = [pt_s[l, b, h, :, 0:BLOCK] for b, h in each(c)]
            gss[c] = []
            for pt, gp in zip(pts, gps.pop(c)):
                pf = pt.astype(F32)
                pg = pf * gp
                gss[c].append(((pg - pf * jnp.sum(pg, 0, keepdims=True)) * qs).astype(BF))
            store(c, 2, [mm(pt, gm, 1, 0) for pt, gm in zip(pts, gms.pop(c))])

        def heads(c):
            gs, both = gss.pop(c), qkv.pop(c)
            store(c, 1, [mm(g, q, 1, 0) for g, (q, k, v) in zip(gs, both)])
            store(c, 0, [mm(g, k, 0, 0) for g, (q, k, v) in zip(gs, both)])

        def project(c):
            gn1[c] = mm(gpk_s[rows(c, nb), :], wqkv(l), 1, 0)

        def first(c):
            r = rows(c, nb)
            gx = gmid_s[r, :] + norm_back(l, 0, load_x(l, c, nb), gn1.pop(c))
            if l == 0:
                gin_ref[0, pl.ds(c * nb, nb)] = gx.reshape(nb, NBLK, SUBL, d)
            else:
                store_perm(gy0_s, c, nb, gx)

        def weights(c):
            r = rows(c, nb)
            wgrad(l, 0, n1_s[l, r, :], gpk_s[r, :])
            wgrad(l, 3 * d, mix_s[l, r, :], gmidl_s[r, :])

        stages = [up, middle, out, probs, soft, heads, project, first]
        if FLAGS[0]:
            stages[7] = lambda c: (first(c), weights(c))
        pipeline(stages, NBLK // nb)

    def wgrad(l, at, a, b):
        gwt_ref[l, :, at : at + b.shape[1]] += mm(a, b, 0, 0)

    def wgrads(l):
        wgrad(l, 0, n1_s[l], gpk_s[...])
        wgrad(l, 3 * d, mix_s[l], gmidl_s[...])

    def region(step):
        pl.when(img >= 0)(step)

    def between(first, step):
        if own:
            pl.when(img == 0 if first else last)(step)

    region(lambda: front(0, NB[0]))
    if not FLAGS[1]:
        region(lambda: ffn_fwd0(SIZE[4]))
    between(True, lambda: move.gather_end(1))
    region(lambda: front(1, NB[1]))
    region(load_gy1)
    region(lambda: ffn_both1(SIZE[0]))
    region(ffn_end1)
    region(lambda: back(1, NB[2]))
    if not FLAGS[0]:
        region(lambda: wgrads(1))
    between(False, lambda: move.sum_start(1))
    region(lambda: ffn_bwd0(SIZE[2]))
    between(False, lambda: move.sum_chip(1))
    region(lambda: back(0, NB[3]))
    if not FLAGS[0]:
        region(lambda: wgrads(0))
    between(False, lambda: move.sum_start(0))
    between(False, lambda: move.sum_across(1))

    @pl.when(last)
    def _():
        if own:
            move.sum_tail(0, lambda: move.sum_column(1))
            move.sum_end(1)
            move.sum_end(0)
            move.drain()
        else:
            for l in range(2):
                gw_ref[l] = whole_grad(gwt_ref, l, 4 * d + ff)
                gvo_ref[l] = jnp.sum(gv_ref[l], 0, keepdims=True)


def whole_grad(gwt_ref, l, cut):
    return jnp.concatenate([gwt_ref[l, :, :cut], 2.0 * gwt_ref[l, :, cut:]], 1).T


MESH = pl.DeviceIdType.MESH


def column(y, x, core):
    return (y * 2 + x) * 2 + core


class Moves:
    def __init__(self, z_count, w_ref, v_ref, gwt_ref, gv_ref, vs_s, gw_ref, gvo_ref, refs):
        self.z_count = z_count
        self.w_ref, self.v_ref, self.gwt_ref, self.gv_ref = w_ref, v_ref, gwt_ref, gv_ref
        self.vs_s, self.gw_ref, self.gvo_ref = vs_s, gw_ref, gvo_ref
        (
            self.full_s, self.gb_s, self.sib_s, self.own_s, self.diag_top_s, self.diag_low_s,
            self.cols_s, self.zr_s,
            self.ag_link, self.ag_core, self.ag_z, self.ag_x, self.ag_y, self.ag_c,
            self.rs_core_send, self.rs_core_recv, self.rs_send, self.rs_recv,
            self.rs_z_send, self.rs_z_recv,
        ) = refs
        self.rows, self.d = w_ref.shape[1], w_ref.shape[2]
        self.block = self.full_s.shape[2]
        self.half = self.diag_top_s.shape[2]
        self.devices = self.full_s.shape[1]
        self.vrow = v_ref.shape[1]
        self.vlen = self.vrow * self.devices
        dp, z = lax.axis_index("dp"), lax.axis_index("sub")
        self.dp, self.z = dp, z
        self.core = dp % 2
        self.x = dp // 2 % 2
        self.y = dp // 4
        y, x = self.y, self.x
        self.chips = ((y, x), (y, 1 - x), (1 - y, x), (1 - y, 1 - x))
        self.dp_x = column(y, 1 - x, self.core)
        self.dp_y = column(1 - y, x, self.core)
        self.dp_c = column(y, x, 1 - self.core)
        self.size = (self.block, self.rows)
        self.cuts = (
            (pl.ds(0, self.half), pl.ds(self.half, self.block - self.half)),
            (pl.ds(0, self.rows // 2), pl.ds(self.rows // 2, self.rows // 2)),
        )
        self.near = list(range(z_count))
        self.order = self.near[1:] + [0]

    def zz(self, k):
        return self.z ^ k

    def index(self, kind, t, core=None):
        yy, xx = self.chips[kind]
        return column(yy, xx, self.core if core is None else core) * self.z_count + t

    def slot(self, kind, t):
        yy, xx = self.chips[kind]
        return (yy * 2 + xx) * self.z_count + t

    def weights(self, l, a, b):
        parts, rows = [], self.rows
        while a < b:
            i = a // rows
            e = min(b, (i + 1) * rows)
            parts.append(self.full_s[l, i, a - i * rows : e - i * rows, :])
            a = e
        return jnp.concatenate(parts, 0)

    def piece(self, l, i, part=None):
        rows = pl.ds(0, self.size[l]) if part is None else self.cuts[l][part]
        return self.full_s.at[l, i, rows, :]

    def remote(self, src, dst, send, recv, target):
        return pltpu.make_async_remote_copy(
            src_ref=src, dst_ref=dst, send_sem=send, recv_sem=recv,
            device_id=target, device_id_type=MESH,
        )

    def ag_copy(self, l, kind, t, way, part=None):
        i, s = self.index(kind, t), self.slot(kind, t)
        ref = self.piece(l, i, part)
        if way == "c":
            return self.remote(
                ref, ref, self.ag_c.at[l, s], self.ag_core.at[l, s], (self.dp_c, self.z)
            )
        send = self.ag_x if way == "x" else self.ag_y
        target = (self.dp_x if way == "x" else self.dp_y, self.z)
        return self.remote(ref, ref, send.at[l, s], self.ag_link.at[l, 1 if part else 0, s], target)

    def ag_along(self, l, k):
        ref = self.piece(l, self.index(0, self.z))
        s = self.slot(0, self.z)
        return self.remote(
            ref, ref, self.ag_z.at[l, k], self.ag_link.at[l, 0, s], (self.dp, self.zz(k))
        )

    def ag_wait(self, l, kind, t, part=None):
        i, s = self.index(kind, t), self.slot(kind, t)
        ref = self.piece(l, i, part)
        self.remote(
            ref, ref, self.ag_c.at[l, s], self.ag_link.at[l, 1 if part else 0, s],
            (self.dp_c, self.z),
        ).wait_recv()

    def gather_along(self, l):
        for k in self.near[1:]:
            self.ag_along(l, k).start()

    def gather_spread(self, l, steps):
        for k in steps:
            t = self.zz(k)
            if k:
                self.ag_wait(l, 0, t)
            for way in "xyc":
                self.ag_copy(l, 0, t, way).start()

    def gather_across(self, l):
        for k in self.near:
            t = self.zz(k)
            self.ag_wait(l, 1, t)
            self.ag_copy(l, 1, t, "y", 0).start()
            self.ag_copy(l, 1, t, "c").start()
            self.ag_wait(l, 2, t)
            self.ag_copy(l, 2, t, "x", 1).start()
            self.ag_copy(l, 2, t, "c").start()

    def gather_diagonal(self, l):
        for k in self.near:
            t = self.zz(k)
            self.ag_wait(l, 3, t, 0)
            self.ag_wait(l, 3, t, 1)
            self.ag_copy(l, 3, t, "c").start()

    def gather_end(self, l):
        for kind in range(4):
            for t in range(self.z_count):
                i, s = self.index(kind, t, 1 - self.core), self.slot(kind, t)
                ref = self.piece(l, i)
                self.remote(
                    ref, ref, self.ag_c.at[l, s], self.ag_core.at[l, s], (self.dp_c, self.z)
                ).wait_recv()
        if l == 1:
            return
        vrow, vlen, rows = self.vrow, self.vlen, self.rows
        tiles = [jnp.zeros((8, 128), F32)] * (vlen // 128 + 1)
        for i in range(self.devices):
            part = self.full_s[0, i, rows : self.block, 0:128].astype(F32)[0:8]
            at = i * vrow // 128
            wide = jnp.concatenate([part, jnp.zeros_like(part)], 1)
            if i * vrow > at * 128:
                wide = pltpu.roll(wide, i * vrow - at * 128, 1)
            tiles[at] += wide[:, 0:128]
            tiles[at + 1] += wide[:, 128:256]
        both = jnp.concatenate(tiles[:-1], 1)
        self.vs_s[0] = both
        self.vs_s[1] = pltpu.roll(both, 7, 0)

    def gather_first(self, meanwhile):
        barrier = pltpu.get_barrier_semaphore()
        partners = [(p, self.z) for p in (self.dp_x, self.dp_y, self.dp_c)]
        partners += [(self.dp, self.zz(k)) for k in self.near[1:]]
        for p in partners:
            pl.semaphore_signal(barrier, inc=1, device_id=p, device_id_type=MESH)
        me, rows = self.index(0, self.z), self.rows
        for l in range(2):
            self.full_s[l, me, 0:rows] = self.w_ref[l]
        tail = jnp.zeros((self.block - rows, self.d - self.vrow), BF)
        v = self.v_ref[...].astype(F32)
        v = jnp.concatenate([v, jnp.zeros((self.block - rows - 2, self.vrow), F32)], 0)
        self.full_s[0, me, rows : self.block, :] = jnp.concatenate([v.astype(BF), tail], 1)
        pl.semaphore_wait(barrier, len(partners))
        self.gather_along(0)
        self.gather_spread(0, (0,))
        self.gather_along(1)
        self.gather_spread(1, (0,))
        meanwhile()
        self.gather_spread(0, self.near[1:])
        self.gather_spread(1, self.near[1:])
        self.gather_across(0)
        self.gather_across(1)
        self.gather_diagonal(0)
        self.gather_diagonal(1)
        self.gather_end(0)

    def rs_core(self, l, kind):
        i = self.index(kind, 0, 1 - self.core)
        return self.remote(
            self.gb_s.at[l, pl.ds(i, self.z_count), pl.ds(0, self.size[l]), :],
            self.sib_s.at[l, kind, :, pl.ds(0, self.size[l]), :],
            self.rs_core_send.at[l, kind], self.rs_core_recv.at[l, kind], (self.dp_c, self.z),
        )

    def rs_across(self, l, slot, t):
        cuts = self.cuts[l]
        kind, half, target, dst = (
            (3, 0, self.dp_y, self.diag_top_s.at[l, t, pl.ds(0, cuts[0].size), :]),
            (3, 1, self.dp_x, self.diag_low_s.at[l, t, pl.ds(0, cuts[1].size), :]),
            (2, 0, self.dp_y, self.cols_s.at[l, 0, t, cuts[0], :]),
            (1, 1, self.dp_x, self.cols_s.at[l, 0, t, cuts[1], :]),
            (1, 0, self.dp_x, self.cols_s.at[l, 1, t, cuts[0], :]),
            (2, 1, self.dp_y, self.cols_s.at[l, 1, t, cuts[1], :]),
        )[slot]
        return self.remote(
            self.gb_s.at[l, self.index(kind, t), cuts[half], :], dst,
            self.rs_send.at[l, slot, t], self.rs_recv.at[l, slot, t], (target, self.z),
        )

    def rs_along(self, l, k):
        return self.remote(
            self.gb_s.at[l, self.index(0, self.zz(k)), pl.ds(0, self.size[l]), :],
            self.zr_s.at[l, k - 1, pl.ds(0, self.size[l]), :],
            self.rs_z_send.at[l, k], self.rs_z_recv.at[l, k], (self.dp, self.zz(k)),
        )

    def sum_start(self, l):
        rows, vrow, vlen, zc = self.rows, self.vrow, self.vlen, self.z_count
        cut = (rows * self.devices) // 2 + 2 * self.d
        gv = [jnp.sum(self.gv_ref[a], 0, keepdims=True) for a in range(2)]
        gv = jnp.concatenate(gv + [jnp.zeros((6, vlen), F32)], 0)
        for g in range(8):
            lo, hi = g * zc * rows, (g + 1) * zc * rows
            mid = min(max(lo, cut), hi)
            part = []
            if lo < mid:
                part.append(self.gwt_ref[l, :, lo:mid])
            if mid < hi:
                part.append(2.0 * self.gwt_ref[l, :, mid:hi])
            part = jnp.concatenate(part, 1).T.astype(BF)
            for j in range(zc):
                i = g * zc + j
                self.gb_s[l, i, 0:rows] = part[j * rows : (j + 1) * rows]
                if l == 1:
                    continue
                at = i * vrow // 128 * 128
                n = min(256, vlen - at)
                wide = gv[:, at : at + n]
                if n < 256:
                    wide = jnp.concatenate([wide, jnp.zeros_like(wide)], 1)
                if i * vrow > at:
                    wide = pltpu.roll(wide, 256 - (i * vrow - at), 1)
                wide = jnp.concatenate([wide, jnp.zeros_like(wide)], 0)
                self.gb_s[l, i, rows : self.block] = wide.astype(BF)
            yy, xx, cc = g // 4, g // 2 % 2, g % 2
            kind = 2 * jnp.abs(self.y - yy) + jnp.abs(self.x - xx)

            @pl.when(self.core == 1 - cc)
            def _():
                self.remote(
                    self.gb_s.at[l, pl.ds(g * zc, zc), pl.ds(0, self.size[l]), :],
                    self.sib_s.at[l, kind, :, pl.ds(0, self.size[l]), :],
                    self.rs_core_send.at[l, kind], self.rs_core_recv.at[l, kind],
                    (self.dp_c, self.z),
                ).start()

    def chip_step(self, l, k):
        t = self.zz(k)
        for kind, slots in ((3, (0, 1)), (1, (3,)), (2, (2,)), (0, ())):
            i = self.index(kind, t)
            size = self.size[l]
            mine, other = self.gb_s[l, i, 0:size], self.sib_s[l, kind, t, 0:size]
            if kind == 0:
                self.own_s[l, t, 0:size] = mine.astype(F32) + other.astype(F32)
            else:
                self.gb_s[l, i, 0:size] = mine + other
            for slot in slots:
                self.rs_across(l, slot, t).start()

    def across_step(self, l, k):
        t = self.zz(k)
        for slot, kind, half, ref in (
            (0, 1, 0, self.diag_top_s), (1, 2, 1, self.diag_low_s),
        ):
            self.rs_across(l, slot, t).wait_recv()
            i, cut = self.index(kind, t), self.cuts[l][half]
            self.gb_s[l, i, cut] = self.gb_s[l, i, cut] + ref[l, t, 0 : cut.size]
            self.rs_across(l, 4 if half == 0 else 5, t).start()

    def column_step(self, l, k):
        t = self.zz(k)
        for slot in (2, 3, 4, 5):
            self.rs_across(l, slot, t).wait_recv()
        size = self.size[l]
        total = self.own_s[l, t, 0:size]
        for a in range(2):
            total = total + self.cols_s[l, a, t, 0:size].astype(F32)
        if k:
            self.gb_s[l, self.index(0, t), 0:size] = total.astype(BF)
            self.rs_along(l, k).start()
        else:
            self.own_s[l, t, 0:size] = total

    def sum_core(self, l):
        for kind in (3, 1, 2, 0):
            self.rs_core(l, kind).wait_recv()

    def sum_chip(self, l):
        self.sum_core(l)
        for k in self.order:
            self.chip_step(l, k)

    def sum_across(self, l):
        for k in self.order:
            self.across_step(l, k)

    def sum_column(self, l):
        for k in self.order:
            self.column_step(l, k)

    def sum_tail(self, l, meanwhile):
        order = self.order
        self.sum_core(l)
        self.chip_step(l, order[0])
        self.chip_step(l, order[1])
        meanwhile()
        for n in range(len(order) + 2):
            if n < len(order):
                self.across_step(l, order[n])
            if 1 <= n <= len(order):
                self.column_step(l, order[n - 1])
            if n + 2 < len(order):
                self.chip_step(l, order[n + 2])

    def sum_end(self, l):
        for k in self.near[1:]:
            self.rs_along(l, k).wait_recv()
        size = self.size[l]
        total = self.own_s[l, self.z, 0:size]
        for k in self.near[1:]:
            total = total + self.zr_s[l, k - 1, 0:size].astype(F32)
        self.gw_ref[l] = total[0 : self.rows]
        if l == 0:
            self.gvo_ref[...] = total[self.rows : self.rows + 2, 0 : self.vrow]

    def drain(self):
        for l in range(2):
            for k in self.near[1:]:
                self.ag_along(l, k).wait_send()
                self.rs_along(l, k).wait_send()
            for t in range(self.z_count):
                for kind in range(4):
                    self.ag_copy(l, kind, t, "c").wait_send()
                self.ag_copy(l, 0, t, "x").wait_send()
                self.ag_copy(l, 0, t, "y").wait_send()
                self.ag_copy(l, 1, t, "y", 0).wait_send()
                self.ag_copy(l, 2, t, "x", 1).wait_send()
                for slot in range(6):
                    self.rs_across(l, slot, t).wait_send()
            for kind in range(4):
                self.rs_core(l, kind).wait_send()


def compute(x, cot, w, v, lengths, dims, own, z_count):
    d, ff = dims
    n = lengths.shape[0]
    mrows, vlen = 4 * d + 2 * ff, 6 * d + ff
    img = pl.BlockSpec((1, ROWS, NBLK, SUBL, d), lambda i: (i, 0, 0, 0, 0))
    shp = (n, ROWS, NBLK, SUBL, d)

    def whole(shape):
        zero = (0,) * len(shape)
        return pl.BlockSpec(shape, lambda i: zero, pipeline_mode=pl.Buffered(1))

    scratch = [
        pltpu.VMEM((2, 8, vlen), F32),
        pltpu.VMEM((2, d, mrows), F32),
        pltpu.VMEM((2, 8, vlen), F32),
        pltpu.VMEM((2, S, d), BF),
        pltpu.VMEM((2, S, 3 * d), BF),
        pltpu.VMEM((2, NBLK, HEADS, BLOCK, 128), BF),
        pltpu.VMEM((2, S, d), BF),
        pltpu.VMEM((2, S, d), F32),
        pltpu.VMEM((2, S, d), BF),
        pltpu.VMEM((2, S, ff), BF),
        pltpu.VMEM((S, ff), BF),
        pltpu.VMEM((NBLK, ROWS, SUBL, d), F32),
        pltpu.VMEM((ROWS, NBLK, SUBL, d), F32),
        pltpu.VMEM((S, d), BF),
        pltpu.VMEM((S, ff), BF),
        pltpu.VMEM((S, d), F32),
        pltpu.VMEM((S, d), BF),
        pltpu.VMEM((S, d), BF),
        pltpu.VMEM((S, 3 * d), BF),
    ]
    if own:
        rows, vrow = w.shape[1], v.shape[1]
        devices = mrows // rows
        block = rows + 16
        half = (block // 2 + 15) // 16 * 16
        zc = z_count
        dma = pltpu.SemaphoreType.DMA
        scratch += [
            pltpu.VMEM((2, devices, block, d), BF),
            pltpu.VMEM((2, devices, block, d), BF),
            pltpu.VMEM((2, 4, zc, block, d), BF),
            pltpu.VMEM((2, zc, block, d), F32),
            pltpu.VMEM((2, zc, half, d), BF),
            pltpu.VMEM((2, zc, block - half, d), BF),
            pltpu.VMEM((2, 2, zc, block, d), BF),
            pltpu.VMEM((2, zc - 1, block, d), BF),
            dma((2, 2, 4 * zc)), dma((2, 4 * zc)), dma((2, zc)),
            dma((2, 4 * zc)), dma((2, 4 * zc)), dma((2, 4 * zc)),
            dma((2, 4)), dma((2, 4)), dma((2, 6, zc)), dma((2, 6, zc)),
            dma((2, zc)), dma((2, zc)),
        ]
        gw_shape, gv_shape = (2, rows, d), (2, vrow)
    else:
        gw_shape, gv_shape = (2, mrows, d), (2, 1, vlen)
    return pl.pallas_call(
        partial(kernel, dims, own, z_count),
        grid=(n,),
        in_specs=[pl.BlockSpec(memory_space=pltpu.SMEM), img, img, whole(w.shape), whole(v.shape)],
        out_specs=[img, img, whole(gw_shape), whole(gv_shape)],
        out_shape=[
            jax.ShapeDtypeStruct(shp, F32),
            jax.ShapeDtypeStruct(shp, F32),
            jax.ShapeDtypeStruct(gw_shape, F32),
            jax.ShapeDtypeStruct(gv_shape, F32),
        ],
        scratch_shapes=scratch,
        compiler_params=pltpu.CompilerParams(
            dimension_semantics=("arbitrary",),
            vmem_limit_bytes=63 << 20,
            collective_id=0 if own else None,
            has_side_effects=own,
        ),
        name="layers",
    )(lengths, x.reshape(shp), cot.reshape(shp), w, v)


def body(z_count, dp_count, inputs, matrices, vectors, lengths, cotangent):
    d = inputs.shape[1]
    devices = z_count * dp_count
    ff = (matrices.shape[1] * devices - 4 * d) // 2
    own = dp_count == 8 and z_count & (z_count - 1) == 0
    split = ("dp", "sub")
    if own:
        w, v = matrices, vectors
    else:
        w = lax.all_gather(matrices, split, axis=1, tiled=True)
        v = lax.all_gather(vectors, split, axis=1, tiled=True).astype(F32)[:, None, :]
    out, gin, gw, gv = compute(inputs, cotangent, w, v, lengths, (d, ff), own, z_count)
    if not own:
        gw = lax.psum_scatter(gw, split, scatter_dimension=1, tiled=True)
        gv = lax.psum_scatter(gv[:, 0], split, scatter_dimension=1, tiled=True)
    return (out.reshape(inputs.shape), gin.reshape(inputs.shape), gw, gv)


def solution(mesh):
    split = ("dp", "sub")
    return jax.shard_map(
        partial(body, mesh.shape["sub"], mesh.shape["dp"]),
        mesh=mesh,
        in_specs=(P(split, None), P(None, split, None), P(None, split), P(split), P(split, None)),
        out_specs=(P(split, None), P(split, None), P(None, split, None), P(None, split)),
        check_vma=False,
    )
```

```python
from functools import partial

import jax
import jax.numpy as jnp
from jax import lax
from jax.experimental import pallas as pl
from jax.experimental.pallas import tpu as pltpu
from jax.sharding import PartitionSpec as P

HEADS = 2
COLS = 96
ROWS = 12
SUBL = 8
BLOCK = 96
NBLK = 12
S = COLS * ROWS
LOG2E = 1.4426950408889634
BF = jnp.bfloat16
F32 = jnp.float32
STATIC = False
SIZE = (288, 576, 576, 576, 576)
NB = (4, 4, 4, 4)
FLAGS = (True, True)


def mm(a, b, ca, cb):
    return lax.dot_general(a, b, (((ca,), (cb,)), ((), ())), preferred_element_type=F32)


def standardize(v):
    c = v - jnp.mean(v, -1, keepdims=True)
    r = lax.rsqrt(jnp.mean(c * c, -1, keepdims=True) + 1e-05)
    return c * r, r


def rowsum8(v):
    return jnp.sum(v.reshape(v.shape[0] // 8, 8, v.shape[1]), axis=0)


def keep_live(length, slab, val):
    col = lax.broadcasted_iota(jnp.int32, (SUBL, val.shape[2]), 0)
    left = length - slab * SUBL
    return jnp.stack([jnp.where(col < left - r * COLS, val[r], 0.0) for r in range(ROWS)])


def kernel(dims, own, z_count, *refs):
    d, ff = dims
    len_ref, x_ref, cot_ref, w_ref, v_ref, out_ref, gin_ref, gw_ref, gvo_ref = refs[:9]
    (
        vs_s, gwt_ref, gv_ref, n1_s, pk_s, pt_s, mix_s, mid_s, n2_s, act_s, dact_s,
        x1_s, gy0_s, gy_s, gup_s, gmid_s, gmidl_s, gmix_s, gpk_s,
    ) = refs[9:28]
    img = pl.program_id(0)
    last = img == pl.num_programs(0) - 1
    length = len_ref[img]
    hw = d // HEADS
    qs = hw ** -0.5
    if own:
        move = Moves(z_count, w_ref, v_ref, gwt_ref, gv_ref, vs_s, gw_ref, gvo_ref, refs[28:])
        wpart = move.weights
    else:

        def wpart(l, a, b):
            return w_ref[l, a:b, :]

    @pl.when(img == 0)
    def _():
        def clear():
            gwt_ref[...] = jnp.zeros_like(gwt_ref)
            gv_ref[...] = jnp.zeros_like(gv_ref)

        if own:
            move.gather_first(clear)
        else:
            clear()
            vs_s[:, 0:1, :] = v_ref[...]

    def wqkv(l):
        return wpart(l, 0, 3 * d)

    def wout(l):
        return wpart(l, 3 * d, 4 * d)

    def vec(l, i, n=1):
        return vs_s[l, 0:1, i * d : (i + n) * d]

    tril_b = lax.broadcasted_iota(jnp.int32, (BLOCK, BLOCK), 0)
    tril_a = lax.broadcasted_iota(jnp.int32, (BLOCK, BLOCK), 1)
    masks = (
        tril_b <= tril_a,
        (tril_b <= tril_a) & ((tril_b & (SUBL - 1)) == (tril_a & (SUBL - 1))),
    )

    def load_x(l, c, nb):
        if l == 0:
            return x_ref[0, pl.ds(c * nb, nb)].reshape(nb * BLOCK, d)
        return x1_s[pl.ds(c * nb, nb)].reshape(nb * BLOCK, d)

    def store_perm(ref, c, nb, val, lead=()):
        v4 = val.reshape(nb, NBLK, SUBL, d)
        for b in range(nb):
            ref[lead + (slice(None), c * nb + b)] = v4[b]

    def rows(c, nb):
        if isinstance(c, int):
            return pl.ds(c * nb * BLOCK, nb * BLOCK)
        return pl.ds(pl.multiple_of(c * nb * BLOCK, BLOCK), nb * BLOCK)

    def loop(n, step):
        if STATIC or n == 1:
            for c in range(n):
                step(c, 0)
        else:
            lax.fori_loop(0, n, step, 0)

    def heads_of(packed):
        return [
            tuple(packed[:, i * d + h * hw : i * d + (h + 1) * hw] for i in range(3))
            for h in range(HEADS)
        ]

    def pipeline(stages, n):
        for i in range(n + len(stages) - 1):
            for j in reversed(range(len(stages))):
                if 0 <= i - j < n:
                    stages[j](i - j)

    def front(l, nb):
        mask = masks[l]
        qkv, scores, ps = {}, {}, {}

        def each(c):
            return [(c * nb + b, h) for b in range(nb) for h in range(HEADS)]

        def normed(c):
            xh, _r = standardize(load_x(l, c, nb))
            n1_s[l, rows(c, nb), :] = (xh * vec(l, 0) + vec(l, 1)).astype(BF)

        def project(c):
            pk_s[l, rows(c, nb), :] = mm(n1_s[l, rows(c, nb), :], wqkv(l), 1, 1).astype(BF)

        def score(c):
            qkv[c] = []
            for b in range(nb):
                qkv[c] += heads_of(pk_s[l, rows(c * nb + b, 1), :])
            scores[c] = [mm(k, q, 1, 1) for q, k, v in qkv[c]]

        def soft(c):
            ps[c] = []
            for st, (b, h) in zip(scores.pop(c), each(c)):
                st = jnp.where(mask, st, -1e30)
                p = jnp.exp2((st - jnp.max(st, 0, keepdims=True)) * (qs * LOG2E))
                p = (p * (1.0 / jnp.sum(p, 0, keepdims=True))).astype(BF)
                pt_s[l, b, h, :, 0:BLOCK] = p
                ps[c].append(p)

        def mix(c):
            for p, (q, k, v), (b, h) in zip(ps.pop(c), qkv.pop(c), each(c)):
                mix_s[l, rows(b, 1), h * hw : (h + 1) * hw] = mm(p, v, 0, 0).astype(BF)

        def middle(c):
            r = rows(c, nb)
            mid = load_x(l, c, nb) + mm(mix_s[l, r, :], wout(l), 1, 1) + vec(l, 2)
            mid_s[l, r, :] = mid
            xh, _r = standardize(mid)
            n2_s[l, r, :] = (xh * vec(l, 3) + vec(l, 4)).astype(BF)

        def hidden(c):
            r = rows(c, nb)
            n = ff // d
            h = mm(n2_s[l, r, :], wup(l, 0), 1, 1)
            for f in range(n):
                ahead = mm(n2_s[l, r, :], wup(l, f + 1), 1, 1) if f + 1 < n else None
                act, dact = gelu_parts(h + vec(l, 6 + f))
                act_s[l, r, cols(f)] = act
                dact_s[r, cols(f)] = dact
                h = ahead

        def result(c):
            r = rows(c, nb)
            y = mm(act_s[l, r, :], wpart(l, 4 * d + ff, 4 * d + 2 * ff), 1, 0)
            store_perm(x1_s, c, nb, y + mid_s[l, r, :] + vec(l, 5))

        stages = [normed, project, score, soft, mix, middle]
        if l == 0 and FLAGS[1]:
            stages += [hidden, result]
        pipeline(stages, NBLK // nb)

    def wup(l, f):
        return wpart(l, (4 + f) * d, (5 + f) * d)

    def wdown(l, f):
        return wpart(l, 4 * d + ff + f * d, 4 * d + ff + (f + 1) * d)

    def cols(f):
        return slice(f * d, (f + 1) * d)

    def gelu_parts(h):
        t = lax.erf(h * (2 ** -0.5)) + 1.0
        act = ((0.5 * h) * t).astype(BF)
        hb = h.astype(BF)
        e = jnp.exp2(hb * hb * BF(-0.5 * LOG2E))
        return act, t.astype(BF) + hb * e * BF(2 * 0.3989422804014327)

    def chunks(size):
        return [slice(r, r + size) for r in range(0, S, size)]

    def ffn_fwd0(size):
        l, n = 0, ff // d
        ahead = {s.start: mm(n2_s[l, s], wup(l, 0), 1, 1) for s in chunks(size)}
        for f in range(n):
            for s in chunks(size):
                h = ahead[s.start]
                if f + 1 < n:
                    ahead[s.start] = mm(n2_s[l, s], wup(l, f + 1), 1, 1)
                act, dact = gelu_parts(h + vec(l, 6 + f))
                act_s[l, s, cols(f)] = act
                dact_s[s, cols(f)] = dact
        y = mid_s[l] + vec(l, 5) + mm(act_s[l], wpart(l, 4 * d + ff, 4 * d + 2 * ff), 1, 0)
        store_perm(x1_s, 0, NBLK, y)

    def load_gy1():
        for b in range(NBLK):
            part = keep_live(length, b, cot_ref[0, :, b]).reshape(BLOCK, d)
            acc_vec(1, 5, part)
            gy_s[b * BLOCK : (b + 1) * BLOCK] = (0.5 * part).astype(BF)

    def ffn_both1(size):
        l, n = 1, ff // d

        def products(f, s):
            return mm(n2_s[l, s], wup(l, f), 1, 1), mm(gy_s[s], wdown(l, f), 1, 1)

        ahead = {s.start: products(0, s) for s in chunks(size)}
        for f in range(n + 1):
            for i, s in enumerate(chunks(size)):
                if f < n:
                    h, ga = ahead[s.start]
                    if f + 1 < n:
                        ahead[s.start] = products(f + 1, s)
                    act, dact = gelu_parts(h + vec(l, 6 + f))
                    act_s[l, s, cols(f)] = act
                    gup = ga * dact.astype(F32)
                    acc_vec(l, 6 + f, gup)
                    gup_s[s, cols(f)] = gup.astype(BF)
                if f > 0 and i == 0:
                    wgrad(l, 4 * d + ff + (f - 1) * d, gy_s[...], act_s[l, :, cols(f - 1)])
                if f > 0 and i == min(1, S // size - 1):
                    wgrad(l, 4 * d + (f - 1) * d, n2_s[l], gup_s[:, cols(f - 1)])

    def ffn_end1():
        l = 1
        y = mid_s[l] + vec(l, 5) + mm(act_s[l], wpart(l, 4 * d + ff, 4 * d + 2 * ff), 1, 0)
        y4 = y.reshape(NBLK, NBLK, SUBL, d)
        for b in range(NBLK):
            out_ref[0, :, b] = keep_live(length, b, y4[b])

    def ffn_bwd0(size):
        l, n = 0, ff // d
        for s in chunks(size):
            gy = gy0_s[s.start // BLOCK : s.stop // BLOCK].reshape(size, d)
            acc_vec(l, 5, gy)
            gy_s[s] = (0.5 * gy).astype(BF)
        ahead = {s.start: mm(gy_s[s], wdown(l, 0), 1, 1) for s in chunks(size)}
        for f in range(n + 1):
            for i, s in enumerate(chunks(size)):
                if f < n:
                    ga = ahead[s.start]
                    if f + 1 < n:
                        ahead[s.start] = mm(gy_s[s], wdown(l, f + 1), 1, 1)
                    gup = ga * dact_s[s, cols(f)].astype(F32)
                    acc_vec(l, 6 + f, gup)
                    gup_s[s, cols(f)] = gup.astype(BF)
                if f > 0 and i == 0:
                    wgrad(l, 4 * d + ff + (f - 1) * d, gy_s[...], act_s[l, :, cols(f - 1)])
                if f > 0 and i == min(1, S // size - 1):
                    wgrad(l, 4 * d + (f - 1) * d, n2_s[l], gup_s[:, cols(f - 1)])

    def acc_vec(l, i, val, n=1):
        gv_ref[l, :, i * d : (i + n) * d] += rowsum8(val)

    def norm_back(l, gi, v, gn):
        xh, r = standardize(v)
        acc_vec(l, gi, gn * xh)
        acc_vec(l, gi + 1, gn)
        e = gn * vec(l, gi)
        me = jnp.mean(e, -1, keepdims=True)
        mx = jnp.mean(e * xh, -1, keepdims=True)
        return r * (e - me - xh * mx)

    def back(l, nb):
        gn2, gn1, qkv, gms, pts, gps, gss = {}, {}, {}, {}, {}, {}, {}

        def each(c):
            return [(c * nb + b, h) for b in range(nb) for h in range(HEADS)]

        def up(c):
            gn2[c] = mm(gup_s[rows(c, nb), :], wpart(l, 4 * d, 4 * d + ff), 1, 0)

        def middle(c):
            r = rows(c, nb)
            if l == 0:
                gy = gy0_s[c * nb : (c + 1) * nb].reshape(nb * BLOCK, d)
            else:
                parts = []
                for b in range(c * nb, (c + 1) * nb):
                    parts.append(keep_live(length, b, cot_ref[0, :, b]).reshape(BLOCK, d))
                gy = jnp.concatenate(parts, 0)
            gmid = gy + norm_back(l, 3, mid_s[l, r, :], gn2.pop(c))
            gmid_s[r, :] = gmid
            acc_vec(l, 2, gmid)
            gmidl_s[r, :] = gmid.astype(BF)

        def out(c):
            r = rows(c, nb)
            gmix_s[r, :] = mm(gmidl_s[r, :], wout(l), 1, 0).astype(BF)

        def probs(c):
            qkv[c], gms[c] = [], []
            for b in range(c * nb, (c + 1) * nb):
                qkv[c] += heads_of(pk_s[l, rows(b, 1), :])
                gm = gmix_s[rows(b, 1), :]
                gms[c] += [gm[:, h * hw : (h + 1) * hw] for h in range(HEADS)]
            gps[c] = [mm(v, gm, 1, 1) for (q, k, v), gm in zip(qkv[c], gms[c])]

        def store(c, i, grads):
            for (b, h), g in zip(each(c), grads):
                gpk_s[rows(b, 1), i * d + h * hw : i * d + (h + 1) * hw] = g.astype(BF)

        def soft(c):
            pts = [pt_s[l, b, h, :, 0:BLOCK] for b, h in each(c)]
            gss[c] = []
            for pt, gp in zip(pts, gps.pop(c)):
                pf = pt.astype(F32)
                pg = pf * gp
                gss[c].append(((pg - pf * jnp.sum(pg, 0, keepdims=True)) * qs).astype(BF))
            store(c, 2, [mm(pt, gm, 1, 0) for pt, gm in zip(pts, gms.pop(c))])

        def heads(c):
            gs, both = gss.pop(c), qkv.pop(c)
            store(c, 1, [mm(g, q, 1, 0) for g, (q, k, v) in zip(gs, both)])
            store(c, 0, [mm(g, k, 0, 0) for g, (q, k, v) in zip(gs, both)])

        def project(c):
            gn1[c] = mm(gpk_s[rows(c, nb), :], wqkv(l), 1, 0)

        def first(c):
            r = rows(c, nb)
            gx = gmid_s[r, :] + norm_back(l, 0, load_x(l, c, nb), gn1.pop(c))
            if l == 0:
                gin_ref[0, pl.ds(c * nb, nb)] = gx.reshape(nb, NBLK, SUBL, d)
            else:
                store_perm(gy0_s, c, nb, gx)

        def weights(c):
            r = rows(c, nb)
            wgrad(l, 0, n1_s[l, r, :], gpk_s[r, :])
            wgrad(l, 3 * d, mix_s[l, r, :], gmidl_s[r, :])

        stages = [up, middle, out, probs, soft, heads, project, first]
        if FLAGS[0]:
            stages[7] = lambda c: (first(c), weights(c))
        pipeline(stages, NBLK // nb)

    def wgrad(l, at, a, b):
        gwt_ref[l, :, at : at + b.shape[1]] += mm(a, b, 0, 0)

    def wgrads(l):
        wgrad(l, 0, n1_s[l], gpk_s[...])
        wgrad(l, 3 * d, mix_s[l], gmidl_s[...])

    def region(step):
        pl.when(img >= 0)(step)

    def between(first, step):
        if own:
            pl.when(img == 0 if first else last)(step)

    region(lambda: front(0, NB[0]))
    if not FLAGS[1]:
        region(lambda: ffn_fwd0(SIZE[4]))
    between(True, lambda: move.gather_end(1))
    region(lambda: front(1, NB[1]))
    region(load_gy1)
    region(lambda: ffn_both1(SIZE[0]))
    region(ffn_end1)
    region(lambda: back(1, NB[2]))
    if not FLAGS[0]:
        region(lambda: wgrads(1))
    between(False, lambda: move.sum_start(1))
    region(lambda: ffn_bwd0(SIZE[2]))
    between(False, lambda: move.sum_chip(1))
    region(lambda: back(0, NB[3]))
    if not FLAGS[0]:
        region(lambda: wgrads(0))
    between(False, lambda: move.sum_start(0))
    between(False, lambda: move.sum_across(1))

    @pl.when(last)
    def _():
        if own:
            move.sum_tail(0, lambda: move.sum_column(1))
            move.sum_end(1)
            move.sum_end(0)
            move.drain()
        else:
            for l in range(2):
                gw_ref[l] = whole_grad(gwt_ref, l, 4 * d + ff)
                gvo_ref[l] = jnp.sum(gv_ref[l], 0, keepdims=True)


def whole_grad(gwt_ref, l, cut):
    return jnp.concatenate([gwt_ref[l, :, :cut], 2.0 * gwt_ref[l, :, cut:]], 1).T


MESH = pl.DeviceIdType.MESH


def column(y, x, core):
    return (y * 2 + x) * 2 + core


class Moves:
    def __init__(self, z_count, w_ref, v_ref, gwt_ref, gv_ref, vs_s, gw_ref, gvo_ref, refs):
        self.z_count = z_count
        self.w_ref, self.v_ref, self.gwt_ref, self.gv_ref = w_ref, v_ref, gwt_ref, gv_ref
        self.vs_s, self.gw_ref, self.gvo_ref = vs_s, gw_ref, gvo_ref
        (
            self.full_s, self.gb_s, self.sib_s, self.own_s, self.diag_top_s, self.diag_low_s,
            self.cols_s, self.zr_s,
            self.ag_link, self.ag_core, self.ag_z, self.ag_x, self.ag_y, self.ag_c,
            self.rs_core_send, self.rs_core_recv, self.rs_send, self.rs_recv,
            self.rs_z_send, self.rs_z_recv,
        ) = refs
        self.rows, self.d = w_ref.shape[1], w_ref.shape[2]
        self.block = self.full_s.shape[2]
        self.half = self.diag_top_s.shape[2]
        self.devices = self.full_s.shape[1]
        self.vrow = v_ref.shape[1]
        self.vlen = self.vrow * self.devices
        dp, z = lax.axis_index("dp"), lax.axis_index("sub")
        self.dp, self.z = dp, z
        self.core = dp % 2
        self.x = dp // 2 % 2
        self.y = dp // 4
        y, x = self.y, self.x
        self.chips = ((y, x), (y, 1 - x), (1 - y, x), (1 - y, 1 - x))
        self.dp_x = column(y, 1 - x, self.core)
        self.dp_y = column(1 - y, x, self.core)
        self.dp_c = column(y, x, 1 - self.core)
        self.size = (self.block, self.rows)
        self.cuts = (
            (pl.ds(0, self.half), pl.ds(self.half, self.block - self.half)),
            (pl.ds(0, self.rows // 2), pl.ds(self.rows // 2, self.rows // 2)),
        )
        self.near = list(range(z_count))
        self.order = self.near[1:] + [0]

    def zz(self, k):
        return self.z ^ k

    def index(self, kind, t, core=None):
        yy, xx = self.chips[kind]
        return column(yy, xx, self.core if core is None else core) * self.z_count + t

    def slot(self, kind, t):
        yy, xx = self.chips[kind]
        return (yy * 2 + xx) * self.z_count + t

    def weights(self, l, a, b):
        parts, rows = [], self.rows
        while a < b:
            i = a // rows
            e = min(b, (i + 1) * rows)
            parts.append(self.full_s[l, i, a - i * rows : e - i * rows, :])
            a = e
        return jnp.concatenate(parts, 0)

    def piece(self, l, i, part=None):
        rows = pl.ds(0, self.size[l]) if part is None else self.cuts[l][part]
        return self.full_s.at[l, i, rows, :]

    def remote(self, src, dst, send, recv, target):
        return pltpu.make_async_remote_copy(
            src_ref=src, dst_ref=dst, send_sem=send, recv_sem=recv,
            device_id=target, device_id_type=MESH,
        )

    def ag_copy(self, l, kind, t, way, part=None):
        i, s = self.index(kind, t), self.slot(kind, t)
        ref = self.piece(l, i, part)
        if way == "c":
            return self.remote(
                ref, ref, self.ag_c.at[l, s], self.ag_core.at[l, s], (self.dp_c, self.z)
            )
        send = self.ag_x if way == "x" else self.ag_y
        target = (self.dp_x if way == "x" else self.dp_y, self.z)
        return self.remote(ref, ref, send.at[l, s], self.ag_link.at[l, 1 if part else 0, s], target)

    def ag_along(self, l, k):
        ref = self.piece(l, self.index(0, self.z))
        s = self.slot(0, self.z)
        return self.remote(
            ref, ref, self.ag_z.at[l, k], self.ag_link.at[l, 0, s], (self.dp, self.zz(k))
        )

    def ag_wait(self, l, kind, t, part=None):
        i, s = self.index(kind, t), self.slot(kind, t)
        ref = self.piece(l, i, part)
        self.remote(
            ref, ref, self.ag_c.at[l, s], self.ag_link.at[l, 1 if part else 0, s],
            (self.dp_c, self.z),
        ).wait_recv()

    def gather_along(self, l):
        for k in self.near[1:]:
            self.ag_along(l, k).start()

    def gather_spread(self, l, steps):
        for k in steps:
            t = self.zz(k)
            if k:
                self.ag_wait(l, 0, t)
            for way in "xyc":
                self.ag_copy(l, 0, t, way).start()

    def gather_across(self, l):
        for k in self.near:
            t = self.zz(k)
            self.ag_wait(l, 1, t)
            self.ag_copy(l, 1, t, "y", 0).start()
            self.ag_copy(l, 1, t, "c").start()
            self.ag_wait(l, 2, t)
            self.ag_copy(l, 2, t, "x", 1).start()
            self.ag_copy(l, 2, t, "c").start()

    def gather_diagonal(self, l):
        for k in self.near:
            t = self.zz(k)
            self.ag_wait(l, 3, t, 0)
            self.ag_wait(l, 3, t, 1)
            self.ag_copy(l, 3, t, "c").start()

    def gather_end(self, l):
        for kind in range(4):
            for t in range(self.z_count):
                i, s = self.index(kind, t, 1 - self.core), self.slot(kind, t)
                ref = self.piece(l, i)
                self.remote(
                    ref, ref, self.ag_c.at[l, s], self.ag_core.at[l, s], (self.dp_c, self.z)
                ).wait_recv()
        if l == 1:
            return
        vrow, vlen, rows = self.vrow, self.vlen, self.rows
        tiles = [jnp.zeros((8, 128), F32)] * (vlen // 128 + 1)
        for i in range(self.devices):
            part = self.full_s[0, i, rows : self.block, 0:128].astype(F32)[0:8]
            at = i * vrow // 128
            wide = jnp.concatenate([part, jnp.zeros_like(part)], 1)
            if i * vrow > at * 128:
                wide = pltpu.roll(wide, i * vrow - at * 128, 1)
            tiles[at] += wide[:, 0:128]
            tiles[at + 1] += wide[:, 128:256]
        both = jnp.concatenate(tiles[:-1], 1)
        self.vs_s[0] = both
        self.vs_s[1] = pltpu.roll(both, 7, 0)

    def gather_first(self, meanwhile):
        barrier = pltpu.get_barrier_semaphore()
        partners = [(p, self.z) for p in (self.dp_x, self.dp_y, self.dp_c)]
        partners += [(self.dp, self.zz(k)) for k in self.near[1:]]
        for p in partners:
            pl.semaphore_signal(barrier, inc=1, device_id=p, device_id_type=MESH)
        me, rows = self.index(0, self.z), self.rows
        for l in range(2):
            self.full_s[l, me, 0:rows] = self.w_ref[l]
        tail = jnp.zeros((self.block - rows, self.d - self.vrow), BF)
        v = self.v_ref[...].astype(F32)
        v = jnp.concatenate([v, jnp.zeros((self.block - rows - 2, self.vrow), F32)], 0)
        self.full_s[0, me, rows : self.block, :] = jnp.concatenate([v.astype(BF), tail], 1)
        pl.semaphore_wait(barrier, len(partners))
        self.gather_along(0)
        self.gather_spread(0, (0,))
        self.gather_along(1)
        self.gather_spread(1, (0,))
        meanwhile()
        self.gather_spread(0, self.near[1:])
        self.gather_spread(1, self.near[1:])
        self.gather_across(0)
        self.gather_across(1)
        self.gather_diagonal(0)
        self.gather_diagonal(1)
        self.gather_end(0)

    def rs_core(self, l, kind):
        i = self.index(kind, 0, 1 - self.core)
        return self.remote(
            self.gb_s.at[l, pl.ds(i, self.z_count), pl.ds(0, self.size[l]), :],
            self.sib_s.at[l, kind, :, pl.ds(0, self.size[l]), :],
            self.rs_core_send.at[l, kind], self.rs_core_recv.at[l, kind], (self.dp_c, self.z),
        )

    def rs_across(self, l, slot, t):
        cuts = self.cuts[l]
        kind, half, target, dst = (
            (3, 0, self.dp_y, self.diag_top_s.at[l, t, pl.ds(0, cuts[0].size), :]),
            (3, 1, self.dp_x, self.diag_low_s.at[l, t, pl.ds(0, cuts[1].size), :]),
            (2, 0, self.dp_y, self.cols_s.at[l, 0, t, cuts[0], :]),
            (1, 1, self.dp_x, self.cols_s.at[l, 0, t, cuts[1], :]),
            (1, 0, self.dp_x, self.cols_s.at[l, 1, t, cuts[0], :]),
            (2, 1, self.dp_y, self.cols_s.at[l, 1, t, cuts[1], :]),
        )[slot]
        return self.remote(
            self.gb_s.at[l, self.index(kind, t), cuts[half], :], dst,
            self.rs_send.at[l, slot, t], self.rs_recv.at[l, slot, t], (target, self.z),
        )

    def rs_along(self, l, k):
        return self.remote(
            self.gb_s.at[l, self.index(0, self.zz(k)), pl.ds(0, self.size[l]), :],
            self.zr_s.at[l, k - 1, pl.ds(0, self.size[l]), :],
            self.rs_z_send.at[l, k], self.rs_z_recv.at[l, k], (self.dp, self.zz(k)),
        )

    def sum_start(self, l):
        rows, vrow, vlen, zc = self.rows, self.vrow, self.vlen, self.z_count
        cut = (rows * self.devices) // 2 + 2 * self.d
        gv = [jnp.sum(self.gv_ref[a], 0, keepdims=True) for a in range(2)]
        gv = jnp.concatenate(gv + [jnp.zeros((6, vlen), F32)], 0)
        for g in range(8):
            lo, hi = g * zc * rows, (g + 1) * zc * rows
            mid = min(max(lo, cut), hi)
            part = []
            if lo < mid:
                part.append(self.gwt_ref[l, :, lo:mid])
            if mid < hi:
                part.append(2.0 * self.gwt_ref[l, :, mid:hi])
            part = jnp.concatenate(part, 1).T.astype(BF)
            for j in range(zc):
                i = g * zc + j
                self.gb_s[l, i, 0:rows] = part[j * rows : (j + 1) * rows]
                if l == 1:
                    continue
                at = i * vrow // 128 * 128
                n = min(256, vlen - at)
                wide = gv[:, at : at + n]
                if n < 256:
                    wide = jnp.concatenate([wide, jnp.zeros_like(wide)], 1)
                if i * vrow > at:
                    wide = pltpu.roll(wide, 256 - (i * vrow - at), 1)
                wide = jnp.concatenate([wide, jnp.zeros_like(wide)], 0)
                self.gb_s[l, i, rows : self.block] = wide.astype(BF)
            yy, xx, cc = g // 4, g // 2 % 2, g % 2
            kind = 2 * jnp.abs(self.y - yy) + jnp.abs(self.x - xx)

            @pl.when(self.core == 1 - cc)
            def _():
                self.remote(
                    self.gb_s.at[l, pl.ds(g * zc, zc), pl.ds(0, self.size[l]), :],
                    self.sib_s.at[l, kind, :, pl.ds(0, self.size[l]), :],
                    self.rs_core_send.at[l, kind], self.rs_core_recv.at[l, kind],
                    (self.dp_c, self.z),
                ).start()

    def chip_step(self, l, k):
        t = self.zz(k)
        for kind, slots in ((3, (0, 1)), (1, (3,)), (2, (2,)), (0, ())):
            i = self.index(kind, t)
            size = self.size[l]
            mine, other = self.gb_s[l, i, 0:size], self.sib_s[l, kind, t, 0:size]
            if kind == 0:
                self.own_s[l, t, 0:size] = mine.astype(F32) + other.astype(F32)
            else:
                self.gb_s[l, i, 0:size] = mine + other
            for slot in slots:
                self.rs_across(l, slot, t).start()

    def across_step(self, l, k):
        t = self.zz(k)
        for slot, kind, half, ref in (
            (0, 1, 0, self.diag_top_s), (1, 2, 1, self.diag_low_s),
        ):
            self.rs_across(l, slot, t).wait_recv()
            i, cut = self.index(kind, t), self.cuts[l][half]
            self.gb_s[l, i, cut] = self.gb_s[l, i, cut] + ref[l, t, 0 : cut.size]
            self.rs_across(l, 4 if half == 0 else 5, t).start()

    def column_step(self, l, k):
        t = self.zz(k)
        for slot in (2, 3, 4, 5):
            self.rs_across(l, slot, t).wait_recv()
        size = self.size[l]
        total = self.own_s[l, t, 0:size]
        for a in range(2):
            total = total + self.cols_s[l, a, t, 0:size].astype(F32)
        if k:
            self.gb_s[l, self.index(0, t), 0:size] = total.astype(BF)
            self.rs_along(l, k).start()
        else:
            self.own_s[l, t, 0:size] = total

    def sum_core(self, l):
        for kind in (3, 1, 2, 0):
            self.rs_core(l, kind).wait_recv()

    def sum_chip(self, l):
        self.sum_core(l)
        for k in self.order:
            self.chip_step(l, k)

    def sum_across(self, l):
        for k in self.order:
            self.across_step(l, k)

    def sum_column(self, l):
        for k in self.order:
            self.column_step(l, k)

    def sum_tail(self, l, meanwhile):
        order = self.order
        self.sum_core(l)
        self.chip_step(l, order[0])
        self.chip_step(l, order[1])
        meanwhile()
        for n in range(len(order) + 2):
            if n < len(order):
                self.across_step(l, order[n])
            if 1 <= n <= len(order):
                self.column_step(l, order[n - 1])
            if n + 2 < len(order):
                self.chip_step(l, order[n + 2])

    def sum_end(self, l):
        for k in self.near[1:]:
            self.rs_along(l, k).wait_recv()
        size = self.size[l]
        total = self.own_s[l, self.z, 0:size]
        for k in self.near[1:]:
            total = total + self.zr_s[l, k - 1, 0:size].astype(F32)
        self.gw_ref[l] = total[0 : self.rows]
        if l == 0:
            self.gvo_ref[...] = total[self.rows : self.rows + 2, 0 : self.vrow]

    def drain(self):
        for l in range(2):
            for k in self.near[1:]:
                self.ag_along(l, k).wait_send()
                self.rs_along(l, k).wait_send()
            for t in range(self.z_count):
                for kind in range(4):
                    self.ag_copy(l, kind, t, "c").wait_send()
                self.ag_copy(l, 0, t, "x").wait_send()
                self.ag_copy(l, 0, t, "y").wait_send()
                self.ag_copy(l, 1, t, "y", 0).wait_send()
                self.ag_copy(l, 2, t, "x", 1).wait_send()
                for slot in range(6):
                    self.rs_across(l, slot, t).wait_send()
            for kind in range(4):
                self.rs_core(l, kind).wait_send()


def compute(x, cot, w, v, lengths, dims, own, z_count):
    d, ff = dims
    n = lengths.shape[0]
    mrows, vlen = 4 * d + 2 * ff, 6 * d + ff
    img = pl.BlockSpec((1, ROWS, NBLK, SUBL, d), lambda i: (i, 0, 0, 0, 0))
    shp = (n, ROWS, NBLK, SUBL, d)

    def whole(shape):
        zero = (0,) * len(shape)
        return pl.BlockSpec(shape, lambda i: zero, pipeline_mode=pl.Buffered(1))

    scratch = [
        pltpu.VMEM((2, 8, vlen), F32),
        pltpu.VMEM((2, d, mrows), F32),
        pltpu.VMEM((2, 8, vlen), F32),
        pltpu.VMEM((2, S, d), BF),
        pltpu.VMEM((2, S, 3 * d), BF),
        pltpu.VMEM((2, NBLK, HEADS, BLOCK, 128), BF),
        pltpu.VMEM((2, S, d), BF),
        pltpu.VMEM((2, S, d), F32),
        pltpu.VMEM((2, S, d), BF),
        pltpu.VMEM((2, S, ff), BF),
        pltpu.VMEM((S, ff), BF),
        pltpu.VMEM((NBLK, ROWS, SUBL, d), F32),
        pltpu.VMEM((ROWS, NBLK, SUBL, d), F32),
        pltpu.VMEM((S, d), BF),
        pltpu.VMEM((S, ff), BF),
        pltpu.VMEM((S, d), F32),
        pltpu.VMEM((S, d), BF),
        pltpu.VMEM((S, d), BF),
        pltpu.VMEM((S, 3 * d), BF),
    ]
    if own:
        rows, vrow = w.shape[1], v.shape[1]
        devices = mrows // rows
        block = rows + 16
        half = (block // 2 + 15) // 16 * 16
        zc = z_count
        dma = pltpu.SemaphoreType.DMA
        scratch += [
            pltpu.VMEM((2, devices, block, d), BF),
            pltpu.VMEM((2, devices, block, d), BF),
            pltpu.VMEM((2, 4, zc, block, d), BF),
            pltpu.VMEM((2, zc, block, d), F32),
            pltpu.VMEM((2, zc, half, d), BF),
            pltpu.VMEM((2, zc, block - half, d), BF),
            pltpu.VMEM((2, 2, zc, block, d), BF),
            pltpu.VMEM((2, zc - 1, block, d), BF),
            dma((2, 2, 4 * zc)), dma((2, 4 * zc)), dma((2, zc)),
            dma((2, 4 * zc)), dma((2, 4 * zc)), dma((2, 4 * zc)),
            dma((2, 4)), dma((2, 4)), dma((2, 6, zc)), dma((2, 6, zc)),
            dma((2, zc)), dma((2, zc)),
        ]
        gw_shape, gv_shape = (2, rows, d), (2, vrow)
    else:
        gw_shape, gv_shape = (2, mrows, d), (2, 1, vlen)
    return pl.pallas_call(
        partial(kernel, dims, own, z_count),
        grid=(n,),
        in_specs=[pl.BlockSpec(memory_space=pltpu.SMEM), img, img, whole(w.shape), whole(v.shape)],
        out_specs=[img, img, whole(gw_shape), whole(gv_shape)],
        out_shape=[
            jax.ShapeDtypeStruct(shp, F32),
            jax.ShapeDtypeStruct(shp, F32),
            jax.ShapeDtypeStruct(gw_shape, F32),
            jax.ShapeDtypeStruct(gv_shape, F32),
        ],
        scratch_shapes=scratch,
        compiler_params=pltpu.CompilerParams(
            dimension_semantics=("arbitrary",),
            vmem_limit_bytes=63 << 20,
            collective_id=0 if own else None,
            has_side_effects=own,
        ),
        name="layers",
    )(lengths, x.reshape(shp), cot.reshape(shp), w, v)


def body(z_count, dp_count, inputs, matrices, vectors, lengths, cotangent):
    d = inputs.shape[1]
    devices = z_count * dp_count
    ff = (matrices.shape[1] * devices - 4 * d) // 2
    own = dp_count == 8 and z_count & (z_count - 1) == 0
    split = ("dp", "sub")
    if own:
        w, v = matrices, vectors
    else:
        w = lax.all_gather(matrices, split, axis=1, tiled=True)
        v = lax.all_gather(vectors, split, axis=1, tiled=True).astype(F32)[:, None, :]
    out, gin, gw, gv = compute(inputs, cotangent, w, v, lengths, (d, ff), own, z_count)
    if not own:
        gw = lax.psum_scatter(gw, split, scatter_dimension=1, tiled=True)
        gv = lax.psum_scatter(gv[:, 0], split, scatter_dimension=1, tiled=True)
    return (out.reshape(inputs.shape), gin.reshape(inputs.shape), gw, gv)


def solution(mesh):
    split = ("dp", "sub")
    return jax.shard_map(
        partial(body, mesh.shape["sub"], mesh.shape["dp"]),
        mesh=mesh,
        in_specs=(P(split, None), P(None, split, None), P(None, split), P(split), P(split, None)),
        out_specs=(P(split, None), P(split, None), P(None, split, None), P(None, split)),
        check_vma=False,
    )
```
